512 devices in a mesh: dp: 16 (over x, z_lo), ctx: 32 (over y, z_hi, core).
Axes of the slice: x: 4, y: 8, z: 8 (z_hi: 2, z_lo: 4; z = z_hi * 4 + z_lo), core: 2. Of those that a mesh axis runs over, the one named last changes fastest.
Arguments:
- series: bfloat16 [16, 4096, 1536], P('dp', 'ctx'), may hold values from -6 to 6
- cotangent: bfloat16 [16, 4096, 1536], P('dp', 'ctx'), may hold values from -6 to 6
- step_times: float32 [16, 4096], P('dp', 'ctx'), may hold values from 0 to 4096
- seg_starts: int32 [16, 4], P('dp'), may hold values from 0 to 4095, as said below
- star_of_row: int32 [16], P('dp'), may hold values from 0 to 15
- block_weight: bfloat16 [1536, 128], replicated, may hold values from -0.5 to 0.5
- star_table: float32 [16, 1536], replicated, may hold values from -6 to 6
- log_rate: float32 [1536], replicated, may hold values from -12 to -3
Outputs:
- grad_series: bfloat16 [16, 4096, 1536], P('dp', 'ctx')
- grad_weight: float32 [1536, 128], P('dp')
- grad_star: float32 [16, 1536], P(None, 'dp')
- grad_log_rate: float32 [1536], P('dp')
The draws below stay inside these ranges and needn't reach their ends.
Inputs may be any that keep to these rules, and one draw needn't show every extreme that they name: `seg_starts`: in each row the offsets strictly rise and the first one is 0.
All inputs are finite; a program needn't handle non-finite values.
Results may differ from the reference program's by a relative error of at most 0.0039.
Values sent between devices are 32-bit elements; how exact they have to be, the bound alone decides.
No kernel may reach another device: no remote copies, remote signals or barrier semaphores. Data moves between devices by JAX's collectives and lax.ppermute only.
A program may use at most 64 MiB of HBM per device.

```python
import math
import jax
import jax.numpy as jnp
from jax import lax

D = 1536
BLOCK = 128
STARS = 16
SEGS = 4
ROWS = 16
L = 4096


def draw_step_times(key, part):
    key_base, key_spot, key_gap = jax.random.split(key, 3)
    base_times = jax.random.uniform(key_base, (ROWS, L), jnp.float32, 0.5, 2.0)
    spots = jax.random.randint(key_spot, (ROWS, 2), 0, L)
    struck = jnp.any(jnp.arange(L)[None, None, :] == spots[:, :, None], axis=1)
    gap_times = L * jax.random.uniform(key_gap, (ROWS, L), jnp.float32, 0.5, 0.8)
    return jnp.where(struck, gap_times, base_times).astype(jnp.float32)


def draw_log_rate(key, part):
    key_pick, key_slow, key_fast = jax.random.split(key, 3)
    fast_share = 0.5
    fast_pick = jax.random.bernoulli(key_pick, fast_share, (D,))
    slow_values = jnp.log(jax.random.uniform(key_slow, (D,), jnp.float32, 0.2, 0.8) / L)
    fast_values = jax.random.uniform(key_fast, (D,), jnp.float32, math.log(1.0 / 50.0), math.log(1.0 / 30.0))
    return jnp.where(fast_pick, fast_values, slow_values).astype(jnp.float32)


def draw_seg_starts(key, part):
    row_keys = jax.random.split(key, ROWS)

    def one_row(row_key):
        picks = jax.random.permutation(row_key, L - 1)[:SEGS - 1] + 1
        return jnp.concatenate([jnp.zeros((1,), jnp.int32), jnp.sort(picks).astype(jnp.int32)])
    starts = jax.vmap(one_row)(row_keys)
    starts = starts.at[0, SEGS - 1].set(L - 1)
    return starts.astype(jnp.int32)


def with_ends(result, rng, low, top_value):
    index_at = [jax.random.randint(jax.random.fold_in(rng, axis), (), 0, length) for axis, length in enumerate(result.shape)]
    main_axis = result.shape.index(max(result.shape))
    next_to = index_at[:main_axis] + [(index_at[main_axis] + 1) % result.shape[main_axis]] + index_at[main_axis + 1:]
    return result.at[tuple(index_at)].set(low).at[tuple(next_to)].set(top_value)


def steps_of(stream_key, dims, cuts, low, high):
    factor_of, own = 1.0, jax.random.fold_in(stream_key, 6)
    for position, shards_of in cuts:
        steps = jnp.exp(jax.random.uniform(jax.random.fold_in(own, position), (shards_of,), jnp.float32, low / len(cuts), high / len(cuts)))
        factor_of = factor_of * jnp.repeat(steps, dims[position] // shards_of).reshape([-1 if axis == position else 1 for axis in range(len(dims))])
    return factor_of


def gaussian(stream_key, dims, scale, limit, cuts=(), kind=jnp.bfloat16):
    loudness = steps_of(stream_key, dims, cuts, -0.22, 0.18) if cuts else 1.0
    drawn = jax.random.normal(stream_key, dims, jnp.float32) * scale * loudness
    return jnp.minimum(jnp.maximum(drawn, -limit), limit).astype(kind)


def setup_inputs(seed: int = 0) -> dict:
    arg_keys = jax.random.split(jax.random.key(seed), 9)
    return {
        "series": gaussian(arg_keys[0], (ROWS, L, D), 1.0, 6.0, ((0, 16), (1, 32))),
        "cotangent": gaussian(arg_keys[1], (ROWS, L, D), 1.0, 6.0, ((0, 16), (1, 32))),
        "step_times": draw_step_times(jax.random.fold_in(arg_keys[8], 71), 0),
        "seg_starts": draw_seg_starts(jax.random.fold_in(arg_keys[8], 71), 0),
        "star_of_row": with_ends(jax.random.randint(arg_keys[4], (ROWS,), 0, STARS), jax.random.fold_in(arg_keys[4], 1), 0, STARS - 1).astype(jnp.int32),
        "block_weight": gaussian(arg_keys[5], (D, BLOCK), BLOCK ** -0.5, 0.5),
        "star_table": gaussian(arg_keys[6], (STARS, D), 1.0, 6.0, (), jnp.float32),
        "log_rate": draw_log_rate(jax.random.fold_in(arg_keys[8], 71), 0),
    }


def reference(series, cotangent, step_times, seg_starts, star_of_row, block_weight, star_table, log_rate):
    head_count = D // BLOCK
    decay_rate = jnp.exp(log_rate)
    input_gain = jnp.sqrt(-jnp.expm1(-2.0 * decay_rate))
    weight_blocks = block_weight.astype(jnp.float32).reshape(head_count, BLOCK, BLOCK)
    positions = jnp.arange(L).astype(jnp.int32)

    def forward_step(state, inputs):
        factor, source = inputs
        state = factor[None, :] * state + source
        return (state, state)

    def one_row(row_items):
        row_series, row_grad, row_times, row_starts, row_star = row_items
        kept_mask = 1.0 - jnp.any(row_starts[:, None] == positions[None, :], axis=0).astype(jnp.float32)
        series_blocks = row_series.astype(jnp.float32).reshape(L, head_count, BLOCK)
        projected = jnp.einsum('thi,hij->thj', series_blocks, weight_blocks).reshape(L, D) + star_table[row_star][None, :]
        drive_in = input_gain[None, :] * projected
        decays = jnp.exp(-decay_rate[None, :] * row_times[:, None]) * kept_mask[:, None]
        grad_out = row_grad.astype(jnp.float32)
        sources = jnp.stack([drive_in, grad_out], axis=1)
        zero_state = jnp.zeros((2, D), jnp.float32)
        _, states_fwd = lax.scan(forward_step, zero_state, (decays, sources))
        shifted = jnp.concatenate([decays[1:], jnp.zeros((1, D), jnp.float32)], axis=0)
        _, states_rev = lax.scan(forward_step, zero_state, (shifted, sources), reverse=True)
        fwd_state = states_fwd[:, 0]
        adj_bwd = states_fwd[:, 1]
        bwd_state = states_rev[:, 0]
        adj_fwd = states_rev[:, 1]
        earlier = jnp.concatenate([jnp.zeros((1, 2, D), jnp.float32), states_fwd[:-1]], axis=0)
        grad_drive = adj_fwd + adj_bwd
        grad_proj = input_gain[None, :] * grad_drive
        rate_term = -lax.optimization_barrier(jnp.sum(row_times[:, None] * decays * (adj_fwd * earlier[:, 0] + earlier[:, 1] * bwd_state), axis=0))
        rate_term = rate_term + jnp.exp(-2.0 * decay_rate) / input_gain * lax.optimization_barrier(jnp.sum(grad_drive * projected, axis=0))
        grad_low = grad_proj.astype(jnp.bfloat16)
        low_blocks = grad_low.astype(jnp.float32).reshape(L, head_count, BLOCK)
        back = jnp.einsum('thj,hij->thi', low_blocks, weight_blocks).reshape(L, D)
        row_dx = (grad_out + back).astype(jnp.bfloat16)
        weight_term = jnp.einsum('thi,thj->hij', series_blocks, low_blocks).reshape(D, BLOCK)
        return (row_dx, weight_term, decay_rate * rate_term, lax.optimization_barrier(jnp.sum(grad_proj, axis=0)))
    grad_series, weight_terms, rate_terms, proj_sums = lax.map(one_row, (series, cotangent, step_times, seg_starts, star_of_row))
    norm_factor = 1.0 / jnp.sqrt(jnp.float32(ROWS * L))
    star_pick = (star_of_row[:, None] == jnp.arange(STARS).astype(jnp.int32)[None, :]).astype(jnp.float32)
    grad_star = jnp.dot(star_pick.T, proj_sums, precision=lax.Precision.HIGHEST) * norm_factor
    grad_weight = lax.optimization_barrier(jnp.sum(weight_terms, axis=0)) * norm_factor
    grad_log_rate = lax.optimization_barrier(jnp.sum(rate_terms, axis=0)) * norm_factor
    return (grad_series, grad_weight, grad_star, grad_log_rate)
```

```python
import functools
import jax
import jax.numpy as jnp
from jax import lax
from jax.experimental import pallas as pl
from jax.experimental.pallas import tpu as pltpu
from jax.sharding import Mesh, PartitionSpec as P

SLAB = 128
LANES = 128
CHUNKS = 8
STEPS = SLAB // CHUNKS
FAR = 1e9
F32 = jnp.float32
BF16 = jnp.bfloat16


def slab_index():
    return (lax.axis_index("y") * 2 + lax.axis_index("zh")) * 2 + lax.axis_index("core")


def elapsed_row(starts_ref, times_ref, me):
    position = lax.broadcasted_iota(jnp.int32, (1, SLAB), 1) + me * SLAB
    reset = position == starts_ref[0, 0]
    for k in range(1, starts_ref.shape[1]):
        reset = jnp.logical_or(reset, position == starts_ref[0, k])
    return jnp.where(reset, FAR, times_ref[...])


def ends_kernel(
    blocks, slabs, starts_ref, star_ref, times_ref, series_ref, cot_ref, w_ref, table_ref, lograte_ref,
    out_ref, ends_ref,
):
    me = slab_index()
    elapsed = elapsed_row(starts_ref, times_ref, me)
    row = lax.broadcasted_iota(jnp.int32, (SLAB, SLAB), 0)
    lane = lax.broadcasted_iota(jnp.int32, (SLAB, SLAB), 1)
    spread = jnp.broadcast_to(elapsed, (SLAB, SLAB))
    to_end = jnp.sum(jnp.where(lane > row, spread, 0.0), axis=1, keepdims=True)
    from_start = jnp.sum(jnp.where(lane <= row, spread, 0.0), axis=1, keepdims=True)
    to_end = jnp.broadcast_to(to_end, (SLAB, LANES))
    from_start = jnp.broadcast_to(from_start, (SLAB, LANES))
    total = jnp.sum(elapsed, axis=1, keepdims=True)
    bias = table_ref[pl.ds(star_ref[0], 1), :]
    for h in range(blocks):
        cols = slice(h * LANES, (h + 1) * LANES)
        proj = jnp.dot(series_ref[0, :, cols], w_ref[cols, :], preferred_element_type=F32) + bias[:, cols]
        grad = cot_ref[0, :, cols].astype(F32)
        slope = -jnp.exp(lograte_ref[h : h + 1, :])
        late = jnp.exp(slope * to_end)
        early = jnp.exp(slope * from_start)
        ends_ref[0, h : h + 1, :] = jnp.sum(late * proj, axis=0, keepdims=True)
        ends_ref[0, blocks + h : blocks + h + 1, :] = jnp.sum(late * grad, axis=0, keepdims=True)
        ends_ref[1, h : h + 1, :] = jnp.sum(early * proj, axis=0, keepdims=True)
        ends_ref[1, blocks + h : blocks + h + 1, :] = jnp.sum(early * grad, axis=0, keepdims=True)
    tail = jnp.broadcast_to(total, (8, LANES))
    ends_ref[0, 2 * blocks : 2 * blocks + 8, :] = tail
    ends_ref[1, 2 * blocks : 2 * blocks + 8, :] = tail
    for d in range(slabs):
        out_ref[d] = ends_ref[jnp.where(d > me, 0, 1)]


def shift(x, k, fill, sublane):
    if k > 0:
        return jnp.where(sublane < k, fill, pltpu.roll(x, k, 0))
    return jnp.where(sublane >= CHUNKS + k, fill, pltpu.roll(x, CHUNKS + k, 0))


def chunk_entries(ends, through, carry, sublane, sign):
    for k in (1, 2, 4):
        ends = ends + through * shift(ends, sign * k, 0.0, sublane)
        through = through * shift(through, sign * k, 1.0, sublane)
    return shift(ends + through * carry, sign, jnp.broadcast_to(carry, ends.shape), sublane)


def main_kernel(
    blocks, slabs, rows_dp, starts_ref, star_ref, times_ref, series_ref, cot_ref, w_ref, table_ref, lograte_ref,
    gain_ref, got_ref, dx_ref, keep_ref, send_ref, carry_ref, sums_ref, part_ref,
):
    me = slab_index()
    width = blocks * LANES
    elapsed = elapsed_row(starts_ref, times_ref, me)
    row = lax.broadcasted_iota(jnp.int32, (SLAB, SLAB), 0)
    lane = lax.broadcasted_iota(jnp.int32, (SLAB, SLAB), 1)
    time_of_row = (row % CHUNKS) * STEPS + row // CHUNKS
    order = (lane == time_of_row).astype(F32).astype(BF16)
    time_of_lane = (lane % CHUNKS) * STEPS + lane // CHUNKS
    unorder = (row == time_of_lane).astype(F32).astype(BF16)
    gap = jnp.sum(jnp.where(lane == time_of_row, jnp.broadcast_to(elapsed, (SLAB, SLAB)), 0.0), axis=1, keepdims=True)
    gap = jnp.broadcast_to(gap, (SLAB, LANES))
    bias = table_ref[pl.ds(star_ref[0], 1), :]
    sublane = lax.broadcasted_iota(jnp.int32, (CHUNKS, LANES), 0)

    slope = -jnp.exp(lograte_ref[...])
    slope2 = jnp.concatenate([slope, slope], axis=0)
    between = [None] * slabs
    run = jnp.zeros((1, LANES), F32)
    for s in reversed(range(slabs)):
        between[s] = run
        run = jnp.where(s < me, run + got_ref[s, 2 * blocks : 2 * blocks + 1, :], 0.0)
    run = jnp.zeros((1, LANES), F32)
    carry_early = jnp.zeros((2 * blocks, LANES), F32)
    carry_late = jnp.zeros((2 * blocks, LANES), F32)
    for s in range(slabs):
        x = jnp.exp(slope2 * jnp.where(s < me, between[s], run)) * got_ref[s, 0 : 2 * blocks, :]
        carry_early = carry_early + jnp.where(s < me, x, 0.0)
        carry_late = carry_late + jnp.where(s > me, x, 0.0)
        run = jnp.where(s > me, run + got_ref[s, 2 * blocks : 2 * blocks + 1, :], 0.0)
    gains = jnp.concatenate([gain_ref[...], jnp.ones((blocks, LANES), F32)], axis=0)
    carry_ref[0] = carry_early * gains
    carry_ref[1] = carry_late * gains

    for h in range(blocks):
        cols = slice(h * LANES, (h + 1) * LANES)
        rate = jnp.exp(lograte_ref[h : h + 1, :])
        gain = gain_ref[h : h + 1, :]
        weight = w_ref[cols, :]
        xs = jnp.dot(order, series_ref[0, :, cols], preferred_element_type=F32).astype(BF16)
        grad = jnp.dot(order, cot_ref[0, :, cols], preferred_element_type=F32)
        proj = jnp.dot(xs, weight, preferred_element_type=F32) + bias[:, cols]
        drive = gain * proj
        decay = jnp.exp(-rate * gap)
        tiles = lambda v: [v[j * CHUNKS : (j + 1) * CHUNKS, :] for j in range(STEPS)]
        a, d, g, pr, dt = tiles(decay), tiles(drive), tiles(grad), tiles(proj), tiles(gap)
        before_d, before_g, through = [None], [None], [a[0]]
        state_d, state_g = d[0], g[0]
        for j in range(1, STEPS):
            before_d.append(a[j] * state_d)
            before_g.append(a[j] * state_g)
            state_d = before_d[j] + d[j]
            state_g = before_g[j] + g[j]
            through.append(a[j] * through[j - 1])
        enter_d = chunk_entries(state_d, through[-1], carry_ref[0, h : h + 1, :], sublane, 1)
        enter_g = chunk_entries(state_g, through[-1], carry_ref[0, blocks + h : blocks + h + 1, :], sublane, 1)
        after_d, after_g, back_through = [None] * STEPS, [None] * STEPS, [None] * STEPS
        after_d[-1], after_g[-1] = d[-1], g[-1]
        for j in reversed(range(STEPS - 1)):
            after_d[j] = a[j + 1] * after_d[j + 1] + d[j]
            after_g[j] = a[j + 1] * after_g[j + 1] + g[j]
            back_through[j] = a[j + 1] if j == STEPS - 2 else a[j + 1] * back_through[j + 1]
        leave_d = chunk_entries(a[0] * after_d[0], through[-1], carry_ref[1, h : h + 1, :], sublane, -1)
        leave_g = chunk_entries(a[0] * after_g[0], through[-1], carry_ref[1, blocks + h : blocks + h + 1, :], sublane, -1)
        rate_sum = jnp.zeros((CHUNKS, LANES), F32)
        grad_sum = jnp.zeros((CHUNKS, LANES), F32)
        cross_sum = jnp.zeros((CHUNKS, LANES), F32)
        low = []
        for j in range(STEPS):
            kept_d = through[j] * enter_d if j == 0 else before_d[j] + through[j] * enter_d
            kept_g = through[j] * enter_g if j == 0 else before_g[j] + through[j] * enter_g
            later_d = after_d[j] + (leave_d if j == STEPS - 1 else back_through[j] * leave_d)
            later_g = after_g[j] + (leave_g if j == STEPS - 1 else back_through[j] * leave_g)
            total = later_g + (kept_g + g[j])
            rate_sum = rate_sum + dt[j] * (later_g * kept_d + kept_g * later_d)
            grad_sum = grad_sum + total
            cross_sum = cross_sum + total * pr[j]
            low.append(gain * total)
        low = jnp.concatenate(low, axis=0).astype(BF16)
        product = lax.dot_general(xs, low, (((0,), (0,)), ((), ())), preferred_element_type=F32)
        back = lax.dot_general(low, weight, (((1,), (1,)), ((), ())), preferred_element_type=F32)
        out = (grad + back).astype(BF16)
        dx_ref[0, :, cols] = jnp.dot(unorder, out, preferred_element_type=F32).astype(BF16)
        for k in range(LANES // 8):
            piece, third = divmod(h * (LANES // 8) + k, 3)
            dp, quarter = divmod(piece, 4)
            core, zh = divmod(quarter, 2)
            part_ref[core, dp * 2 + zh, third * 8 : third * 8 + 8, :] = product[k * 8 : k * 8 + 8, :]
        total = lambda v: jnp.sum(v, axis=0, keepdims=True)
        sums_ref[0:1, cols] = gain * total(grad_sum)
        sums_ref[1:2, cols] = rate * (jnp.exp(-2.0 * rate) / gain * total(cross_sum) - total(rate_sum))
    share = width // rows_dp
    lane8 = lax.broadcasted_iota(jnp.int32, (8, LANES), 1)
    sub8 = lax.broadcasted_iota(jnp.int32, (8, LANES), 0)
    sums_ref[2:8, :] = jnp.zeros((6, sums_ref.shape[1]), F32)
    sums_ref[0:2, width:] = jnp.zeros((2, sums_ref.shape[1] - width), F32)
    star_half = jnp.broadcast_to(0.5 * star_ref[0].astype(F32), (8, LANES))
    for dp in range(rows_dp):
        window = sums_ref[:, dp * share : dp * share + LANES]
        tile = jnp.where(sub8 == 2, star_half, jnp.where(lane8 < share, window, 0.0))
        for core in range(2):
            for zh in range(2):
                part_ref[core, dp * 2 + zh, 24:32, :] = tile
    core = lax.axis_index("core")
    keep_ref[...] = part_ref[core]
    send_ref[...] = part_ref[1 - core]


def piece_kernel(norm, got_ref, out_ref):
    first = (lax.axis_index("core") * 2 + lax.axis_index("zh")) * 4
    total = got_ref[0, 0:24, :]
    logs = got_ref[0, 25:26, :]
    stars = [jnp.zeros((1, LANES), F32)] * 4
    for s in range(got_ref.shape[0]):
        if s:
            total = total + got_ref[s, 0:24, :]
            logs = logs + got_ref[s, 25:26, :]
        for k in range(4):
            hit = got_ref[s, 26:27, :] == (first + k).astype(F32)
            stars[k] = stars[k] + jnp.where(hit, got_ref[s, 24:25, :], 0.0)
    total = total * norm
    tail = jnp.concatenate(stars + [logs] + [jnp.zeros((3, LANES), F32)], axis=0) * norm
    for d in range(out_ref.shape[0]):
        out_ref[d, 0:24, :] = total
        out_ref[d, 24:32, :] = tail


def final_kernel(got_ref, weight_ref, star_ref, log_ref):
    share = star_ref.shape[1]
    for core in range(2):
        for zh in range(2):
            q = core * 2 + zh
            total = got_ref[core, zh]
            for y in range(1, got_ref.shape[1] // 2):
                total = total + got_ref[core, y * 2 + zh]
            weight_ref[q * 24 : q * 24 + 24, :] = total[0:24, :]
            star_ref[q * 4 : q * 4 + 4, :] = total[24:28, 0:share]
            if q == 0:
                log_ref[...] = total[28:29, 0:share]


def body(series, cotangent, step_times, seg_starts, star_of_row, block_weight, star_table, log_rate):
    _, slab_len, width = series.shape
    blocks = width // LANES
    slabs = lax.axis_size(("y", "zh", "core"))
    rows_dp = lax.axis_size(("x", "zl"))
    norm = float(1.0 / (rows_dp * slabs * slab_len) ** 0.5)
    log_blocks = log_rate.reshape(blocks, LANES)
    gain = jnp.sqrt(-jnp.expm1(-2.0 * jnp.exp(log_blocks)))
    smem = pl.BlockSpec(memory_space=pltpu.SMEM)
    vmem = pl.BlockSpec(memory_space=pltpu.VMEM)
    params = pltpu.CompilerParams(vmem_limit_bytes=40 * 1024 * 1024)
    common = (seg_starts, star_of_row, step_times, series, cotangent, block_weight, star_table, log_blocks)
    ends = pl.pallas_call(
        functools.partial(ends_kernel, blocks, slabs),
        out_shape=jax.ShapeDtypeStruct((slabs, 32, LANES), F32),
        in_specs=[smem, smem] + [vmem] * 6,
        out_specs=vmem,
        scratch_shapes=[pltpu.VMEM((2, 32, LANES), F32)],
        compiler_params=params,
        name="slab_ends",
    )(*common)
    got = lax.all_to_all(ends, ("y", "zh", "core"), 0, 0)
    grad_series, keep, send = pl.pallas_call(
        functools.partial(main_kernel, blocks, slabs, rows_dp),
        out_shape=[
            jax.ShapeDtypeStruct(series.shape, BF16),
            jax.ShapeDtypeStruct((rows_dp * 2, 32, LANES), F32),
            jax.ShapeDtypeStruct((rows_dp * 2, 32, LANES), F32),
        ],
        in_specs=[smem, smem] + [vmem] * 8,
        out_specs=[vmem] * 3,
        scratch_shapes=[
            pltpu.VMEM((2, 2 * blocks, LANES), F32),
            pltpu.VMEM((8, width + LANES), F32),
            pltpu.VMEM((2, rows_dp * 2, 32, LANES), F32),
        ],
        compiler_params=params,
        name="gradients",
    )(*common, gain, got)
    pair = keep + lax.ppermute(send, "core", [(0, 1), (1, 0)])
    pieces = lax.all_to_all(pair, ("x", "zl", "zh"), 0, 0)
    piece = pl.pallas_call(
        functools.partial(piece_kernel, norm),
        out_shape=jax.ShapeDtypeStruct((slabs // 2, 32, LANES), F32),
        in_specs=[vmem],
        out_specs=vmem,
        compiler_params=params,
        name="sum_pieces",
    )(pieces)
    spread = lax.all_to_all(piece, ("y", "zh"), 0, 0)
    both = lax.all_gather(spread, "core")
    share = width // rows_dp
    grad_weight, grad_star, grad_log = pl.pallas_call(
        final_kernel,
        out_shape=[
            jax.ShapeDtypeStruct((share, LANES), F32),
            jax.ShapeDtypeStruct((star_table.shape[0], share), F32),
            jax.ShapeDtypeStruct((1, share), F32),
        ],
        in_specs=[vmem],
        out_specs=[vmem] * 3,
        compiler_params=params,
        name="outputs",
    )(both)
    return grad_series, grad_weight, grad_star, grad_log.reshape(share)


def solution(mesh):
    fine = Mesh(mesh.devices.reshape(4, 4, 8, 2, 2), ("x", "zl", "y", "zh", "core"))
    dp, ctx = ("x", "zl"), ("y", "zh", "core")
    in_specs = (P(dp, ctx, None), P(dp, ctx, None), P(dp, ctx), P(dp, None), P(dp), P(), P(), P())
    out_specs = (P(dp, ctx, None), P(dp, None), P(None, dp), P(dp))
    return jax.shard_map(body, mesh=fine, in_specs=in_specs, out_specs=out_specs, check_vma=False)
```

```python
import functools
import jax
import jax.numpy as jnp
from jax import lax
from jax.experimental import pallas as pl
from jax.experimental.pallas import tpu as pltpu
from jax.sharding import Mesh, PartitionSpec as P

SLAB = 128
LANES = 128
CHUNKS = 8
STEPS = SLAB // CHUNKS
FAR = 1e9
F32 = jnp.float32
BF16 = jnp.bfloat16


def slab_index():
    return (lax.axis_index("y") * 2 + lax.axis_index("zh")) * 2 + lax.axis_index("core")


def elapsed_row(starts_ref, times_ref, me):
    position = lax.broadcasted_iota(jnp.int32, (1, SLAB), 1) + me * SLAB
    reset = position == starts_ref[0, 0]
    for k in range(1, starts_ref.shape[1]):
        reset = jnp.logical_or(reset, position == starts_ref[0, k])
    return jnp.where(reset, FAR, times_ref[...])


def ends_kernel(
    blocks, chips, starts_hbm, star_hbm, times_hbm, series_hbm, cot_hbm, w_hbm, table_hbm, lograte_hbm,
    out_ref, ends_ref, starts_ref, star_ref, times_ref, series_ref, cot_ref, w_ref, table_ref, lograte_ref, sems,
):
    sources = (starts_hbm, star_hbm, times_hbm, table_hbm, lograte_hbm, series_hbm, w_hbm, cot_hbm)
    targets = (starts_ref, star_ref, times_ref, table_ref, lograte_ref, series_ref, w_ref, cot_ref)
    copies = [pltpu.make_async_copy(a, b, sems.at[k]) for k, (a, b) in enumerate(zip(sources, targets))]
    for copy in copies:
        copy.start()
    core = lax.axis_index("core")
    me = slab_index()
    for copy in copies[:3]:
        copy.wait()
    elapsed = elapsed_row(starts_ref, times_ref, me)
    row = lax.broadcasted_iota(jnp.int32, (SLAB, SLAB), 0)
    lane = lax.broadcasted_iota(jnp.int32, (SLAB, SLAB), 1)
    spread = jnp.broadcast_to(elapsed, (SLAB, SLAB))
    to_end = jnp.sum(jnp.where(lane > row, spread, 0.0), axis=1, keepdims=True)
    from_start = jnp.sum(jnp.where(lane <= row, spread, 0.0), axis=1, keepdims=True)
    to_end = jnp.broadcast_to(to_end, (SLAB, LANES))
    from_start = jnp.broadcast_to(from_start, (SLAB, LANES))
    total = jnp.sum(elapsed, axis=1, keepdims=True)
    for copy in copies[3:]:
        copy.wait()
    bias = table_ref[pl.ds(star_ref[0], 1), :]
    for h in range(blocks):
        cols = slice(h * LANES, (h + 1) * LANES)
        proj = jnp.dot(series_ref[0, :, cols], w_ref[cols, :], preferred_element_type=F32) + bias[:, cols]
        grad = cot_ref[0, :, cols].astype(F32)
        slope = -jnp.exp(lograte_ref[h : h + 1, :])
        late = jnp.exp(slope * to_end)
        early = jnp.exp(slope * from_start)
        ends_ref[0, h : h + 1, :] = jnp.sum(late * proj, axis=0, keepdims=True)
        ends_ref[0, blocks + h : blocks + h + 1, :] = jnp.sum(late * grad, axis=0, keepdims=True)
        ends_ref[1, h : h + 1, :] = jnp.sum(early * proj, axis=0, keepdims=True)
        ends_ref[1, blocks + h : blocks + h + 1, :] = jnp.sum(early * grad, axis=0, keepdims=True)
    tail = jnp.broadcast_to(total, (8, LANES))
    ends_ref[0, 2 * blocks : 2 * blocks + 8, :] = tail
    ends_ref[1, 2 * blocks : 2 * blocks + 8, :] = tail
    for chip in range(chips):
        out_ref[chip] = ends_ref[jnp.where(2 * chip + 1 - core > me, 0, 1)]


def shift(x, k, fill, sublane):
    if k > 0:
        return jnp.where(sublane < k, fill, pltpu.roll(x, k, 0))
    return jnp.where(sublane >= CHUNKS + k, fill, pltpu.roll(x, CHUNKS + k, 0))


def chunk_entries(ends, through, carry, sublane, sign):
    for k in (1, 2, 4):
        ends = ends + through * shift(ends, sign * k, 0.0, sublane)
        through = through * shift(through, sign * k, 1.0, sublane)
    return shift(ends + through * carry, sign, jnp.broadcast_to(carry, ends.shape), sublane)


def local_kernel(
    blocks, starts_ref, star_ref, times_ref, series_ref, cot_ref, w_ref, table_ref, lograte_ref, gain_ref,
    base_ref, onward_ref, backward_ref, xt_ref, chunk_ref,
):
    me = slab_index()
    elapsed = elapsed_row(starts_ref, times_ref, me)
    row = lax.broadcasted_iota(jnp.int32, (SLAB, SLAB), 0)
    lane = lax.broadcasted_iota(jnp.int32, (SLAB, SLAB), 1)
    time_of_row = (row % CHUNKS) * STEPS + row // CHUNKS
    order = (lane == time_of_row).astype(F32).astype(BF16)
    gap = jnp.sum(jnp.where(lane == time_of_row, jnp.broadcast_to(elapsed, (SLAB, SLAB)), 0.0), axis=1, keepdims=True)
    gap = jnp.broadcast_to(gap, (SLAB, LANES))
    bias = table_ref[pl.ds(star_ref[0], 1), :]
    for h in range(blocks):
        cols = slice(h * LANES, (h + 1) * LANES)
        rate = jnp.exp(lograte_ref[h : h + 1, :])
        gain = gain_ref[h : h + 1, :]
        x = jnp.dot(order, series_ref[0, :, cols], preferred_element_type=F32)
        xt_ref[cols, :] = x.T.astype(BF16)
        grad = jnp.dot(order, cot_ref[0, :, cols], preferred_element_type=F32)
        proj = jnp.dot(x.astype(BF16), w_ref[cols, :], preferred_element_type=F32) + bias[:, cols]
        drive = gain * proj
        decay = jnp.exp(-rate * gap)
        tiles = lambda v: [v[j * CHUNKS : (j + 1) * CHUNKS, :] for j in range(STEPS)]
        a, d, g, pr, dt = tiles(decay), tiles(drive), tiles(grad), tiles(proj), tiles(gap)
        zero = jnp.zeros((CHUNKS, LANES), F32)
        before_d, before_g, through = [zero], [zero], [a[0]]
        state_d, state_g = d[0], g[0]
        for j in range(1, STEPS):
            before_d.append(a[j] * state_d)
            before_g.append(a[j] * state_g)
            state_d = before_d[j] + d[j]
            state_g = before_g[j] + g[j]
            through.append(a[j] * through[j - 1])
        after_d, after_g, back = [None] * STEPS, [None] * STEPS, [None] * STEPS
        after_d[-1], after_g[-1], back[-1] = d[-1], g[-1], jnp.ones((CHUNKS, LANES), F32)
        for j in reversed(range(STEPS - 1)):
            after_d[j] = a[j + 1] * after_d[j + 1] + d[j]
            after_g[j] = a[j + 1] * after_g[j + 1] + g[j]
            back[j] = a[j + 1] * back[j + 1]
        sums = [zero] * 12
        for j in range(STEPS):
            base = after_g[j] + before_g[j] + g[j]
            rows = slice(j * CHUNKS, (j + 1) * CHUNKS)
            base_ref[rows, cols] = base
            onward_ref[rows, cols] = through[j]
            backward_ref[rows, cols] = back[j]
            dt_on, dt_back = dt[j] * through[j], dt[j] * back[j]
            terms = (
                dt[j] * (after_g[j] * before_d[j] + before_g[j] * after_d[j]),
                dt_back * before_d[j],
                dt_on * after_g[j],
                dt_on * back[j],
                dt_back * before_g[j],
                dt_on * after_d[j],
                base,
                through[j],
                back[j],
                base * pr[j],
                through[j] * pr[j],
                back[j] * pr[j],
            )
            sums = [s + t for s, t in zip(sums, terms)]
        heads = [state_d, state_g, through[-1], a[0] * after_d[0], a[0] * after_g[0]]
        for k, v in enumerate(heads + sums):
            chunk_ref[k, :, cols] = v


def combine_kernel(
    blocks, slabs, rows_dp, lograte_ref, gain_ref, got_ref, chunk_hbm, base_hbm, onward_hbm, backward_hbm, xt_hbm,
    low_ref, keep_ref, send_ref, carry_ref, sums_ref, part_ref, chunk_ref, base_ref, onward_ref, backward_ref, xt_ref, sems,
):
    sources = (chunk_hbm, base_hbm, onward_hbm, backward_hbm, xt_hbm)
    targets = (chunk_ref, base_ref, onward_ref, backward_ref, xt_ref)
    copies = [pltpu.make_async_copy(a, b, sems.at[k]) for k, (a, b) in enumerate(zip(sources, targets))]
    for copy in copies:
        copy.start()
    me = slab_index()
    width = blocks * LANES
    sublane = lax.broadcasted_iota(jnp.int32, (CHUNKS, LANES), 0)
    slope = -jnp.exp(lograte_ref[...])
    slope2 = jnp.concatenate([slope, slope], axis=0)
    took = lambda s: got_ref[s % 2, s // 2, 2 * blocks : 2 * blocks + 1, :]
    between = [None] * slabs
    run = jnp.zeros((1, LANES), F32)
    for s in reversed(range(slabs)):
        between[s] = run
        run = jnp.where(s < me, run + took(s), 0.0)
    run = jnp.zeros((1, LANES), F32)
    carry_early = jnp.zeros((2 * blocks, LANES), F32)
    carry_late = jnp.zeros((2 * blocks, LANES), F32)
    for s in range(slabs):
        x = jnp.exp(slope2 * jnp.where(s < me, between[s], run)) * got_ref[s % 2, s // 2, 0 : 2 * blocks, :]
        carry_early = carry_early + jnp.where(s < me, x, 0.0)
        carry_late = carry_late + jnp.where(s > me, x, 0.0)
        run = jnp.where(s > me, run + took(s), 0.0)
    gains = jnp.concatenate([gain_ref[...], jnp.ones((blocks, LANES), F32)], axis=0)
    carry_ref[0] = carry_early * gains
    carry_ref[1] = carry_late * gains
    for copy in copies:
        copy.wait()

    for h in range(blocks):
        cols = slice(h * LANES, (h + 1) * LANES)
        rate = jnp.exp(lograte_ref[h : h + 1, :])
        gain = gain_ref[h : h + 1, :]
        end_d, end_g, through, head_d, head_g = [chunk_ref[k, :, cols] for k in range(5)]
        enter_d = chunk_entries(end_d, through, carry_ref[0, h : h + 1, :], sublane, 1)
        enter_g = chunk_entries(end_g, through, carry_ref[0, blocks + h : blocks + h + 1, :], sublane, 1)
        leave_d = chunk_entries(head_d, through, carry_ref[1, h : h + 1, :], sublane, -1)
        leave_g = chunk_entries(head_g, through, carry_ref[1, blocks + h : blocks + h + 1, :], sublane, -1)
        enter_low, leave_low = gain * enter_g, gain * leave_g
        low = []
        for j in range(STEPS):
            rows = slice(j * CHUNKS, (j + 1) * CHUNKS)
            low.append(gain * base_ref[rows, cols] + onward_ref[rows, cols] * enter_low + backward_ref[rows, cols] * leave_low)
        low = jnp.concatenate(low, axis=0).astype(BF16)
        low_ref[:, cols] = low
        product = jnp.dot(xt_ref[cols, :], low, preferred_element_type=F32)
        for k in range(LANES // 8):
            piece, third = divmod(h * (LANES // 8) + k, 3)
            dp, quarter = divmod(piece, 4)
            core, zh = divmod(quarter, 2)
            at = (dp * 2 + zh) * 24 + third * 8
            part_ref[core, at : at + 8, :] = product[k * 8 : k * 8 + 8, :]
        c = [chunk_ref[5 + k, :, cols] for k in range(12)]
        rate_sum = c[0] + leave_g * c[1] + enter_d * c[2] + (leave_g * enter_d + enter_g * leave_d) * c[3]
        rate_sum = rate_sum + leave_d * c[4] + enter_g * c[5]
        grad_sum = c[6] + enter_g * c[7] + leave_g * c[8]
        cross_sum = c[9] + enter_g * c[10] + leave_g * c[11]
        total = lambda v: jnp.sum(v, axis=0, keepdims=True)
        sums_ref[0:1, cols] = gain * total(grad_sum)
        sums_ref[1:2, cols] = rate * (jnp.exp(-2.0 * rate) / gain * total(cross_sum) - total(rate_sum))
    share = width // rows_dp
    half = width // 2
    sums_ref[0:2, width:] = jnp.zeros((2, sums_ref.shape[1] - width), F32)
    for dp in range(rows_dp):
        for k in range(2):
            window = sums_ref[k : k + 1, dp * share : dp * share + LANES]
            for core in range(2):
                part_ref[core, half + k * rows_dp + dp : half + k * rows_dp + dp + 1, :] = window
    core = lax.axis_index("core")
    keep_ref[...] = part_ref[core]
    send_ref[...] = part_ref[1 - core]


def pair_kernel(rows_dp, star_ref, keep_ref, sent_ref, out_ref):
    other = 1 - lax.axis_index("core")
    half = keep_ref.shape[0] - 2 * rows_dp
    star = jnp.broadcast_to(star_ref[0].astype(F32), (1, LANES))
    for dp in range(rows_dp):
        extra = []
        for k in range(2):
            at = slice(half + k * rows_dp + dp, half + k * rows_dp + dp + 1)
            extra.append(keep_ref[at, :] + sent_ref[other, at, :])
        tile = jnp.concatenate(extra + [star], axis=0)
        for zh in range(2):
            piece = dp * 2 + zh
            rows = slice(piece * 24, piece * 24 + 24)
            out_ref[piece, 0:24, :] = keep_ref[rows, :] + sent_ref[other, rows, :]
            out_ref[piece, 24:27, :] = tile


def series_kernel(blocks, low_ref, cot_ref, w_ref, dx_ref):
    row = lax.broadcasted_iota(jnp.int32, (SLAB, SLAB), 0)
    lane = lax.broadcasted_iota(jnp.int32, (SLAB, SLAB), 1)
    unorder = (row == (lane % CHUNKS) * STEPS + lane // CHUNKS).astype(F32).astype(BF16)
    for h in range(blocks):
        cols = slice(h * LANES, (h + 1) * LANES)
        low = jnp.dot(unorder, low_ref[:, cols], preferred_element_type=F32).astype(BF16)
        back = lax.dot_general(low, w_ref[cols, :], (((1,), (1,)), ((), ())), preferred_element_type=F32)
        dx_ref[0, :, cols] = (cot_ref[0, :, cols].astype(F32) + back).astype(BF16)


def piece_kernel(norm, got_ref, out_ref):
    first = (lax.axis_index("core") * 2 + lax.axis_index("zh")) * 4
    total = got_ref[0, 0:24, :]
    logs = got_ref[0, 25:26, :]
    stars = [jnp.zeros((1, LANES), F32)] * 4
    for s in range(got_ref.shape[0]):
        if s:
            total = total + got_ref[s, 0:24, :]
            logs = logs + got_ref[s, 25:26, :]
        for k in range(4):
            hit = got_ref[s, 26:27, :] == (first + k).astype(F32)
            stars[k] = stars[k] + jnp.where(hit, got_ref[s, 24:25, :], 0.0)
    total = total * norm
    tail = jnp.concatenate(stars + [logs] + [jnp.zeros((3, LANES), F32)], axis=0) * norm
    for d in range(out_ref.shape[0]):
        out_ref[d, 0:24, :] = total
        out_ref[d, 24:32, :] = tail


def final_kernel(got_ref, weight_ref, star_ref, log_ref):
    share = star_ref.shape[1]
    for core in range(2):
        for zh in range(2):
            q = core * 2 + zh
            total = got_ref[core, zh]
            for y in range(1, got_ref.shape[1] // 2):
                total = total + got_ref[core, y * 2 + zh]
            weight_ref[q * 24 : q * 24 + 24, :] = total[0:24, :]
            star_ref[q * 4 : q * 4 + 4, :] = total[24:28, 0:share]
            if q == 0:
                log_ref[...] = total[28:29, 0:share]


def body(series, cotangent, step_times, seg_starts, star_of_row, block_weight, star_table, log_rate):
    _, slab_len, width = series.shape
    blocks = width // LANES
    slabs = lax.axis_size(("y", "zh", "core"))
    rows_dp = lax.axis_size(("x", "zl"))
    norm = float(1.0 / (rows_dp * slabs * slab_len) ** 0.5)
    chips = slabs // 2
    log_blocks = log_rate.reshape(blocks, LANES)
    gain = jnp.sqrt(-jnp.expm1(-2.0 * jnp.exp(log_blocks)))
    smem = pl.BlockSpec(memory_space=pltpu.SMEM)
    vmem = pl.BlockSpec(memory_space=pltpu.VMEM)
    hbm = pl.BlockSpec(memory_space=pl.ANY)
    params = pltpu.CompilerParams(vmem_limit_bytes=24 * 1024 * 1024)
    big = pltpu.CompilerParams(vmem_limit_bytes=60 * 1024 * 1024)
    shape = jax.ShapeDtypeStruct
    common = (seg_starts, star_of_row, step_times, series, cotangent, block_weight, star_table, log_blocks)
    ends = pl.pallas_call(
        functools.partial(ends_kernel, blocks, chips),
        out_shape=shape((chips, 32, LANES), F32),
        in_specs=[hbm] * 8,
        out_specs=vmem,
        scratch_shapes=[pltpu.VMEM((2, 32, LANES), F32)]
        + [pltpu.SMEM(v.shape, v.dtype) for v in common[:2]]
        + [pltpu.VMEM(v.shape, v.dtype) for v in common[2:]]
        + [pltpu.SemaphoreType.DMA((8,))],
        compiler_params=big,
        name="slab_ends",
    )(*common)
    got = lax.all_gather(lax.all_to_all(ends, ("y", "zh"), 0, 0), "core")
    wide = shape((slab_len, width), F32)
    base, onward, backward, xt, chunk = pl.pallas_call(
        functools.partial(local_kernel, blocks),
        out_shape=[wide, wide, wide, shape((width, slab_len), BF16), shape((17, CHUNKS, width), F32)],
        in_specs=[smem, smem] + [vmem] * 7,
        out_specs=[vmem] * 5,
        compiler_params=params,
        cost_estimate=pl.CostEstimate(flops=20_000_000, bytes_accessed=4_000_000, transcendentals=200_000),
        name="local_scans",
    )(*common, gain)
    low, keep, send = pl.pallas_call(
        functools.partial(combine_kernel, blocks, slabs, rows_dp),
        out_shape=[shape((slab_len, width), BF16)] + [shape((width // 2 + 2 * rows_dp, LANES), F32)] * 2,
        in_specs=[vmem] * 3 + [hbm] * 5,
        out_specs=[vmem] * 3,
        scratch_shapes=[
            pltpu.VMEM((2, 2 * blocks, LANES), F32),
            pltpu.VMEM((8, width + LANES), F32),
            pltpu.VMEM((2, width // 2 + 2 * rows_dp, LANES), F32),
        ]
        + [pltpu.VMEM(v.shape, v.dtype) for v in (chunk, base, onward, backward, xt)]
        + [pltpu.SemaphoreType.DMA((5,))],
        compiler_params=big,
        name="gradients",
    )(log_blocks, gain, got, chunk, base, onward, backward, xt)
    sent = lax.all_gather(send, "core")
    pair = pl.pallas_call(
        functools.partial(pair_kernel, rows_dp),
        out_shape=shape((rows_dp * 2, 27, LANES), F32),
        in_specs=[smem, vmem, vmem],
        out_specs=vmem,
        compiler_params=params,
        name="pair_sum",
    )(star_of_row, keep, sent)
    grad_series = pl.pallas_call(
        functools.partial(series_kernel, blocks),
        out_shape=shape(series.shape, BF16),
        in_specs=[vmem] * 3,
        out_specs=vmem,
        compiler_params=params,
        cost_estimate=pl.CostEstimate(flops=100_000_000, bytes_accessed=1_600_000, transcendentals=0),
        name="series_gradient",
    )(low, cotangent, block_weight)
    pieces = lax.all_to_all(pair, ("x", "zl", "zh"), 0, 0)
    piece = pl.pallas_call(
        functools.partial(piece_kernel, norm),
        out_shape=jax.ShapeDtypeStruct((slabs // 2, 32, LANES), F32),
        in_specs=[vmem],
        out_specs=vmem,
        compiler_params=params,
        name="sum_pieces",
    )(pieces)
    spread = lax.all_to_all(piece, ("y", "zh"), 0, 0)
    both = lax.all_gather(spread, "core")
    share = width // rows_dp
    grad_weight, grad_star, grad_log = pl.pallas_call(
        final_kernel,
        out_shape=[
            jax.ShapeDtypeStruct((share, LANES), F32),
            jax.ShapeDtypeStruct((star_table.shape[0], share), F32),
            jax.ShapeDtypeStruct((1, share), F32),
        ],
        in_specs=[vmem],
        out_specs=[vmem] * 3,
        compiler_params=params,
        name="outputs",
    )(both)
    return grad_series, grad_weight, grad_star, grad_log.reshape(share)


def solution(mesh):
    fine = Mesh(mesh.devices.reshape(4, 4, 8, 2, 2), ("x", "zl", "y", "zh", "core"))
    dp, ctx = ("x", "zl"), ("y", "zh", "core")
    in_specs = (P(dp, ctx, None), P(dp, ctx, None), P(dp, ctx), P(dp, None), P(dp), P(), P(), P())
    out_specs = (P(dp, ctx, None), P(dp, None), P(None, dp), P(dp))
    return jax.shard_map(body, mesh=fine, in_specs=in_specs, out_specs=out_specs, check_vma=False)
```

```python
import functools
import jax
import jax.numpy as jnp
from jax import lax
from jax.experimental import pallas as pl
from jax.experimental.pallas import tpu as pltpu
from jax.sharding import Mesh, PartitionSpec as P

SLAB = 128
LANES = 128
CHUNKS = 8
STEPS = SLAB // CHUNKS
FAR = 1e9
GROUPS = 4
F32 = jnp.float32
BF16 = jnp.bfloat16


def slab_index():
    return (lax.axis_index("y") * 2 + lax.axis_index("zh")) * 2 + lax.axis_index("core")


def elapsed_row(starts_ref, times_ref, me):
    position = lax.broadcasted_iota(jnp.int32, (1, SLAB), 1) + me * SLAB
    reset = position == starts_ref[0, 0]
    for k in range(1, starts_ref.shape[1]):
        reset = jnp.logical_or(reset, position == starts_ref[0, k])
    return jnp.where(reset, FAR, times_ref[...])


def ends_kernel(
    blocks, chips, starts_hbm, star_hbm, times_hbm, series_hbm, cot_hbm, w_hbm, table_hbm, lograte_hbm,
    out_ref, ends_ref, starts_ref, star_ref, times_ref, series_ref, cot_ref, w_ref, table_ref, lograte_ref, sems,
):
    sources = (starts_hbm, star_hbm, times_hbm, table_hbm, lograte_hbm, series_hbm, w_hbm, cot_hbm)
    targets = (starts_ref, star_ref, times_ref, table_ref, lograte_ref, series_ref, w_ref, cot_ref)
    copies = [pltpu.make_async_copy(a, b, sems.at[k]) for k, (a, b) in enumerate(zip(sources, targets))]
    for copy in copies:
        copy.start()
    core = lax.axis_index("core")
    me = slab_index()
    for copy in copies[:3]:
        copy.wait()
    elapsed = elapsed_row(starts_ref, times_ref, me)
    row = lax.broadcasted_iota(jnp.int32, (SLAB, SLAB), 0)
    lane = lax.broadcasted_iota(jnp.int32, (SLAB, SLAB), 1)
    spread = jnp.broadcast_to(elapsed, (SLAB, SLAB))
    to_end = jnp.sum(jnp.where(lane > row, spread, 0.0), axis=1, keepdims=True)
    from_start = jnp.sum(jnp.where(lane <= row, spread, 0.0), axis=1, keepdims=True)
    to_end = jnp.broadcast_to(to_end, (SLAB, LANES))
    from_start = jnp.broadcast_to(from_start, (SLAB, LANES))
    total = jnp.sum(elapsed, axis=1, keepdims=True)
    for copy in copies[3:]:
        copy.wait()
    bias = table_ref[pl.ds(star_ref[0], 1), :]
    for h in range(blocks):
        cols = slice(h * LANES, (h + 1) * LANES)
        proj = jnp.dot(series_ref[0, :, cols], w_ref[cols, :], preferred_element_type=F32) + bias[:, cols]
        grad = cot_ref[0, :, cols].astype(F32)
        slope = -jnp.exp(lograte_ref[h : h + 1, :])
        late = jnp.exp(slope * to_end)
        early = jnp.exp(slope * from_start)
        ends_ref[0, h : h + 1, :] = jnp.sum(late * proj, axis=0, keepdims=True)
        ends_ref[0, blocks + h : blocks + h + 1, :] = jnp.sum(late * grad, axis=0, keepdims=True)
        ends_ref[1, h : h + 1, :] = jnp.sum(early * proj, axis=0, keepdims=True)
        ends_ref[1, blocks + h : blocks + h + 1, :] = jnp.sum(early * grad, axis=0, keepdims=True)
    tail = jnp.broadcast_to(total, (8, LANES))
    ends_ref[0, 2 * blocks : 2 * blocks + 8, :] = tail
    ends_ref[1, 2 * blocks : 2 * blocks + 8, :] = tail
    for chip in range(chips):
        out_ref[chip] = ends_ref[jnp.where(2 * chip + 1 - core > me, 0, 1)]


def shift(x, k, fill, sublane):
    if k > 0:
        return jnp.where(sublane < k, fill, pltpu.roll(x, k, 0))
    return jnp.where(sublane >= CHUNKS + k, fill, pltpu.roll(x, CHUNKS + k, 0))


def chunk_entries(ends, through, sublane, sign):
    for k in (1, 2, 4):
        ends = ends + through * shift(ends, sign * k, 0.0, sublane)
        through = through * shift(through, sign * k, 1.0, sublane)
    return shift(ends, sign, 0.0, sublane), shift(through, sign, 1.0, sublane)


def local_kernel(
    blocks, starts_ref, star_ref, times_ref, series_ref, cot_ref, w_ref, table_ref, lograte_ref, gain_ref,
    base_ref, onward_ref, backward_ref, xt_ref, table_sums_ref,
):
    me = slab_index()
    elapsed = elapsed_row(starts_ref, times_ref, me)
    row = lax.broadcasted_iota(jnp.int32, (SLAB, SLAB), 0)
    lane = lax.broadcasted_iota(jnp.int32, (SLAB, SLAB), 1)
    sublane = lax.broadcasted_iota(jnp.int32, (CHUNKS, LANES), 0)
    time_of_row = (row % CHUNKS) * STEPS + row // CHUNKS
    order = (lane == time_of_row).astype(F32).astype(BF16)
    gap = jnp.sum(jnp.where(lane == time_of_row, jnp.broadcast_to(elapsed, (SLAB, SLAB)), 0.0), axis=1, keepdims=True)
    gap = jnp.broadcast_to(gap, (SLAB, LANES))
    bias = table_ref[pl.ds(star_ref[0], 1), :]
    for h in range(blocks):
        cols = slice(h * LANES, (h + 1) * LANES)
        rate = jnp.exp(lograte_ref[h : h + 1, :])
        gain = gain_ref[h : h + 1, :]
        x = jnp.dot(order, series_ref[0, :, cols], preferred_element_type=F32)
        xt_ref[cols, :] = x.T.astype(BF16)
        grad = jnp.dot(order, cot_ref[0, :, cols], preferred_element_type=F32)
        proj = jnp.dot(x.astype(BF16), w_ref[cols, :], preferred_element_type=F32) + bias[:, cols]
        drive = gain * proj
        decay = jnp.exp(-rate * gap)
        tiles = lambda v: [v[j * CHUNKS : (j + 1) * CHUNKS, :] for j in range(STEPS)]
        a, d, g, pr, dt = tiles(decay), tiles(drive), tiles(grad), tiles(proj), tiles(gap)
        zero = jnp.zeros((CHUNKS, LANES), F32)
        before_d, before_g, through = [zero], [zero], [a[0]]
        state_d, state_g = d[0], g[0]
        for j in range(1, STEPS):
            before_d.append(a[j] * state_d)
            before_g.append(a[j] * state_g)
            state_d = before_d[j] + d[j]
            state_g = before_g[j] + g[j]
            through.append(a[j] * through[j - 1])
        after_d, after_g, back = [None] * STEPS, [None] * STEPS, [None] * STEPS
        after_d[-1], after_g[-1], back[-1] = d[-1], g[-1], jnp.ones((CHUNKS, LANES), F32)
        for j in reversed(range(STEPS - 1)):
            after_d[j] = a[j + 1] * after_d[j + 1] + d[j]
            after_g[j] = a[j + 1] * after_g[j + 1] + g[j]
            back[j] = a[j + 1] * back[j + 1]
        enter_d, onto = chunk_entries(state_d, through[-1], sublane, 1)
        enter_g, _ = chunk_entries(state_g, through[-1], sublane, 1)
        leave_d, off = chunk_entries(a[0] * after_d[0], through[-1], sublane, -1)
        leave_g, _ = chunk_entries(a[0] * after_g[0], through[-1], sublane, -1)
        sums = [zero] * 12
        for j in range(STEPS):
            kept_d = before_d[j] + through[j] * enter_d
            kept_g = before_g[j] + through[j] * enter_g
            later_d = after_d[j] + back[j] * leave_d
            later_g = after_g[j] + back[j] * leave_g
            on, off_j = through[j] * onto, back[j] * off
            base = later_g + kept_g + g[j]
            rows = slice(h * LANES + j * CHUNKS, h * LANES + (j + 1) * CHUNKS)
            base_ref[rows, :] = gain * base
            onward_ref[rows, :] = gain * on
            backward_ref[rows, :] = gain * off_j
            dt_on, dt_off = dt[j] * on, dt[j] * off_j
            terms = (
                dt[j] * (later_g * kept_d + kept_g * later_d),
                dt_off * kept_d,
                dt_on * later_g,
                dt_on * off_j,
                dt_off * kept_g,
                dt_on * later_d,
                base,
                on,
                off_j,
                base * pr[j],
                on * pr[j],
                off_j * pr[j],
            )
            sums = [s + t for s, t in zip(sums, terms)]
        for k, v in enumerate(sums):
            table_sums_ref[k, h : h + 1, :] = jnp.sum(v, axis=0, keepdims=True)


def combine_kernel(
    blocks, slabs, rows_dp, lograte_ref, gain_ref, got_ref, sums_hbm, base_hbm, onward_hbm, backward_hbm, xt_hbm,
    low_hbm, keep_hbm, send_hbm, part_ref, low_ref, sums_ref, base_ref, onward_ref, backward_ref, xt_ref, sum_sem, sems, out_sems,
):
    groups = GROUPS
    rows_in = blocks // groups * LANES
    rows_out = rows_in // 2
    half = blocks * LANES // 2
    sums_copy = pltpu.make_async_copy(sums_hbm, sums_ref, sum_sem.at[0])
    sums_copy.start()
    pairs = ((base_hbm, base_ref), (onward_hbm, onward_ref), (backward_hbm, backward_ref), (xt_hbm, xt_ref))
    loads = []
    for group in range(groups):
        rows = slice(group * rows_in, (group + 1) * rows_in)
        loads.append([pltpu.make_async_copy(a.at[rows], b.at[rows], sems.at[group, k]) for k, (a, b) in enumerate(pairs)])
        for copy in loads[-1]:
            copy.start()
    me = slab_index()
    mine = lax.axis_index("core")
    slope = -jnp.exp(lograte_ref[...])
    slope2 = jnp.concatenate([slope, slope], axis=0)
    took = lambda s: got_ref[s % 2, s // 2, 2 * blocks : 2 * blocks + 1, :]
    between = [None] * slabs
    run = jnp.zeros((1, LANES), F32)
    for s in reversed(range(slabs)):
        between[s] = run
        run = jnp.where(s < me, run + took(s), 0.0)
    run = jnp.zeros((1, LANES), F32)
    carry_early = jnp.zeros((2 * blocks, LANES), F32)
    carry_late = jnp.zeros((2 * blocks, LANES), F32)
    for s in range(slabs):
        x = jnp.exp(slope2 * jnp.where(s < me, between[s], run)) * got_ref[s % 2, s // 2, 0 : 2 * blocks, :]
        carry_early = carry_early + jnp.where(s < me, x, 0.0)
        carry_late = carry_late + jnp.where(s > me, x, 0.0)
        run = jnp.where(s > me, run + took(s), 0.0)
    gain = gain_ref[...]
    early_d, early_g = gain * carry_early[0:blocks], carry_early[blocks:]
    late_d, late_g = gain * carry_late[0:blocks], carry_late[blocks:]
    sums_copy.wait()
    c = [sums_ref[k, 0:blocks, :] for k in range(12)]
    rate_sum = c[0] + late_g * c[1] + early_d * c[2] + (late_g * early_d + early_g * late_d) * c[3]
    rate_sum = rate_sum + late_d * c[4] + early_g * c[5]
    grad_sum = c[6] + early_g * c[7] + late_g * c[8]
    cross_sum = c[9] + early_g * c[10] + late_g * c[11]
    proj_sum = gain * grad_sum
    log_sum = jnp.exp(2.0 * slope) / gain * cross_sum - rate_sum
    log_sum = -slope * log_sum
    for core in range(2):
        part_ref[core, half : half + blocks, :] = proj_sum
        part_ref[core, half + 16 : half + 16 + blocks, :] = log_sum

    stores = []
    for group in range(groups):
        for copy in loads[group]:
            copy.wait()
        for h in range(group * blocks // groups, (group + 1) * blocks // groups):
            rows = slice(h * LANES, (h + 1) * LANES)
            low = base_ref[rows, :] + onward_ref[rows, :] * early_g[h : h + 1, :] + backward_ref[rows, :] * late_g[h : h + 1, :]
            low = low.astype(BF16)
            low_ref[rows, :] = low
            product = jnp.dot(xt_ref[rows, :], low, preferred_element_type=F32)
            for k in range(LANES // 8):
                piece, third = divmod(h * (LANES // 8) + k, 3)
                dp, quarter = divmod(piece, 4)
                core, zh = divmod(quarter, 2)
                at = (dp * 2 + zh) * 24 + third * 8
                part_ref[core, at : at + 8, :] = product[k * 8 : k * 8 + 8, :]
        end = half + 32 if group == groups - 1 else (group + 1) * rows_out
        rows = slice(group * rows_out, end)
        stores.append(pltpu.make_async_copy(part_ref.at[1 - mine, rows], send_hbm.at[rows], out_sems.at[group, 0]))
        stores.append(pltpu.make_async_copy(part_ref.at[mine, rows], keep_hbm.at[rows], out_sems.at[group, 1]))
        rows = slice(group * rows_in, (group + 1) * rows_in)
        stores.append(pltpu.make_async_copy(low_ref.at[rows], low_hbm.at[rows], out_sems.at[group, 2]))
        for copy in stores[-3:]:
            copy.start()
    for copy in stores:
        copy.wait()


def pair_kernel(rows_dp, star_ref, keep_ref, sent_ref, out_ref, flat_ref):
    other = 1 - lax.axis_index("core")
    half = keep_ref.shape[0] - 32
    width = 2 * half
    share = width // rows_dp
    flat_ref[0:2, width:] = jnp.zeros((2, flat_ref.shape[1] - width), F32)
    for k in range(2):
        table = keep_ref[half + 16 * k : half + 16 * k + 16, :] + sent_ref[other, half + 16 * k : half + 16 * k + 16, :]
        for h in range(width // LANES):
            flat_ref[k : k + 1, h * LANES : (h + 1) * LANES] = table[h : h + 1, :]
    star = jnp.broadcast_to(star_ref[0].astype(F32), (1, LANES))
    for dp in range(rows_dp):
        window = flat_ref[0:2, dp * share : dp * share + LANES]
        tile = jnp.concatenate([window, star], axis=0)
        for zh in range(2):
            piece = dp * 2 + zh
            rows = slice(piece * 24, piece * 24 + 24)
            out_ref[piece, 0:24, :] = keep_ref[rows, :] + sent_ref[other, rows, :]
            out_ref[piece, 24:27, :] = tile


def series_kernel(blocks, low_ref, cot_ref, w_ref, dx_ref):
    row = lax.broadcasted_iota(jnp.int32, (SLAB, SLAB), 0)
    lane = lax.broadcasted_iota(jnp.int32, (SLAB, SLAB), 1)
    unorder = (row == (lane % CHUNKS) * STEPS + lane // CHUNKS).astype(F32).astype(BF16)
    for h in range(blocks):
        cols = slice(h * LANES, (h + 1) * LANES)
        low = jnp.dot(unorder, low_ref[cols, :], preferred_element_type=F32).astype(BF16)
        back = lax.dot_general(low, w_ref[cols, :], (((1,), (1,)), ((), ())), preferred_element_type=F32)
        dx_ref[0, :, cols] = (cot_ref[0, :, cols].astype(F32) + back).astype(BF16)


def piece_kernel(norm, got_ref, out_ref):
    first = (lax.axis_index("core") * 2 + lax.axis_index("zh")) * 4
    total = got_ref[0, 0:24, :]
    logs = got_ref[0, 25:26, :]
    stars = [jnp.zeros((1, LANES), F32)] * 4
    for s in range(got_ref.shape[0]):
        if s:
            total = total + got_ref[s, 0:24, :]
            logs = logs + got_ref[s, 25:26, :]
        for k in range(4):
            hit = got_ref[s, 26:27, :] == (first + k).astype(F32)
            stars[k] = stars[k] + jnp.where(hit, got_ref[s, 24:25, :], 0.0)
    total = total * norm
    tail = jnp.concatenate(stars + [logs] + [jnp.zeros((3, LANES), F32)], axis=0) * norm
    for d in range(out_ref.shape[0]):
        out_ref[d, 0:24, :] = total
        out_ref[d, 24:32, :] = tail


def final_kernel(got_ref, weight_ref, star_ref, log_ref):
    share = star_ref.shape[1]
    for core in range(2):
        for zh in range(2):
            q = core * 2 + zh
            total = got_ref[core, zh]
            for y in range(1, got_ref.shape[1] // 2):
                total = total + got_ref[core, y * 2 + zh]
            weight_ref[q * 24 : q * 24 + 24, :] = total[0:24, :]
            star_ref[q * 4 : q * 4 + 4, :] = total[24:28, 0:share]
            if q == 0:
                log_ref[...] = total[28:29, 0:share]


def body(series, cotangent, step_times, seg_starts, star_of_row, block_weight, star_table, log_rate):
    _, slab_len, width = series.shape
    blocks = width // LANES
    slabs = lax.axis_size(("y", "zh", "core"))
    rows_dp = lax.axis_size(("x", "zl"))
    norm = float(1.0 / (rows_dp * slabs * slab_len) ** 0.5)
    chips = slabs // 2
    log_blocks = log_rate.reshape(blocks, LANES)
    gain = jnp.sqrt(-jnp.expm1(-2.0 * jnp.exp(log_blocks)))
    smem = pl.BlockSpec(memory_space=pltpu.SMEM)
    vmem = pl.BlockSpec(memory_space=pltpu.VMEM)
    hbm = pl.BlockSpec(memory_space=pl.ANY)
    params = pltpu.CompilerParams(vmem_limit_bytes=24 * 1024 * 1024)
    big = pltpu.CompilerParams(vmem_limit_bytes=60 * 1024 * 1024)
    shape = jax.ShapeDtypeStruct
    common = (seg_starts, star_of_row, step_times, series, cotangent, block_weight, star_table, log_blocks)
    ends = pl.pallas_call(
        functools.partial(ends_kernel, blocks, chips),
        out_shape=shape((chips, 32, LANES), F32),
        in_specs=[hbm] * 8,
        out_specs=vmem,
        scratch_shapes=[pltpu.VMEM((2, 32, LANES), F32)]
        + [pltpu.SMEM(v.shape, v.dtype) for v in common[:2]]
        + [pltpu.VMEM(v.shape, v.dtype) for v in common[2:]]
        + [pltpu.SemaphoreType.DMA((8,))],
        compiler_params=big,
        name="slab_ends",
    )(*common)
    got = lax.all_gather(lax.all_to_all(ends, ("y", "zh"), 0, 0), "core")
    wide = shape((width, slab_len), F32)
    base, onward, backward, xt, sums = pl.pallas_call(
        functools.partial(local_kernel, blocks),
        out_shape=[wide, wide, wide, shape((width, slab_len), BF16), shape((12, 16, LANES), F32)],
        in_specs=[smem, smem] + [vmem] * 7,
        out_specs=[vmem] * 5,
        compiler_params=big,
        cost_estimate=pl.CostEstimate(flops=20_000_000, bytes_accessed=4_000_000, transcendentals=200_000),
        name="local_scans",
    )(*common, gain)
    loaded = (base, onward, backward, xt)
    half_rows = width // 2 + 32
    low, keep, send = pl.pallas_call(
        functools.partial(combine_kernel, blocks, slabs, rows_dp),
        out_shape=[shape((width, slab_len), BF16)] + [shape((half_rows, LANES), F32)] * 2,
        in_specs=[vmem] * 3 + [hbm] * 5,
        out_specs=[hbm] * 3,
        scratch_shapes=[
            pltpu.VMEM((2, half_rows, LANES), F32),
            pltpu.VMEM((width, slab_len), BF16),
            pltpu.VMEM(sums.shape, F32),
        ]
        + [pltpu.VMEM(v.shape, v.dtype) for v in loaded]
        + [
            pltpu.SemaphoreType.DMA((1,)),
            pltpu.SemaphoreType.DMA((GROUPS, len(loaded))),
            pltpu.SemaphoreType.DMA((GROUPS, 3)),
        ],
        compiler_params=big,
        name="gradients",
    )(log_blocks, gain, got, sums, *loaded)
    sent = lax.all_gather(send, "core")
    pair = pl.pallas_call(
        functools.partial(pair_kernel, rows_dp),
        out_shape=shape((rows_dp * 2, 27, LANES), F32),
        in_specs=[smem, vmem, vmem],
        out_specs=vmem,
        scratch_shapes=[pltpu.VMEM((8, width + LANES), F32)],
        compiler_params=params,
        name="pair_sum",
    )(star_of_row, keep, sent)
    grad_series = pl.pallas_call(
        functools.partial(series_kernel, blocks),
        out_shape=shape(series.shape, BF16),
        in_specs=[vmem] * 3,
        out_specs=vmem,
        compiler_params=params,
        cost_estimate=pl.CostEstimate(flops=100_000_000, bytes_accessed=1_600_000, transcendentals=0),
        name="series_gradient",
    )(low, cotangent, block_weight)
    pieces = lax.all_to_all(pair, ("x", "zl", "zh"), 0, 0)
    piece = pl.pallas_call(
        functools.partial(piece_kernel, norm),
        out_shape=jax.ShapeDtypeStruct((slabs // 2, 32, LANES), F32),
        in_specs=[vmem],
        out_specs=vmem,
        compiler_params=params,
        name="sum_pieces",
    )(pieces)
    spread = lax.all_to_all(piece, ("y", "zh"), 0, 0)
    both = lax.all_gather(spread, "core")
    share = width // rows_dp
    grad_weight, grad_star, grad_log = pl.pallas_call(
        final_kernel,
        out_shape=[
            jax.ShapeDtypeStruct((share, LANES), F32),
            jax.ShapeDtypeStruct((star_table.shape[0], share), F32),
            jax.ShapeDtypeStruct((1, share), F32),
        ],
        in_specs=[vmem],
        out_specs=[vmem] * 3,
        compiler_params=params,
        name="outputs",
    )(both)
    return grad_series, grad_weight, grad_star, grad_log.reshape(share)


def solution(mesh):
    fine = Mesh(mesh.devices.reshape(4, 4, 8, 2, 2), ("x", "zl", "y", "zh", "core"))
    dp, ctx = ("x", "zl"), ("y", "zh", "core")
    in_specs = (P(dp, ctx, None), P(dp, ctx, None), P(dp, ctx), P(dp, None), P(dp), P(), P(), P())
    out_specs = (P(dp, ctx, None), P(dp, None), P(None, dp), P(dp))
    return jax.shard_map(body, mesh=fine, in_specs=in_specs, out_specs=out_specs, check_vma=False)
```

```python
import functools
import jax
import jax.numpy as jnp
from jax import lax
from jax.experimental import pallas as pl
from jax.experimental.pallas import tpu as pltpu
from jax.sharding import Mesh, PartitionSpec as P

SLAB = 128
LANES = 128
CHUNKS = 8
STEPS = SLAB // CHUNKS
FAR = 1e9
GROUPS = 4
F32 = jnp.float32
BF16 = jnp.bfloat16


def slab_index():
    chip = (lax.axis_index("yh") * 2 + lax.axis_index("yl")) * 2 + lax.axis_index("zh")
    return chip * 2 + lax.axis_index("core")


def elapsed_row(starts_ref, times_ref, me):
    position = lax.broadcasted_iota(jnp.int32, (1, SLAB), 1) + me * SLAB
    reset = position == starts_ref[0, 0]
    for k in range(1, starts_ref.shape[1]):
        reset = jnp.logical_or(reset, position == starts_ref[0, k])
    return jnp.where(reset, FAR, times_ref[...])


def ends_kernel(
    blocks, chips, starts_hbm, star_hbm, times_hbm, series_hbm, cot_hbm, w_hbm, table_hbm, lograte_hbm,
    out_ref, ends_ref, starts_ref, star_ref, times_ref, series_ref, cot_ref, w_ref, table_ref, lograte_ref, sems, group_sems,
):
    sources = (starts_hbm, star_hbm, times_hbm, table_hbm, lograte_hbm)
    targets = (starts_ref, star_ref, times_ref, table_ref, lograte_ref)
    copies = [pltpu.make_async_copy(a, b, sems.at[k]) for k, (a, b) in enumerate(zip(sources, targets))]
    span = blocks // GROUPS * LANES
    loads = []
    for group in range(GROUPS):
        part = slice(group * span, (group + 1) * span)
        views = (
            (series_hbm.at[:, :, part], series_ref.at[:, :, part]),
            (w_hbm.at[part], w_ref.at[part]),
            (cot_hbm.at[:, :, part], cot_ref.at[:, :, part]),
        )
        loads.append([pltpu.make_async_copy(a, b, group_sems.at[group, k]) for k, (a, b) in enumerate(views)])
    for copy in copies + sum(loads, []):
        copy.start()
    core = lax.axis_index("core")
    me = slab_index()
    for copy in copies[:3]:
        copy.wait()
    elapsed = elapsed_row(starts_ref, times_ref, me)
    row = lax.broadcasted_iota(jnp.int32, (SLAB, SLAB), 0)
    lane = lax.broadcasted_iota(jnp.int32, (SLAB, SLAB), 1)
    spread = jnp.broadcast_to(elapsed, (SLAB, SLAB))
    to_end = jnp.sum(jnp.where(lane > row, spread, 0.0), axis=1, keepdims=True)
    from_start = jnp.sum(jnp.where(lane <= row, spread, 0.0), axis=1, keepdims=True)
    to_end = jnp.broadcast_to(to_end, (SLAB, LANES))
    from_start = jnp.broadcast_to(from_start, (SLAB, LANES))
    total = jnp.sum(elapsed, axis=1, keepdims=True)
    for copy in copies[3:]:
        copy.wait()
    bias = table_ref[pl.ds(star_ref[0], 1), :]
    for h in range(blocks):
        if h % (blocks // GROUPS) == 0:
            for copy in loads[h // (blocks // GROUPS)]:
                copy.wait()
        cols = slice(h * LANES, (h + 1) * LANES)
        proj = jnp.dot(series_ref[0, :, cols], w_ref[cols, :], preferred_element_type=F32) + bias[:, cols]
        grad = cot_ref[0, :, cols].astype(F32)
        slope = -jnp.exp(lograte_ref[h : h + 1, :])
        late = jnp.exp(slope * to_end)
        early = jnp.exp(slope * from_start)
        ends_ref[0, h : h + 1, :] = jnp.sum(late * proj, axis=0, keepdims=True)
        ends_ref[0, blocks + h : blocks + h + 1, :] = jnp.sum(late * grad, axis=0, keepdims=True)
        ends_ref[1, h : h + 1, :] = jnp.sum(early * proj, axis=0, keepdims=True)
        ends_ref[1, blocks + h : blocks + h + 1, :] = jnp.sum(early * grad, axis=0, keepdims=True)
    tail = jnp.broadcast_to(total, (8, LANES))
    ends_ref[0, 2 * blocks : 2 * blocks + 8, :] = tail
    ends_ref[1, 2 * blocks : 2 * blocks + 8, :] = tail
    for chip in range(chips):
        out_ref[chip] = ends_ref[jnp.where(2 * chip + 1 - core > me, 0, 1)]


def shift(x, k, fill, sublane):
    if k > 0:
        return jnp.where(sublane < k, fill, pltpu.roll(x, k, 0))
    return jnp.where(sublane >= CHUNKS + k, fill, pltpu.roll(x, CHUNKS + k, 0))


def chunk_entries(ends, through, sublane, sign):
    for k in (1, 2, 4):
        ends = ends + through * shift(ends, sign * k, 0.0, sublane)
        through = through * shift(through, sign * k, 1.0, sublane)
    return shift(ends, sign, 0.0, sublane), shift(through, sign, 1.0, sublane)


def local_kernel(
    blocks, starts_ref, star_ref, times_ref, series_ref, cot_ref, w_ref, table_ref, lograte_ref, gain_ref,
    base_ref, xt_ref, table_sums_ref, reach_ref,
):
    me = slab_index()
    elapsed = elapsed_row(starts_ref, times_ref, me)
    row = lax.broadcasted_iota(jnp.int32, (SLAB, SLAB), 0)
    lane = lax.broadcasted_iota(jnp.int32, (SLAB, SLAB), 1)
    sublane = lax.broadcasted_iota(jnp.int32, (CHUNKS, LANES), 0)
    time_of_row = (row % CHUNKS) * STEPS + row // CHUNKS
    order = (lane == time_of_row).astype(F32).astype(BF16)
    gap = jnp.sum(jnp.where(lane == time_of_row, jnp.broadcast_to(elapsed, (SLAB, SLAB)), 0.0), axis=1, keepdims=True)
    gap = jnp.broadcast_to(gap, (SLAB, LANES))
    spread = jnp.broadcast_to(elapsed, (SLAB, SLAB))
    for k, mask in enumerate((lane <= time_of_row, lane > time_of_row)):
        reach = jnp.sum(jnp.where(mask, spread, 0.0), axis=1, keepdims=True)
        reach_ref[k] = jnp.broadcast_to(reach, (SLAB, LANES))
    bias = table_ref[pl.ds(star_ref[0], 1), :]
    for h in range(blocks):
        cols = slice(h * LANES, (h + 1) * LANES)
        rate = jnp.exp(lograte_ref[h : h + 1, :])
        gain = gain_ref[h : h + 1, :]
        x = jnp.dot(order, series_ref[0, :, cols], preferred_element_type=F32)
        xt_ref[cols, :] = x.T.astype(BF16)
        grad = jnp.dot(order, cot_ref[0, :, cols], preferred_element_type=F32)
        proj = jnp.dot(x.astype(BF16), w_ref[cols, :], preferred_element_type=F32) + bias[:, cols]
        drive = gain * proj
        decay = jnp.exp(-rate * gap)
        tiles = lambda v: [v[j * CHUNKS : (j + 1) * CHUNKS, :] for j in range(STEPS)]
        a, d, g, pr, dt = tiles(decay), tiles(drive), tiles(grad), tiles(proj), tiles(gap)
        zero = jnp.zeros((CHUNKS, LANES), F32)
        before_d, before_g, through = [zero], [zero], [a[0]]
        state_d, state_g = d[0], g[0]
        for j in range(1, STEPS):
            before_d.append(a[j] * state_d)
            before_g.append(a[j] * state_g)
            state_d = before_d[j] + d[j]
            state_g = before_g[j] + g[j]
            through.append(a[j] * through[j - 1])
        after_d, after_g, back = [None] * STEPS, [None] * STEPS, [None] * STEPS
        after_d[-1], after_g[-1], back[-1] = d[-1], g[-1], jnp.ones((CHUNKS, LANES), F32)
        for j in reversed(range(STEPS - 1)):
            after_d[j] = a[j + 1] * after_d[j + 1] + d[j]
            after_g[j] = a[j + 1] * after_g[j + 1] + g[j]
            back[j] = a[j + 1] * back[j + 1]
        enter_d, onto = chunk_entries(state_d, through[-1], sublane, 1)
        enter_g, _ = chunk_entries(state_g, through[-1], sublane, 1)
        leave_d, off = chunk_entries(a[0] * after_d[0], through[-1], sublane, -1)
        leave_g, _ = chunk_entries(a[0] * after_g[0], through[-1], sublane, -1)
        sums = [zero] * 12
        for j in range(STEPS):
            kept_d = before_d[j] + through[j] * enter_d
            kept_g = before_g[j] + through[j] * enter_g
            later_d = after_d[j] + back[j] * leave_d
            later_g = after_g[j] + back[j] * leave_g
            on, off_j = through[j] * onto, back[j] * off
            base = later_g + kept_g + g[j]
            rows = slice(h * LANES + j * CHUNKS, h * LANES + (j + 1) * CHUNKS)
            base_ref[rows, :] = gain * base
            dt_on, dt_off = dt[j] * on, dt[j] * off_j
            terms = (
                dt[j] * (later_g * kept_d + kept_g * later_d),
                dt_off * kept_d,
                dt_on * later_g,
                dt_on * off_j,
                dt_off * kept_g,
                dt_on * later_d,
                base,
                on,
                off_j,
                base * pr[j],
                on * pr[j],
                off_j * pr[j],
            )
            sums = [s + t for s, t in zip(sums, terms)]
        for k, v in enumerate(sums):
            table_sums_ref[k, h : h + 1, :] = jnp.sum(v, axis=0, keepdims=True)


def combine_kernel(
    blocks, slabs, rows_dp, lograte_ref, gain_ref, got_ref, sums_ref, base_ref, xt_ref, reach_ref,
    low_ref, keep_ref, send_ref, part_ref,
):
    half = blocks * LANES // 2
    me = slab_index()
    mine = lax.axis_index("core")
    slope = -jnp.exp(lograte_ref[...])
    slope2 = jnp.concatenate([slope, slope], axis=0)
    took = lambda s: got_ref[s % 2, s // 2, 2 * blocks : 2 * blocks + 1, :]
    between = [None] * slabs
    run = jnp.zeros((1, LANES), F32)
    for s in reversed(range(slabs)):
        between[s] = run
        run = jnp.where(s < me, run + took(s), 0.0)
    run = jnp.zeros((1, LANES), F32)
    carry_early = jnp.zeros((2 * blocks, LANES), F32)
    carry_late = jnp.zeros((2 * blocks, LANES), F32)
    for s in range(slabs):
        x = jnp.exp(slope2 * jnp.where(s < me, between[s], run)) * got_ref[s % 2, s // 2, 0 : 2 * blocks, :]
        carry_early = carry_early + jnp.where(s < me, x, 0.0)
        carry_late = carry_late + jnp.where(s > me, x, 0.0)
        run = jnp.where(s > me, run + took(s), 0.0)
    gain = gain_ref[...]
    early_d, early_g = gain * carry_early[0:blocks], carry_early[blocks:]
    late_d, late_g = gain * carry_late[0:blocks], carry_late[blocks:]
    c = [sums_ref[k, 0:blocks, :] for k in range(12)]
    rate_sum = c[0] + late_g * c[1] + early_d * c[2] + (late_g * early_d + early_g * late_d) * c[3]
    rate_sum = rate_sum + late_d * c[4] + early_g * c[5]
    grad_sum = c[6] + early_g * c[7] + late_g * c[8]
    cross_sum = c[9] + early_g * c[10] + late_g * c[11]
    proj_sum = gain * grad_sum
    log_sum = jnp.exp(2.0 * slope) / gain * cross_sum - rate_sum
    log_sum = -slope * log_sum
    for core in range(2):
        part_ref[core, half : half + blocks, :] = proj_sum
        part_ref[core, half + 16 : half + 16 + blocks, :] = log_sum

    enter, leave = gain * early_g, gain * late_g
    from_start, to_end = reach_ref[0], reach_ref[1]
    for h in range(blocks):
        rows = slice(h * LANES, (h + 1) * LANES)
        row = slice(h, h + 1)
        low = base_ref[rows, :] + jnp.exp(slope[row] * from_start) * enter[row] + jnp.exp(slope[row] * to_end) * leave[row]
        low = low.astype(BF16)
        low_ref[rows, :] = low
        product = jnp.dot(xt_ref[rows, :], low, preferred_element_type=F32)
        for k in range(LANES // 8):
            piece, third = divmod(h * (LANES // 8) + k, 3)
            dp, quarter = divmod(piece, 4)
            core, yl = divmod(quarter, 2)
            at = (dp * 2 + yl) * 24 + third * 8
            part_ref[core, at : at + 8, :] = product[k * 8 : k * 8 + 8, :]
    keep_ref[...] = part_ref[mine]
    send_ref[...] = part_ref[1 - mine]


def pair_kernel(rows_dp, star_ref, keep_ref, sent_ref, out_ref, flat_ref):
    other = 1 - lax.axis_index("core")
    half = keep_ref.shape[0] - 32
    width = 2 * half
    share = width // rows_dp
    flat_ref[0:2, width:] = jnp.zeros((2, flat_ref.shape[1] - width), F32)
    for k in range(2):
        table = keep_ref[half + 16 * k : half + 16 * k + 16, :] + sent_ref[other, half + 16 * k : half + 16 * k + 16, :]
        for h in range(width // LANES):
            flat_ref[k : k + 1, h * LANES : (h + 1) * LANES] = table[h : h + 1, :]
    star = jnp.broadcast_to(star_ref[0].astype(F32), (1, LANES))
    for dp in range(rows_dp):
        window = flat_ref[0:2, dp * share : dp * share + LANES]
        tile = jnp.concatenate([window, star], axis=0)
        for yl in range(2):
            piece = dp * 2 + yl
            rows = slice(piece * 24, piece * 24 + 24)
            out_ref[piece, 0:24, :] = keep_ref[rows, :] + sent_ref[other, rows, :]
            out_ref[piece, 24:27, :] = tile


def series_kernel(blocks, low_ref, cot_ref, w_ref, dx_ref):
    row = lax.broadcasted_iota(jnp.int32, (SLAB, SLAB), 0)
    lane = lax.broadcasted_iota(jnp.int32, (SLAB, SLAB), 1)
    unorder = (row == (lane % CHUNKS) * STEPS + lane // CHUNKS).astype(F32).astype(BF16)
    for h in range(blocks):
        cols = slice(h * LANES, (h + 1) * LANES)
        low = jnp.dot(unorder, low_ref[cols, :], preferred_element_type=F32).astype(BF16)
        back = lax.dot_general(low, w_ref[cols, :], (((1,), (1,)), ((), ())), preferred_element_type=F32)
        dx_ref[0, :, cols] = (cot_ref[0, :, cols].astype(F32) + back).astype(BF16)


def piece_kernel(norm, got_ref, out_ref):
    first = (lax.axis_index("core") * 2 + lax.axis_index("yl")) * 4
    total = got_ref[0, 0:24, :]
    logs = got_ref[0, 25:26, :]
    stars = [jnp.zeros((1, LANES), F32)] * 4
    for s in range(got_ref.shape[0]):
        if s:
            total = total + got_ref[s, 0:24, :]
            logs = logs + got_ref[s, 25:26, :]
        for k in range(4):
            hit = got_ref[s, 26:27, :] == (first + k).astype(F32)
            stars[k] = stars[k] + jnp.where(hit, got_ref[s, 24:25, :], 0.0)
    total = total * norm
    tail = jnp.concatenate(stars + [logs] + [jnp.zeros((3, LANES), F32)], axis=0) * norm
    for d in range(out_ref.shape[0]):
        out_ref[d, 0:24, :] = total
        out_ref[d, 24:32, :] = tail


def final_kernel(got_ref, weight_ref, star_ref, log_ref):
    share = star_ref.shape[1]
    for core in range(2):
        for yl in range(2):
            q = core * 2 + yl
            total = None
            for source in range(got_ref.shape[1]):
                if source // 2 % 2 == yl:
                    total = got_ref[core, source] if total is None else total + got_ref[core, source]
            weight_ref[q * 24 : q * 24 + 24, :] = total[0:24, :]
            star_ref[q * 4 : q * 4 + 4, :] = total[24:28, 0:share]
            if q == 0:
                log_ref[...] = total[28:29, 0:share]


def body(series, cotangent, step_times, seg_starts, star_of_row, block_weight, star_table, log_rate):
    _, slab_len, width = series.shape
    blocks = width // LANES
    slabs = lax.axis_size(("yh", "yl", "zh", "core"))
    rows_dp = lax.axis_size(("x", "zl"))
    norm = float(1.0 / (rows_dp * slabs * slab_len) ** 0.5)
    chips = slabs // 2
    log_blocks = log_rate.reshape(blocks, LANES)
    gain = jnp.sqrt(-jnp.expm1(-2.0 * jnp.exp(log_blocks)))
    smem = pl.BlockSpec(memory_space=pltpu.SMEM)
    vmem = pl.BlockSpec(memory_space=pltpu.VMEM)
    hbm = pl.BlockSpec(memory_space=pl.ANY)
    params = pltpu.CompilerParams(vmem_limit_bytes=24 * 1024 * 1024)
    big = pltpu.CompilerParams(vmem_limit_bytes=60 * 1024 * 1024)
    shape = jax.ShapeDtypeStruct
    common = (seg_starts, star_of_row, step_times, series, cotangent, block_weight, star_table, log_blocks)
    ends = pl.pallas_call(
        functools.partial(ends_kernel, blocks, chips),
        out_shape=shape((chips, 32, LANES), F32),
        in_specs=[hbm] * 8,
        out_specs=vmem,
        scratch_shapes=[pltpu.VMEM((2, 32, LANES), F32)]
        + [pltpu.SMEM(v.shape, v.dtype) for v in common[:2]]
        + [pltpu.VMEM(v.shape, v.dtype) for v in common[2:]]
        + [pltpu.SemaphoreType.DMA((5,)), pltpu.SemaphoreType.DMA((GROUPS, 3))],
        compiler_params=big,
        name="slab_ends",
    )(*common)
    got = lax.all_gather(lax.all_to_all(ends, ("yh", "yl", "zh"), 0, 0), "core")
    base, xt, sums, reach = pl.pallas_call(
        functools.partial(local_kernel, blocks),
        out_shape=[
            shape((width, slab_len), F32),
            shape((width, slab_len), BF16),
            shape((12, 16, LANES), F32),
            shape((2, slab_len, LANES), F32),
        ],
        in_specs=[smem, smem] + [vmem] * 7,
        out_specs=[vmem] * 4,
        compiler_params=params,
        cost_estimate=pl.CostEstimate(flops=20_000_000, bytes_accessed=4_000_000, transcendentals=200_000),
        name="local_scans",
    )(*common, gain)
    half_rows = width // 2 + 32
    low, keep, send = pl.pallas_call(
        functools.partial(combine_kernel, blocks, slabs, rows_dp),
        out_shape=[shape((width, slab_len), BF16)] + [shape((half_rows, LANES), F32)] * 2,
        in_specs=[vmem] * 7,
        out_specs=[vmem] * 3,
        scratch_shapes=[pltpu.VMEM((2, half_rows, LANES), F32)],
        compiler_params=params,
        name="gradients",
    )(log_blocks, gain, got, sums, base, xt, reach)
    sent = lax.all_gather(send, "core")
    pair = pl.pallas_call(
        functools.partial(pair_kernel, rows_dp),
        out_shape=shape((rows_dp * 2, 27, LANES), F32),
        in_specs=[smem, vmem, vmem],
        out_specs=vmem,
        scratch_shapes=[pltpu.VMEM((8, width + LANES), F32)],
        compiler_params=params,
        name="pair_sum",
    )(star_of_row, keep, sent)
    grad_series = pl.pallas_call(
        functools.partial(series_kernel, blocks),
        out_shape=shape(series.shape, BF16),
        in_specs=[vmem] * 3,
        out_specs=vmem,
        compiler_params=params,
        cost_estimate=pl.CostEstimate(flops=100_000_000, bytes_accessed=1_600_000, transcendentals=0),
        name="series_gradient",
    )(low, cotangent, block_weight)
    pieces = lax.all_to_all(pair, ("x", "zl", "yl"), 0, 0)
    piece = pl.pallas_call(
        functools.partial(piece_kernel, norm),
        out_shape=jax.ShapeDtypeStruct((slabs // 2, 32, LANES), F32),
        in_specs=[vmem],
        out_specs=vmem,
        compiler_params=params,
        name="sum_pieces",
    )(pieces)
    spread = lax.all_to_all(piece, ("yh", "yl", "zh"), 0, 0)
    both = lax.all_gather(spread, "core")
    share = width // rows_dp
    grad_weight, grad_star, grad_log = pl.pallas_call(
        final_kernel,
        out_shape=[
            jax.ShapeDtypeStruct((share, LANES), F32),
            jax.ShapeDtypeStruct((star_table.shape[0], share), F32),
            jax.ShapeDtypeStruct((1, share), F32),
        ],
        in_specs=[vmem],
        out_specs=[vmem] * 3,
        compiler_params=params,
        name="outputs",
    )(both)
    return grad_series, grad_weight, grad_star, grad_log.reshape(share)


def solution(mesh):
    fine = Mesh(mesh.devices.reshape(4, 4, 4, 2, 2, 2), ("x", "zl", "yh", "yl", "zh", "core"))
    dp, ctx = ("x", "zl"), ("yh", "yl", "zh", "core")
    in_specs = (P(dp, ctx, None), P(dp, ctx, None), P(dp, ctx), P(dp, None), P(dp), P(), P(), P())
    out_specs = (P(dp, ctx, None), P(dp, None), P(None, dp), P(dp))
    return jax.shard_map(body, mesh=fine, in_specs=in_specs, out_specs=out_specs, check_vma=False)
```

```python
import functools
import jax
import jax.numpy as jnp
from jax import lax
from jax.experimental import pallas as pl
from jax.experimental.pallas import tpu as pltpu
from jax.sharding import Mesh, PartitionSpec as P

SLAB = 128
LANES = 128
CHUNKS = 8
STEPS = SLAB // CHUNKS
FAR = 1e9
GROUPS = 4
PIECE = 26
F32 = jnp.float32
BF16 = jnp.bfloat16


def slab_index():
    chip = (lax.axis_index("yh") * 2 + lax.axis_index("yl")) * 2 + lax.axis_index("zh")
    return chip * 2 + lax.axis_index("core")


def elapsed_row(starts_ref, times_ref, me):
    position = lax.broadcasted_iota(jnp.int32, (1, SLAB), 1) + me * SLAB
    reset = position == starts_ref[0, 0]
    for k in range(1, starts_ref.shape[1]):
        reset = jnp.logical_or(reset, position == starts_ref[0, k])
    return jnp.where(reset, FAR, times_ref[...])


def ends_kernel(
    blocks, chips, starts_hbm, star_hbm, times_hbm, series_hbm, cot_hbm, w_hbm, table_hbm, lograte_hbm,
    out_ref, ends_ref, starts_ref, star_ref, times_ref, series_ref, cot_ref, w_ref, table_ref, lograte_ref, sems, group_sems,
):
    sources = (starts_hbm, star_hbm, times_hbm, table_hbm, lograte_hbm)
    targets = (starts_ref, star_ref, times_ref, table_ref, lograte_ref)
    copies = [pltpu.make_async_copy(a, b, sems.at[k]) for k, (a, b) in enumerate(zip(sources, targets))]
    span = blocks // GROUPS * LANES
    loads = []
    for group in range(GROUPS):
        part = slice(group * span, (group + 1) * span)
        views = (
            (series_hbm.at[:, :, part], series_ref.at[:, :, part]),
            (w_hbm.at[part], w_ref.at[part]),
            (cot_hbm.at[:, :, part], cot_ref.at[:, :, part]),
        )
        loads.append([pltpu.make_async_copy(a, b, group_sems.at[group, k]) for k, (a, b) in enumerate(views)])
    for copy in copies + sum(loads, []):
        copy.start()
    core = lax.axis_index("core")
    me = slab_index()
    for copy in copies[:3]:
        copy.wait()
    elapsed = elapsed_row(starts_ref, times_ref, me)
    row = lax.broadcasted_iota(jnp.int32, (SLAB, SLAB), 0)
    lane = lax.broadcasted_iota(jnp.int32, (SLAB, SLAB), 1)
    spread = jnp.broadcast_to(elapsed, (SLAB, SLAB))
    to_end = jnp.sum(jnp.where(lane > row, spread, 0.0), axis=1, keepdims=True)
    from_start = jnp.sum(jnp.where(lane <= row, spread, 0.0), axis=1, keepdims=True)
    to_end = jnp.broadcast_to(to_end, (SLAB, LANES))
    from_start = jnp.broadcast_to(from_start, (SLAB, LANES))
    total = jnp.sum(elapsed, axis=1, keepdims=True)
    for copy in copies[3:]:
        copy.wait()
    bias = table_ref[pl.ds(star_ref[0], 1), :]
    for h in range(blocks):
        if h % (blocks // GROUPS) == 0:
            for copy in loads[h // (blocks // GROUPS)]:
                copy.wait()
        cols = slice(h * LANES, (h + 1) * LANES)
        proj = jnp.dot(series_ref[0, :, cols], w_ref[cols, :], preferred_element_type=F32) + bias[:, cols]
        grad = cot_ref[0, :, cols].astype(F32)
        slope = -jnp.exp(lograte_ref[h : h + 1, :])
        late = jnp.exp(slope * to_end)
        early = jnp.exp(slope * from_start)
        ends_ref[0, h : h + 1, :] = jnp.sum(late * proj, axis=0, keepdims=True)
        ends_ref[0, blocks + h : blocks + h + 1, :] = jnp.sum(late * grad, axis=0, keepdims=True)
        ends_ref[1, h : h + 1, :] = jnp.sum(early * proj, axis=0, keepdims=True)
        ends_ref[1, blocks + h : blocks + h + 1, :] = jnp.sum(early * grad, axis=0, keepdims=True)
    tail = jnp.broadcast_to(total, (8, LANES))
    ends_ref[0, 2 * blocks : 2 * blocks + 8, :] = tail
    ends_ref[1, 2 * blocks : 2 * blocks + 8, :] = tail
    for chip in range(chips):
        out_ref[chip] = ends_ref[jnp.where(2 * chip + 1 - core > me, 0, 1)]


def shift(x, k, fill, sublane):
    if k > 0:
        return jnp.where(sublane < k, fill, pltpu.roll(x, k, 0))
    return jnp.where(sublane >= CHUNKS + k, fill, pltpu.roll(x, CHUNKS + k, 0))


def chunk_entries(ends, through, sublane, sign):
    for k in (1, 2, 4):
        ends = ends + through * shift(ends, sign * k, 0.0, sublane)
        through = through * shift(through, sign * k, 1.0, sublane)
    return shift(ends, sign, 0.0, sublane), shift(through, sign, 1.0, sublane)


def local_kernel(
    blocks, starts_ref, star_ref, times_ref, series_ref, cot_ref, w_ref, table_ref, lograte_ref, gain_ref,
    base_ref, xt_ref, table_sums_ref, reach_ref,
):
    me = slab_index()
    elapsed = elapsed_row(starts_ref, times_ref, me)
    row = lax.broadcasted_iota(jnp.int32, (SLAB, SLAB), 0)
    lane = lax.broadcasted_iota(jnp.int32, (SLAB, SLAB), 1)
    sublane = lax.broadcasted_iota(jnp.int32, (CHUNKS, LANES), 0)
    time_of_row = (row % CHUNKS) * STEPS + row // CHUNKS
    order = (lane == time_of_row).astype(F32).astype(BF16)
    gap = jnp.sum(jnp.where(lane == time_of_row, jnp.broadcast_to(elapsed, (SLAB, SLAB)), 0.0), axis=1, keepdims=True)
    gap = jnp.broadcast_to(gap, (SLAB, LANES))
    spread = jnp.broadcast_to(elapsed, (SLAB, SLAB))
    for k, mask in enumerate((lane <= time_of_row, lane > time_of_row)):
        reach = jnp.sum(jnp.where(mask, spread, 0.0), axis=1, keepdims=True)
        reach_ref[k] = jnp.broadcast_to(reach, (SLAB, LANES))
    bias = table_ref[pl.ds(star_ref[0], 1), :]
    for h in range(blocks):
        cols = slice(h * LANES, (h + 1) * LANES)
        rate = jnp.exp(lograte_ref[h : h + 1, :])
        gain = gain_ref[h : h + 1, :]
        x = jnp.dot(order, series_ref[0, :, cols], preferred_element_type=F32)
        xt_ref[cols, :] = x.T.astype(BF16)
        grad = jnp.dot(order, cot_ref[0, :, cols], preferred_element_type=F32)
        proj = jnp.dot(x.astype(BF16), w_ref[cols, :], preferred_element_type=F32) + bias[:, cols]
        drive = gain * proj
        decay = jnp.exp(-rate * gap)
        tiles = lambda v: [v[j * CHUNKS : (j + 1) * CHUNKS, :] for j in range(STEPS)]
        a, d, g, pr, dt = tiles(decay), tiles(drive), tiles(grad), tiles(proj), tiles(gap)
        zero = jnp.zeros((CHUNKS, LANES), F32)
        before_d, before_g, through = [zero], [zero], [a[0]]
        state_d, state_g = d[0], g[0]
        for j in range(1, STEPS):
            before_d.append(a[j] * state_d)
            before_g.append(a[j] * state_g)
            state_d = before_d[j] + d[j]
            state_g = before_g[j] + g[j]
            through.append(a[j] * through[j - 1])
        after_d, after_g, back = [None] * STEPS, [None] * STEPS, [None] * STEPS
        after_d[-1], after_g[-1], back[-1] = d[-1], g[-1], jnp.ones((CHUNKS, LANES), F32)
        for j in reversed(range(STEPS - 1)):
            after_d[j] = a[j + 1] * after_d[j + 1] + d[j]
            after_g[j] = a[j + 1] * after_g[j + 1] + g[j]
            back[j] = a[j + 1] * back[j + 1]
        enter_d, onto = chunk_entries(state_d, through[-1], sublane, 1)
        enter_g, _ = chunk_entries(state_g, through[-1], sublane, 1)
        leave_d, off = chunk_entries(a[0] * after_d[0], through[-1], sublane, -1)
        leave_g, _ = chunk_entries(a[0] * after_g[0], through[-1], sublane, -1)
        sums = [zero] * 12
        for j in range(STEPS):
            kept_d = before_d[j] + through[j] * enter_d
            kept_g = before_g[j] + through[j] * enter_g
            later_d = after_d[j] + back[j] * leave_d
            later_g = after_g[j] + back[j] * leave_g
            on, off_j = through[j] * onto, back[j] * off
            base = later_g + kept_g + g[j]
            rows = slice(h * LANES + j * CHUNKS, h * LANES + (j + 1) * CHUNKS)
            base_ref[rows, :] = gain * base
            dt_on, dt_off = dt[j] * on, dt[j] * off_j
            terms = (
                dt[j] * (later_g * kept_d + kept_g * later_d),
                dt_off * kept_d,
                dt_on * later_g,
                dt_on * off_j,
                dt_off * kept_g,
                dt_on * later_d,
                base,
                on,
                off_j,
                base * pr[j],
                on * pr[j],
                off_j * pr[j],
            )
            sums = [s + t for s, t in zip(sums, terms)]
        for k, v in enumerate(sums):
            table_sums_ref[k, h : h + 1, :] = jnp.sum(v, axis=0, keepdims=True)


def combine_kernel(
    blocks, slabs, rows_dp, lograte_ref, gain_ref, got_ref, sums_ref, base_ref, xt_ref, reach_ref,
    low_ref, keep_ref, send_ref, part_ref,
):
    half = blocks * LANES // 2
    me = slab_index()
    mine = lax.axis_index("core")
    slope = -jnp.exp(lograte_ref[...])
    slope2 = jnp.concatenate([slope, slope], axis=0)
    took = lambda s: got_ref[s % 2, s // 2, 2 * blocks : 2 * blocks + 1, :]
    between = [None] * slabs
    run = jnp.zeros((1, LANES), F32)
    for s in reversed(range(slabs)):
        between[s] = run
        run = jnp.where(s < me, run + took(s), 0.0)
    run = jnp.zeros((1, LANES), F32)
    carry_early = jnp.zeros((2 * blocks, LANES), F32)
    carry_late = jnp.zeros((2 * blocks, LANES), F32)
    for s in range(slabs):
        x = jnp.exp(slope2 * jnp.where(s < me, between[s], run)) * got_ref[s % 2, s // 2, 0 : 2 * blocks, :]
        carry_early = carry_early + jnp.where(s < me, x, 0.0)
        carry_late = carry_late + jnp.where(s > me, x, 0.0)
        run = jnp.where(s > me, run + took(s), 0.0)
    gain = gain_ref[...]
    early_d, early_g = gain * carry_early[0:blocks], carry_early[blocks:]
    late_d, late_g = gain * carry_late[0:blocks], carry_late[blocks:]
    c = [sums_ref[k, 0:blocks, :] for k in range(12)]
    rate_sum = c[0] + late_g * c[1] + early_d * c[2] + (late_g * early_d + early_g * late_d) * c[3]
    rate_sum = rate_sum + late_d * c[4] + early_g * c[5]
    grad_sum = c[6] + early_g * c[7] + late_g * c[8]
    cross_sum = c[9] + early_g * c[10] + late_g * c[11]
    proj_sum = gain * grad_sum
    log_sum = jnp.exp(2.0 * slope) / gain * cross_sum - rate_sum
    log_sum = -slope * log_sum
    for core in range(2):
        part_ref[core, half : half + blocks, :] = proj_sum
        part_ref[core, half + 16 : half + 16 + blocks, :] = log_sum

    enter, leave = gain * early_g, gain * late_g
    from_start, to_end = reach_ref[0], reach_ref[1]
    for h in range(blocks):
        rows = slice(h * LANES, (h + 1) * LANES)
        row = slice(h, h + 1)
        low = base_ref[rows, :] + jnp.exp(slope[row] * from_start) * enter[row] + jnp.exp(slope[row] * to_end) * leave[row]
        low = low.astype(BF16)
        low_ref[rows, :] = low
        product = jnp.dot(xt_ref[rows, :], low, preferred_element_type=F32)
        for k in range(LANES // 8):
            piece, third = divmod(h * (LANES // 8) + k, 3)
            dp, quarter = divmod(piece, 4)
            core, yl = divmod(quarter, 2)
            at = (dp * 2 + yl) * 24 + third * 8
            part_ref[core, at : at + 8, :] = product[k * 8 : k * 8 + 8, :]
    keep_ref[...] = part_ref[mine]
    send_ref[...] = part_ref[1 - mine]


def pair_kernel(rows_dp, star_ref, keep_ref, sent_ref, out_ref, flat_ref):
    other = 1 - lax.axis_index("core")
    half = keep_ref.shape[0] - 32
    width = 2 * half
    share = width // rows_dp
    flat_ref[0:2, width:] = jnp.zeros((2, flat_ref.shape[1] - width), F32)
    for k in range(2):
        table = keep_ref[half + 16 * k : half + 16 * k + 16, :] + sent_ref[other, half + 16 * k : half + 16 * k + 16, :]
        for h in range(width // LANES):
            flat_ref[k : k + 1, h * LANES : (h + 1) * LANES] = table[h : h + 1, :]
    lane = lax.broadcasted_iota(jnp.int32, (2, LANES), 1)
    star = jnp.broadcast_to(star_ref[0].astype(F32), (2, LANES))
    for dp in range(rows_dp):
        tile = jnp.where(lane < share, flat_ref[0:2, dp * share : dp * share + LANES], star)
        for yl in range(2):
            piece = dp * 2 + yl
            rows = slice(piece * 24, piece * 24 + 24)
            at = piece * PIECE
            out_ref[at : at + 24, :] = keep_ref[rows, :] + sent_ref[other, rows, :]
            out_ref[at + 24 : at + 26, :] = tile


def series_kernel(blocks, low_ref, cot_ref, w_ref, dx_ref):
    row = lax.broadcasted_iota(jnp.int32, (SLAB, SLAB), 0)
    lane = lax.broadcasted_iota(jnp.int32, (SLAB, SLAB), 1)
    unorder = (row == (lane % CHUNKS) * STEPS + lane // CHUNKS).astype(F32).astype(BF16)
    for h in range(blocks):
        cols = slice(h * LANES, (h + 1) * LANES)
        low = jnp.dot(unorder, low_ref[cols, :], preferred_element_type=F32).astype(BF16)
        back = lax.dot_general(low, w_ref[cols, :], (((1,), (1,)), ((), ())), preferred_element_type=F32)
        dx_ref[0, :, cols] = (cot_ref[0, :, cols].astype(F32) + back).astype(BF16)


def piece_kernel(norm, share, got_ref, out_ref):
    first = (lax.axis_index("core") * 2 + lax.axis_index("yl")) * 4
    sources = got_ref.shape[0] // PIECE
    total = got_ref[0:24, :]
    for s in range(1, sources):
        total = total + got_ref[s * PIECE : s * PIECE + 24, :]
    terms = got_ref[pl.ds(24, sources, stride=PIECE), :]
    logs = jnp.sum(got_ref[pl.ds(25, sources, stride=PIECE), :], axis=0, keepdims=True)
    star = jnp.broadcast_to(terms[:, share : share + 1], terms.shape)
    hits = [star == (first + k).astype(F32) for k in range(4)]
    stars = [jnp.sum(jnp.where(hit, terms, 0.0), axis=0, keepdims=True) for hit in hits]
    total = total * norm
    tail = jnp.concatenate(stars + [logs] + [jnp.zeros((3, LANES), F32)], axis=0) * norm
    for d in range(out_ref.shape[0]):
        out_ref[d, 0:24, :] = total
        out_ref[d, 24:32, :] = tail


def final_kernel(got_ref, weight_ref, star_ref, log_ref):
    share = star_ref.shape[1]
    for core in range(2):
        for yl in range(2):
            q = core * 2 + yl
            total = None
            for source in range(got_ref.shape[1]):
                if source // 2 % 2 == yl:
                    total = got_ref[core, source] if total is None else total + got_ref[core, source]
            weight_ref[q * 24 : q * 24 + 24, :] = total[0:24, :]
            star_ref[q * 4 : q * 4 + 4, :] = total[24:28, 0:share]
            if q == 0:
                log_ref[...] = total[28:29, 0:share]


def body(series, cotangent, step_times, seg_starts, star_of_row, block_weight, star_table, log_rate):
    _, slab_len, width = series.shape
    blocks = width // LANES
    slabs = lax.axis_size(("yh", "yl", "zh", "core"))
    rows_dp = lax.axis_size(("x", "zl"))
    norm = float(1.0 / (rows_dp * slabs * slab_len) ** 0.5)
    chips = slabs // 2
    log_blocks = log_rate.reshape(blocks, LANES)
    gain = jnp.sqrt(-jnp.expm1(-2.0 * jnp.exp(log_blocks)))
    smem = pl.BlockSpec(memory_space=pltpu.SMEM)
    vmem = pl.BlockSpec(memory_space=pltpu.VMEM)
    hbm = pl.BlockSpec(memory_space=pl.ANY)
    params = pltpu.CompilerParams(vmem_limit_bytes=24 * 1024 * 1024)
    big = pltpu.CompilerParams(vmem_limit_bytes=60 * 1024 * 1024)
    shape = jax.ShapeDtypeStruct
    common = (seg_starts, star_of_row, step_times, series, cotangent, block_weight, star_table, log_blocks)
    ends = pl.pallas_call(
        functools.partial(ends_kernel, blocks, chips),
        out_shape=shape((chips, 32, LANES), F32),
        in_specs=[hbm] * 8,
        out_specs=vmem,
        scratch_shapes=[pltpu.VMEM((2, 32, LANES), F32)]
        + [pltpu.SMEM(v.shape, v.dtype) for v in common[:2]]
        + [pltpu.VMEM(v.shape, v.dtype) for v in common[2:]]
        + [pltpu.SemaphoreType.DMA((5,)), pltpu.SemaphoreType.DMA((GROUPS, 3))],
        compiler_params=big,
        name="slab_ends",
    )(*common)
    got = lax.all_gather(lax.all_to_all(ends, ("yh", "yl", "zh"), 0, 0), "core")
    base, xt, sums, reach = pl.pallas_call(
        functools.partial(local_kernel, blocks),
        out_shape=[
            shape((width, slab_len), F32),
            shape((width, slab_len), BF16),
            shape((12, 16, LANES), F32),
            shape((2, slab_len, LANES), F32),
        ],
        in_specs=[smem, smem] + [vmem] * 7,
        out_specs=[vmem] * 4,
        compiler_params=params,
        cost_estimate=pl.CostEstimate(flops=20_000_000, bytes_accessed=4_000_000, transcendentals=200_000),
        name="local_scans",
    )(*common, gain)
    half_rows = width // 2 + 32
    low, keep, send = pl.pallas_call(
        functools.partial(combine_kernel, blocks, slabs, rows_dp),
        out_shape=[shape((width, slab_len), BF16)] + [shape((half_rows, LANES), F32)] * 2,
        in_specs=[vmem] * 7,
        out_specs=[vmem] * 3,
        scratch_shapes=[pltpu.VMEM((2, half_rows, LANES), F32)],
        compiler_params=params,
        name="gradients",
    )(log_blocks, gain, got, sums, base, xt, reach)
    sent = lax.all_gather(send, "core")
    pair = pl.pallas_call(
        functools.partial(pair_kernel, rows_dp),
        out_shape=shape((rows_dp * 2 * PIECE, LANES), F32),
        in_specs=[smem, vmem, vmem],
        out_specs=vmem,
        scratch_shapes=[pltpu.VMEM((8, width + LANES), F32)],
        compiler_params=params,
        name="pair_sum",
    )(star_of_row, keep, sent)
    grad_series = pl.pallas_call(
        functools.partial(series_kernel, blocks),
        out_shape=shape(series.shape, BF16),
        in_specs=[vmem] * 3,
        out_specs=vmem,
        compiler_params=params,
        cost_estimate=pl.CostEstimate(flops=100_000_000, bytes_accessed=1_600_000, transcendentals=0),
        name="series_gradient",
    )(low, cotangent, block_weight)
    pair = pair.reshape(rows_dp * 2, 1, PIECE * LANES)
    pieces = lax.all_to_all(pair, ("x", "zl", "yl"), 0, 0).reshape(rows_dp * 2 * PIECE, LANES)
    piece = pl.pallas_call(
        functools.partial(piece_kernel, norm, width // rows_dp),
        out_shape=jax.ShapeDtypeStruct((slabs // 2, 32, LANES), F32),
        in_specs=[vmem],
        out_specs=vmem,
        compiler_params=params,
        name="sum_pieces",
    )(pieces)
    spread = lax.all_to_all(piece, ("yh", "yl", "zh"), 0, 0)
    both = lax.all_gather(spread, "core")
    share = width // rows_dp
    grad_weight, grad_star, grad_log = pl.pallas_call(
        final_kernel,
        out_shape=[
            jax.ShapeDtypeStruct((share, LANES), F32),
            jax.ShapeDtypeStruct((star_table.shape[0], share), F32),
            jax.ShapeDtypeStruct((1, share), F32),
        ],
        in_specs=[vmem],
        out_specs=[vmem] * 3,
        compiler_params=params,
        name="outputs",
    )(both)
    return grad_series, grad_weight, grad_star, grad_log.reshape(share)


def solution(mesh):
    fine = Mesh(mesh.devices.reshape(4, 4, 4, 2, 2, 2), ("x", "zl", "yh", "yl", "zh", "core"))
    dp, ctx = ("x", "zl"), ("yh", "yl", "zh", "core")
    in_specs = (P(dp, ctx, None), P(dp, ctx, None), P(dp, ctx), P(dp, None), P(dp), P(), P(), P())
    out_specs = (P(dp, ctx, None), P(dp, None), P(None, dp), P(dp))
    return jax.shard_map(body, mesh=fine, in_specs=in_specs, out_specs=out_specs, check_vma=False)
```

```python
import functools
import jax
import jax.numpy as jnp
from jax import lax
from jax.experimental import pallas as pl
from jax.experimental.pallas import tpu as pltpu
from jax.sharding import Mesh, PartitionSpec as P

SLAB = 128
LANES = 128
CHUNKS = 8
STEPS = SLAB // CHUNKS
FAR = 1e9
CARRY = 25
SHARE = 29
PIECE = 26
F32 = jnp.float32
BF16 = jnp.bfloat16


def slab_index():
    chip = (lax.axis_index("yh") * 2 + lax.axis_index("yl")) * 2 + lax.axis_index("zh")
    return chip * 2 + lax.axis_index("core")


def elapsed_row(starts_ref, times_ref, me):
    position = lax.broadcasted_iota(jnp.int32, (1, SLAB), 1) + me * SLAB
    reset = position == starts_ref[0, 0]
    for k in range(1, starts_ref.shape[1]):
        reset = jnp.logical_or(reset, position == starts_ref[0, k])
    return jnp.where(reset, FAR, times_ref[...])


def ends_kernel(
    blocks, chips, starts_hbm, star_hbm, times_hbm, series_hbm, cot_hbm, w_hbm, table_hbm, lograte_hbm,
    out_ref, ends_ref, starts_ref, star_ref, times_ref, series_ref, cot_ref, w_ref, table_ref, lograte_ref, sems, load_sems,
):
    sources = (starts_hbm, star_hbm, times_hbm, table_hbm, lograte_hbm)
    targets = (starts_ref, star_ref, times_ref, table_ref, lograte_ref)
    copies = [pltpu.make_async_copy(a, b, sems.at[k]) for k, (a, b) in enumerate(zip(sources, targets))]
    sources, targets = (series_hbm, w_hbm, cot_hbm), (series_ref, w_ref, cot_ref)
    loads = [pltpu.make_async_copy(a, b, load_sems.at[k]) for k, (a, b) in enumerate(zip(sources, targets))]
    for copy in copies[:3] + loads + copies[3:]:
        copy.start()
    core = lax.axis_index("core")
    me = slab_index()
    for copy in copies[:3]:
        copy.wait()
    elapsed = elapsed_row(starts_ref, times_ref, me)
    row = lax.broadcasted_iota(jnp.int32, (SLAB, SLAB), 0)
    lane = lax.broadcasted_iota(jnp.int32, (SLAB, SLAB), 1)
    spread = jnp.broadcast_to(elapsed, (SLAB, SLAB))
    to_end = jnp.sum(jnp.where(lane > row, spread, 0.0), axis=1, keepdims=True)
    from_start = jnp.sum(jnp.where(lane <= row, spread, 0.0), axis=1, keepdims=True)
    to_end = jnp.broadcast_to(to_end, (SLAB, LANES))
    from_start = jnp.broadcast_to(from_start, (SLAB, LANES))
    total = jnp.sum(elapsed, axis=1, keepdims=True)
    for copy in copies[3:] + loads:
        copy.wait()
    bias = table_ref[pl.ds(star_ref[0], 1), :]
    for h in range(blocks):
        cols = slice(h * LANES, (h + 1) * LANES)
        proj = jnp.dot(series_ref[0, :, cols], w_ref[cols, :], preferred_element_type=F32) + bias[:, cols]
        grad = cot_ref[0, :, cols].astype(F32)
        slope = -jnp.exp(lograte_ref[h : h + 1, :])
        late = jnp.exp(slope * to_end)
        early = jnp.exp(slope * from_start)
        ends_ref[0, h : h + 1, :] = jnp.sum(late * proj, axis=0, keepdims=True)
        ends_ref[0, blocks + h : blocks + h + 1, :] = jnp.sum(late * grad, axis=0, keepdims=True)
        ends_ref[1, h : h + 1, :] = jnp.sum(early * proj, axis=0, keepdims=True)
        ends_ref[1, blocks + h : blocks + h + 1, :] = jnp.sum(early * grad, axis=0, keepdims=True)
    tail = jnp.broadcast_to(total, (8, LANES))
    ends_ref[0, 2 * blocks : 2 * blocks + 8, :] = tail
    ends_ref[1, 2 * blocks : 2 * blocks + 8, :] = tail
    for chip in range(chips):
        out_ref[chip * CARRY : (chip + 1) * CARRY, :] = ends_ref[jnp.where(2 * chip + 1 - core > me, 0, 1), 0:CARRY, :]


def shift(x, k, fill, sublane):
    if k > 0:
        return jnp.where(sublane < k, fill, pltpu.roll(x, k, 0))
    return jnp.where(sublane >= CHUNKS + k, fill, pltpu.roll(x, CHUNKS + k, 0))


def chunk_entries(ends, through, sublane, sign):
    for k in (1, 2, 4):
        ends = ends + through * shift(ends, sign * k, 0.0, sublane)
        through = through * shift(through, sign * k, 1.0, sublane)
    return shift(ends, sign, 0.0, sublane), shift(through, sign, 1.0, sublane)


def local_kernel(
    blocks, starts_ref, star_ref, times_ref, series_ref, cot_ref, w_ref, table_ref, lograte_ref, gain_ref,
    base_ref, xt_ref, table_sums_ref, reach_ref,
):
    me = slab_index()
    elapsed = elapsed_row(starts_ref, times_ref, me)
    row = lax.broadcasted_iota(jnp.int32, (SLAB, SLAB), 0)
    lane = lax.broadcasted_iota(jnp.int32, (SLAB, SLAB), 1)
    sublane = lax.broadcasted_iota(jnp.int32, (CHUNKS, LANES), 0)
    time_of_row = (row % CHUNKS) * STEPS + row // CHUNKS
    order = (lane == time_of_row).astype(F32).astype(BF16)
    gap = jnp.sum(jnp.where(lane == time_of_row, jnp.broadcast_to(elapsed, (SLAB, SLAB)), 0.0), axis=1, keepdims=True)
    gap = jnp.broadcast_to(gap, (SLAB, LANES))
    spread = jnp.broadcast_to(elapsed, (SLAB, SLAB))
    for k, mask in enumerate((lane <= time_of_row, lane > time_of_row)):
        reach = jnp.sum(jnp.where(mask, spread, 0.0), axis=1, keepdims=True)
        reach_ref[k] = jnp.broadcast_to(reach, (SLAB, LANES))
    bias = table_ref[pl.ds(star_ref[0], 1), :]
    for h in range(blocks):
        cols = slice(h * LANES, (h + 1) * LANES)
        rate = jnp.exp(lograte_ref[h : h + 1, :])
        gain = gain_ref[h : h + 1, :]
        x = jnp.dot(order, series_ref[0, :, cols], preferred_element_type=F32)
        xt_ref[cols, :] = x.T.astype(BF16)
        grad = jnp.dot(order, cot_ref[0, :, cols], preferred_element_type=F32)
        proj = jnp.dot(x.astype(BF16), w_ref[cols, :], preferred_element_type=F32) + bias[:, cols]
        drive = gain * proj
        decay = jnp.exp(-rate * gap)
        tiles = lambda v: [v[j * CHUNKS : (j + 1) * CHUNKS, :] for j in range(STEPS)]
        a, d, g, pr, dt = tiles(decay), tiles(drive), tiles(grad), tiles(proj), tiles(gap)
        zero = jnp.zeros((CHUNKS, LANES), F32)
        before_d, before_g, through = [zero], [zero], [a[0]]
        state_d, state_g = d[0], g[0]
        for j in range(1, STEPS):
            before_d.append(a[j] * state_d)
            before_g.append(a[j] * state_g)
            state_d = before_d[j] + d[j]
            state_g = before_g[j] + g[j]
            through.append(a[j] * through[j - 1])
        after_d, after_g, back = [None] * STEPS, [None] * STEPS, [None] * STEPS
        after_d[-1], after_g[-1], back[-1] = d[-1], g[-1], jnp.ones((CHUNKS, LANES), F32)
        for j in reversed(range(STEPS - 1)):
            after_d[j] = a[j + 1] * after_d[j + 1] + d[j]
            after_g[j] = a[j + 1] * after_g[j + 1] + g[j]
            back[j] = a[j + 1] * back[j + 1]
        enter_d, onto = chunk_entries(state_d, through[-1], sublane, 1)
        enter_g, _ = chunk_entries(state_g, through[-1], sublane, 1)
        leave_d, off = chunk_entries(a[0] * after_d[0], through[-1], sublane, -1)
        leave_g, _ = chunk_entries(a[0] * after_g[0], through[-1], sublane, -1)
        sums = [zero] * 12
        for j in range(STEPS):
            kept_d = before_d[j] + through[j] * enter_d
            kept_g = before_g[j] + through[j] * enter_g
            later_d = after_d[j] + back[j] * leave_d
            later_g = after_g[j] + back[j] * leave_g
            on, off_j = through[j] * onto, back[j] * off
            base = later_g + kept_g + g[j]
            rows = slice(h * LANES + j * CHUNKS, h * LANES + (j + 1) * CHUNKS)
            base_ref[rows, :] = gain * base
            dt_on, dt_off = dt[j] * on, dt[j] * off_j
            terms = (
                dt[j] * (later_g * kept_d + kept_g * later_d),
                dt_off * kept_d,
                dt_on * later_g,
                dt_on * off_j,
                dt_off * kept_g,
                dt_on * later_d,
                base,
                on,
                off_j,
                base * pr[j],
                on * pr[j],
                off_j * pr[j],
            )
            sums = [s + t for s, t in zip(sums, terms)]
        for k, v in enumerate(sums):
            table_sums_ref[k, h : h + 1, :] = jnp.sum(v, axis=0, keepdims=True)


def combine_kernel(
    blocks, slabs, rows_dp, lograte_ref, gain_ref, got_ref, sums_ref, base_ref, xt_ref, reach_ref,
    low_ref, keep_ref, send_ref, part_ref,
):
    half = blocks * LANES // 2
    me = slab_index()
    mine = lax.axis_index("core")
    slope = -jnp.exp(lograte_ref[...])
    slope2 = jnp.concatenate([slope, slope], axis=0)
    start = lambda s: (s % 2 * (slabs // 2) + s // 2) * CARRY
    took = lambda s: got_ref[start(s) + 2 * blocks : start(s) + 2 * blocks + 1, :]
    between = [None] * slabs
    run = jnp.zeros((1, LANES), F32)
    for s in reversed(range(slabs)):
        between[s] = run
        run = jnp.where(s < me, run + took(s), 0.0)
    run = jnp.zeros((1, LANES), F32)
    carry_early = jnp.zeros((2 * blocks, LANES), F32)
    carry_late = jnp.zeros((2 * blocks, LANES), F32)
    for s in range(slabs):
        x = jnp.exp(slope2 * jnp.where(s < me, between[s], run)) * got_ref[start(s) : start(s) + 2 * blocks, :]
        carry_early = carry_early + jnp.where(s < me, x, 0.0)
        carry_late = carry_late + jnp.where(s > me, x, 0.0)
        run = jnp.where(s > me, run + took(s), 0.0)
    gain = gain_ref[...]
    early_d, early_g = gain * carry_early[0:blocks], carry_early[blocks:]
    late_d, late_g = gain * carry_late[0:blocks], carry_late[blocks:]
    c = [sums_ref[k, 0:blocks, :] for k in range(12)]
    rate_sum = c[0] + late_g * c[1] + early_d * c[2] + (late_g * early_d + early_g * late_d) * c[3]
    rate_sum = rate_sum + late_d * c[4] + early_g * c[5]
    grad_sum = c[6] + early_g * c[7] + late_g * c[8]
    cross_sum = c[9] + early_g * c[10] + late_g * c[11]
    proj_sum = gain * grad_sum
    log_sum = jnp.exp(2.0 * slope) / gain * cross_sum - rate_sum
    log_sum = -slope * log_sum
    for core in range(2):
        part_ref[core, half : half + blocks, :] = proj_sum
        part_ref[core, half + 16 : half + 16 + blocks, :] = log_sum

    enter, leave = gain * early_g, gain * late_g
    from_start, to_end = reach_ref[0], reach_ref[1]
    for h in range(blocks):
        rows = slice(h * LANES, (h + 1) * LANES)
        row = slice(h, h + 1)
        low = base_ref[rows, :] + jnp.exp(slope[row] * from_start) * enter[row] + jnp.exp(slope[row] * to_end) * leave[row]
        low = low.astype(BF16)
        low_ref[rows, :] = low
        product = jnp.dot(xt_ref[rows, :], low, preferred_element_type=F32)
        for k in range(LANES // 8):
            piece, third = divmod(h * (LANES // 8) + k, 3)
            dp, quarter = divmod(piece, 4)
            core, yl = divmod(quarter, 2)
            at = (dp * 2 + yl) * 24 + third * 8
            part_ref[core, at : at + 8, :] = product[k * 8 : k * 8 + 8, :]
    keep_ref[...] = part_ref[mine]
    send_ref[...] = part_ref[1 - mine]


def pair_kernel(rows_dp, star_ref, keep_ref, sent_ref, out_ref, flat_ref):
    other = 1 - lax.axis_index("core")
    half = keep_ref.shape[0] - 32
    width = 2 * half
    share = width // rows_dp
    flat_ref[0:2, width:] = jnp.zeros((2, flat_ref.shape[1] - width), F32)
    for k in range(2):
        table = keep_ref[half + 16 * k : half + 16 * k + 16, :] + sent_ref[other, half + 16 * k : half + 16 * k + 16, :]
        for h in range(width // LANES):
            flat_ref[k : k + 1, h * LANES : (h + 1) * LANES] = table[h : h + 1, :]
    lane = lax.broadcasted_iota(jnp.int32, (2, LANES), 1)
    star = jnp.broadcast_to(star_ref[0].astype(F32), (2, LANES))
    for dp in range(rows_dp):
        tile = jnp.where(lane < share, flat_ref[0:2, dp * share : dp * share + LANES], star)
        for yl in range(2):
            piece = dp * 2 + yl
            rows = slice(piece * 24, piece * 24 + 24)
            at = piece * PIECE
            out_ref[at : at + 24, :] = keep_ref[rows, :] + sent_ref[other, rows, :]
            out_ref[at + 24 : at + 26, :] = tile


def series_kernel(blocks, low_ref, cot_ref, w_ref, dx_ref):
    row = lax.broadcasted_iota(jnp.int32, (SLAB, SLAB), 0)
    lane = lax.broadcasted_iota(jnp.int32, (SLAB, SLAB), 1)
    unorder = (row == (lane % CHUNKS) * STEPS + lane // CHUNKS).astype(F32).astype(BF16)
    for h in range(blocks):
        cols = slice(h * LANES, (h + 1) * LANES)
        low = jnp.dot(unorder, low_ref[cols, :], preferred_element_type=F32).astype(BF16)
        back = lax.dot_general(low, w_ref[cols, :], (((1,), (1,)), ((), ())), preferred_element_type=F32)
        dx_ref[0, :, cols] = (cot_ref[0, :, cols].astype(F32) + back).astype(BF16)


def piece_kernel(norm, share, got_ref, out_ref):
    first = (lax.axis_index("core") * 2 + lax.axis_index("yl")) * 4
    sources = got_ref.shape[0] // PIECE
    total = got_ref[0:24, :]
    for s in range(1, sources):
        total = total + got_ref[s * PIECE : s * PIECE + 24, :]
    terms = got_ref[pl.ds(24, sources, stride=PIECE), :]
    logs = jnp.sum(got_ref[pl.ds(25, sources, stride=PIECE), :], axis=0, keepdims=True)
    star = jnp.broadcast_to(terms[:, share : share + 1], terms.shape)
    hits = [star == (first + k).astype(F32) for k in range(4)]
    stars = [jnp.sum(jnp.where(hit, terms, 0.0), axis=0, keepdims=True) for hit in hits]
    total = total * norm
    tail = jnp.concatenate(stars + [logs], axis=0) * norm
    for d in range(out_ref.shape[0] // SHARE):
        out_ref[d * SHARE : d * SHARE + 24, :] = total
        out_ref[d * SHARE + 24 : d * SHARE + 29, :] = tail


def final_kernel(got_ref, weight_ref, star_ref, log_ref):
    share = star_ref.shape[1]
    chips = got_ref.shape[0] // SHARE // 2
    for core in range(2):
        for yl in range(2):
            q = core * 2 + yl
            parts = [(core * chips + chip) * SHARE for chip in range(chips) if chip // 2 % 2 == yl]
            total = got_ref[parts[0] : parts[0] + SHARE, :]
            for at in parts[1:]:
                total = total + got_ref[at : at + SHARE, :]
            weight_ref[q * 24 : q * 24 + 24, :] = total[0:24, :]
            star_ref[q * 4 : q * 4 + 4, :] = total[24:28, 0:share]
            if q == 0:
                log_ref[...] = total[28:29, 0:share]


def body(series, cotangent, step_times, seg_starts, star_of_row, block_weight, star_table, log_rate):
    _, slab_len, width = series.shape
    blocks = width // LANES
    slabs = lax.axis_size(("yh", "yl", "zh", "core"))
    rows_dp = lax.axis_size(("x", "zl"))
    norm = float(1.0 / (rows_dp * slabs * slab_len) ** 0.5)
    chips = slabs // 2
    log_blocks = log_rate.reshape(blocks, LANES)
    gain = jnp.sqrt(-jnp.expm1(-2.0 * jnp.exp(log_blocks)))
    smem = pl.BlockSpec(memory_space=pltpu.SMEM)
    vmem = pl.BlockSpec(memory_space=pltpu.VMEM)
    hbm = pl.BlockSpec(memory_space=pl.ANY)
    params = pltpu.CompilerParams(vmem_limit_bytes=24 * 1024 * 1024)
    big = pltpu.CompilerParams(vmem_limit_bytes=60 * 1024 * 1024)
    shape = jax.ShapeDtypeStruct
    common = (seg_starts, star_of_row, step_times, series, cotangent, block_weight, star_table, log_blocks)
    ends = pl.pallas_call(
        functools.partial(ends_kernel, blocks, chips),
        out_shape=shape((chips * CARRY, LANES), F32),
        in_specs=[hbm] * 8,
        out_specs=vmem,
        scratch_shapes=[pltpu.VMEM((2, 32, LANES), F32)]
        + [pltpu.SMEM(v.shape, v.dtype) for v in common[:2]]
        + [pltpu.VMEM(v.shape, v.dtype) for v in common[2:]]
        + [pltpu.SemaphoreType.DMA((5,)), pltpu.SemaphoreType.DMA((3,))],
        compiler_params=big,
        name="slab_ends",
    )(*common)
    ends = ends.reshape(chips, 1, CARRY * LANES)
    got = lax.all_gather(lax.all_to_all(ends, ("yh", "yl", "zh"), 0, 0), "core").reshape(slabs * CARRY, LANES)
    base, xt, sums, reach = pl.pallas_call(
        functools.partial(local_kernel, blocks),
        out_shape=[
            shape((width, slab_len), F32),
            shape((width, slab_len), BF16),
            shape((12, 16, LANES), F32),
            shape((2, slab_len, LANES), F32),
        ],
        in_specs=[smem, smem] + [vmem] * 7,
        out_specs=[vmem] * 4,
        compiler_params=params,
        cost_estimate=pl.CostEstimate(flops=20_000_000, bytes_accessed=4_000_000, transcendentals=200_000),
        name="local_scans",
    )(*common, gain)
    half_rows = width // 2 + 32
    low, keep, send = pl.pallas_call(
        functools.partial(combine_kernel, blocks, slabs, rows_dp),
        out_shape=[shape((width, slab_len), BF16)] + [shape((half_rows, LANES), F32)] * 2,
        in_specs=[vmem] * 7,
        out_specs=[vmem] * 3,
        scratch_shapes=[pltpu.VMEM((2, half_rows, LANES), F32)],
        compiler_params=params,
        name="gradients",
    )(log_blocks, gain, got, sums, base, xt, reach)
    sent = lax.all_gather(send, "core")
    pair = pl.pallas_call(
        functools.partial(pair_kernel, rows_dp),
        out_shape=shape((rows_dp * 2 * PIECE, LANES), F32),
        in_specs=[smem, vmem, vmem],
        out_specs=vmem,
        scratch_shapes=[pltpu.VMEM((8, width + LANES), F32)],
        compiler_params=params,
        name="pair_sum",
    )(star_of_row, keep, sent)
    grad_series = pl.pallas_call(
        functools.partial(series_kernel, blocks),
        out_shape=shape(series.shape, BF16),
        in_specs=[vmem] * 3,
        out_specs=vmem,
        compiler_params=params,
        cost_estimate=pl.CostEstimate(flops=100_000_000, bytes_accessed=1_600_000, transcendentals=0),
        name="series_gradient",
    )(low, cotangent, block_weight)
    pair = pair.reshape(rows_dp * 2, 1, PIECE * LANES)
    pieces = lax.all_to_all(pair, ("x", "zl", "yl"), 0, 0).reshape(rows_dp * 2 * PIECE, LANES)
    piece = pl.pallas_call(
        functools.partial(piece_kernel, norm, width // rows_dp),
        out_shape=shape((chips * SHARE, LANES), F32),
        in_specs=[vmem],
        out_specs=vmem,
        compiler_params=params,
        name="sum_pieces",
    )(pieces)
    spread = lax.all_to_all(piece.reshape(chips, 1, SHARE * LANES), ("yh", "yl", "zh"), 0, 0)
    both = lax.all_gather(spread, "core").reshape(slabs * SHARE, LANES)
    share = width // rows_dp
    grad_weight, grad_star, grad_log = pl.pallas_call(
        final_kernel,
        out_shape=[
            jax.ShapeDtypeStruct((share, LANES), F32),
            jax.ShapeDtypeStruct((star_table.shape[0], share), F32),
            jax.ShapeDtypeStruct((1, share), F32),
        ],
        in_specs=[vmem],
        out_specs=[vmem] * 3,
        compiler_params=params,
        name="outputs",
    )(both)
    return grad_series, grad_weight, grad_star, grad_log.reshape(share)


def solution(mesh):
    fine = Mesh(mesh.devices.reshape(4, 4, 4, 2, 2, 2), ("x", "zl", "yh", "yl", "zh", "core"))
    dp, ctx = ("x", "zl"), ("yh", "yl", "zh", "core")
    in_specs = (P(dp, ctx, None), P(dp, ctx, None), P(dp, ctx), P(dp, None), P(dp), P(), P(), P())
    out_specs = (P(dp, ctx, None), P(dp, None), P(None, dp), P(dp))
    return jax.shard_map(body, mesh=fine, in_specs=in_specs, out_specs=out_specs, check_vma=False)
```

```python
import functools
import jax
import jax.numpy as jnp
from jax import lax
from jax.experimental import pallas as pl
from jax.experimental.pallas import tpu as pltpu
from jax.sharding import Mesh, PartitionSpec as P

SLAB = 128
LANES = 128
CHUNKS = 8
STEPS = SLAB // CHUNKS
FAR = 1e9
CARRY = 25
SHARE = 29
PIECE = 26
F32 = jnp.float32
BF16 = jnp.bfloat16


def slab_index():
    chip = (lax.axis_index("yh") * 2 + lax.axis_index("yl")) * 2 + lax.axis_index("zh")
    return chip * 2 + lax.axis_index("core")


def chip_slot(chip, chips):
    return chip % 2 * (chips // 2) + chip // 2


def elapsed_row(starts_ref, times_ref, me):
    position = lax.broadcasted_iota(jnp.int32, (1, SLAB), 1) + me * SLAB
    reset = position == starts_ref[0, 0]
    for k in range(1, starts_ref.shape[1]):
        reset = jnp.logical_or(reset, position == starts_ref[0, k])
    return jnp.where(reset, FAR, times_ref[...])


def ends_kernel(
    blocks, chips, starts_hbm, star_hbm, times_hbm, series_hbm, cot_hbm, w_hbm, table_hbm, lograte_hbm,
    out_ref, ends_ref, starts_ref, star_ref, times_ref, series_ref, cot_ref, w_ref, table_ref, lograte_ref, sems, load_sems,
):
    sources = (starts_hbm, star_hbm, times_hbm, table_hbm, lograte_hbm)
    targets = (starts_ref, star_ref, times_ref, table_ref, lograte_ref)
    copies = [pltpu.make_async_copy(a, b, sems.at[k]) for k, (a, b) in enumerate(zip(sources, targets))]
    sources, targets = (series_hbm, w_hbm, cot_hbm), (series_ref, w_ref, cot_ref)
    loads = [pltpu.make_async_copy(a, b, load_sems.at[k]) for k, (a, b) in enumerate(zip(sources, targets))]
    for copy in copies[:3] + loads + copies[3:]:
        copy.start()
    core = lax.axis_index("core")
    me = slab_index()
    for copy in copies[:3]:
        copy.wait()
    elapsed = elapsed_row(starts_ref, times_ref, me)
    row = lax.broadcasted_iota(jnp.int32, (SLAB, SLAB), 0)
    lane = lax.broadcasted_iota(jnp.int32, (SLAB, SLAB), 1)
    spread = jnp.broadcast_to(elapsed, (SLAB, SLAB))
    to_end = jnp.sum(jnp.where(lane > row, spread, 0.0), axis=1, keepdims=True)
    from_start = jnp.sum(jnp.where(lane <= row, spread, 0.0), axis=1, keepdims=True)
    to_end = jnp.broadcast_to(to_end, (SLAB, LANES))
    from_start = jnp.broadcast_to(from_start, (SLAB, LANES))
    total = jnp.sum(elapsed, axis=1, keepdims=True)
    for copy in copies[3:] + loads:
        copy.wait()
    bias = table_ref[pl.ds(star_ref[0], 1), :]
    for h in range(blocks):
        cols = slice(h * LANES, (h + 1) * LANES)
        proj = jnp.dot(series_ref[0, :, cols], w_ref[cols, :], preferred_element_type=F32) + bias[:, cols]
        grad = cot_ref[0, :, cols].astype(F32)
        slope = -jnp.exp(lograte_ref[h : h + 1, :])
        late = jnp.exp(slope * to_end)
        early = jnp.exp(slope * from_start)
        ends_ref[0, h : h + 1, :] = jnp.sum(late * proj, axis=0, keepdims=True)
        ends_ref[0, blocks + h : blocks + h + 1, :] = jnp.sum(late * grad, axis=0, keepdims=True)
        ends_ref[1, h : h + 1, :] = jnp.sum(early * proj, axis=0, keepdims=True)
        ends_ref[1, blocks + h : blocks + h + 1, :] = jnp.sum(early * grad, axis=0, keepdims=True)
    tail = jnp.broadcast_to(total, (8, LANES))
    ends_ref[0, 2 * blocks : 2 * blocks + 8, :] = tail
    ends_ref[1, 2 * blocks : 2 * blocks + 8, :] = tail
    for chip in range(chips):
        at = chip_slot(chip, chips) * CARRY
        out_ref[at : at + CARRY, :] = ends_ref[jnp.where(2 * chip + 1 - core > me, 0, 1), 0:CARRY, :]


def shift(x, k, fill, sublane):
    if k > 0:
        return jnp.where(sublane < k, fill, pltpu.roll(x, k, 0))
    return jnp.where(sublane >= CHUNKS + k, fill, pltpu.roll(x, CHUNKS + k, 0))


def chunk_entries(ends, through, sublane, sign):
    for k in (1, 2, 4):
        ends = ends + through * shift(ends, sign * k, 0.0, sublane)
        through = through * shift(through, sign * k, 1.0, sublane)
    return shift(ends, sign, 0.0, sublane), shift(through, sign, 1.0, sublane)


def local_kernel(
    blocks, starts_ref, star_ref, times_ref, series_ref, cot_ref, w_ref, table_ref, lograte_ref, gain_ref,
    base_ref, xt_ref, table_sums_ref, reach_ref,
):
    me = slab_index()
    elapsed = elapsed_row(starts_ref, times_ref, me)
    row = lax.broadcasted_iota(jnp.int32, (SLAB, SLAB), 0)
    lane = lax.broadcasted_iota(jnp.int32, (SLAB, SLAB), 1)
    sublane = lax.broadcasted_iota(jnp.int32, (CHUNKS, LANES), 0)
    time_of_row = (row % CHUNKS) * STEPS + row // CHUNKS
    order = (lane == time_of_row).astype(F32).astype(BF16)
    gap = jnp.sum(jnp.where(lane == time_of_row, jnp.broadcast_to(elapsed, (SLAB, SLAB)), 0.0), axis=1, keepdims=True)
    gap = jnp.broadcast_to(gap, (SLAB, LANES))
    spread = jnp.broadcast_to(elapsed, (SLAB, SLAB))
    for k, mask in enumerate((lane <= time_of_row, lane > time_of_row)):
        reach = jnp.sum(jnp.where(mask, spread, 0.0), axis=1, keepdims=True)
        reach_ref[k] = jnp.broadcast_to(reach, (SLAB, LANES))
    bias = table_ref[pl.ds(star_ref[0], 1), :]
    for h in range(blocks):
        cols = slice(h * LANES, (h + 1) * LANES)
        rate = jnp.exp(lograte_ref[h : h + 1, :])
        gain = gain_ref[h : h + 1, :]
        x = jnp.dot(order, series_ref[0, :, cols], preferred_element_type=F32)
        xt_ref[cols, :] = x.T.astype(BF16)
        grad = jnp.dot(order, cot_ref[0, :, cols], preferred_element_type=F32)
        proj = jnp.dot(x.astype(BF16), w_ref[cols, :], preferred_element_type=F32) + bias[:, cols]
        drive = gain * proj
        decay = jnp.exp(-rate * gap)
        tiles = lambda v: [v[j * CHUNKS : (j + 1) * CHUNKS, :] for j in range(STEPS)]
        a, d, g, pr, dt = tiles(decay), tiles(drive), tiles(grad), tiles(proj), tiles(gap)
        zero = jnp.zeros((CHUNKS, LANES), F32)
        before_d, before_g, through = [zero], [zero], [a[0]]
        state_d, state_g = d[0], g[0]
        for j in range(1, STEPS):
            before_d.append(a[j] * state_d)
            before_g.append(a[j] * state_g)
            state_d = before_d[j] + d[j]
            state_g = before_g[j] + g[j]
            through.append(a[j] * through[j - 1])
        after_d, after_g, back = [None] * STEPS, [None] * STEPS, [None] * STEPS
        after_d[-1], after_g[-1], back[-1] = d[-1], g[-1], jnp.ones((CHUNKS, LANES), F32)
        for j in reversed(range(STEPS - 1)):
            after_d[j] = a[j + 1] * after_d[j + 1] + d[j]
            after_g[j] = a[j + 1] * after_g[j + 1] + g[j]
            back[j] = a[j + 1] * back[j + 1]
        enter_d, onto = chunk_entries(state_d, through[-1], sublane, 1)
        enter_g, _ = chunk_entries(state_g, through[-1], sublane, 1)
        leave_d, off = chunk_entries(a[0] * after_d[0], through[-1], sublane, -1)
        leave_g, _ = chunk_entries(a[0] * after_g[0], through[-1], sublane, -1)
        sums = [zero] * 12
        for j in range(STEPS):
            kept_d = before_d[j] + through[j] * enter_d
            kept_g = before_g[j] + through[j] * enter_g
            later_d = after_d[j] + back[j] * leave_d
            later_g = after_g[j] + back[j] * leave_g
            on, off_j = through[j] * onto, back[j] * off
            base = later_g + kept_g + g[j]
            rows = slice(h * LANES + j * CHUNKS, h * LANES + (j + 1) * CHUNKS)
            base_ref[rows, :] = gain * base
            dt_on, dt_off = dt[j] * on, dt[j] * off_j
            terms = (
                dt[j] * (later_g * kept_d + kept_g * later_d),
                dt_off * kept_d,
                dt_on * later_g,
                dt_on * off_j,
                dt_off * kept_g,
                dt_on * later_d,
                base,
                on,
                off_j,
                base * pr[j],
                on * pr[j],
                off_j * pr[j],
            )
            sums = [s + t for s, t in zip(sums, terms)]
        for k, v in enumerate(sums):
            table_sums_ref[k, h : h + 1, :] = jnp.sum(v, axis=0, keepdims=True)


def combine_kernel(
    blocks, slabs, rows_dp, lograte_ref, gain_ref, got_ref, sums_ref, base_ref, xt_ref, reach_ref,
    low_ref, keep_ref, send_ref, part_ref,
):
    half = blocks * LANES // 2
    me = slab_index()
    mine = lax.axis_index("core")
    slope = -jnp.exp(lograte_ref[...])
    slope2 = jnp.concatenate([slope, slope], axis=0)
    start = lambda s: (s % 2 * (slabs // 2) + chip_slot(s // 2, slabs // 2)) * CARRY
    took = lambda s: got_ref[start(s) + 2 * blocks : start(s) + 2 * blocks + 1, :]
    between = [None] * slabs
    run = jnp.zeros((1, LANES), F32)
    for s in reversed(range(slabs)):
        between[s] = run
        run = jnp.where(s < me, run + took(s), 0.0)
    run = jnp.zeros((1, LANES), F32)
    carry_early = jnp.zeros((2 * blocks, LANES), F32)
    carry_late = jnp.zeros((2 * blocks, LANES), F32)
    for s in range(slabs):
        x = jnp.exp(slope2 * jnp.where(s < me, between[s], run)) * got_ref[start(s) : start(s) + 2 * blocks, :]
        carry_early = carry_early + jnp.where(s < me, x, 0.0)
        carry_late = carry_late + jnp.where(s > me, x, 0.0)
        run = jnp.where(s > me, run + took(s), 0.0)
    gain = gain_ref[...]
    early_d, early_g = gain * carry_early[0:blocks], carry_early[blocks:]
    late_d, late_g = gain * carry_late[0:blocks], carry_late[blocks:]
    c = [sums_ref[k, 0:blocks, :] for k in range(12)]
    rate_sum = c[0] + late_g * c[1] + early_d * c[2] + (late_g * early_d + early_g * late_d) * c[3]
    rate_sum = rate_sum + late_d * c[4] + early_g * c[5]
    grad_sum = c[6] + early_g * c[7] + late_g * c[8]
    cross_sum = c[9] + early_g * c[10] + late_g * c[11]
    proj_sum = gain * grad_sum
    log_sum = jnp.exp(2.0 * slope) / gain * cross_sum - rate_sum
    log_sum = -slope * log_sum
    for core in range(2):
        part_ref[core, half : half + blocks, :] = proj_sum
        part_ref[core, half + 16 : half + 16 + blocks, :] = log_sum

    enter, leave = gain * early_g, gain * late_g
    from_start, to_end = reach_ref[0], reach_ref[1]
    for h in range(blocks):
        rows = slice(h * LANES, (h + 1) * LANES)
        row = slice(h, h + 1)
        low = base_ref[rows, :] + jnp.exp(slope[row] * from_start) * enter[row] + jnp.exp(slope[row] * to_end) * leave[row]
        low = low.astype(BF16)
        low_ref[rows, :] = low
        product = jnp.dot(xt_ref[rows, :], low, preferred_element_type=F32)
        for k in range(LANES // 8):
            piece, third = divmod(h * (LANES // 8) + k, 3)
            dp, quarter = divmod(piece, 4)
            core, yl = divmod(quarter, 2)
            at = (dp * 2 + yl) * 24 + third * 8
            part_ref[core, at : at + 8, :] = product[k * 8 : k * 8 + 8, :]
    keep_ref[...] = part_ref[mine]
    send_ref[...] = part_ref[1 - mine]


def pair_kernel(rows_dp, star_ref, keep_ref, sent_ref, out_ref, flat_ref):
    other = 1 - lax.axis_index("core")
    half = keep_ref.shape[0] - 32
    width = 2 * half
    share = width // rows_dp
    flat_ref[0:2, width:] = jnp.zeros((2, flat_ref.shape[1] - width), F32)
    for k in range(2):
        table = keep_ref[half + 16 * k : half + 16 * k + 16, :] + sent_ref[other, half + 16 * k : half + 16 * k + 16, :]
        for h in range(width // LANES):
            flat_ref[k : k + 1, h * LANES : (h + 1) * LANES] = table[h : h + 1, :]
    lane = lax.broadcasted_iota(jnp.int32, (2, LANES), 1)
    star = jnp.broadcast_to(star_ref[0].astype(F32), (2, LANES))
    for dp in range(rows_dp):
        tile = jnp.where(lane < share, flat_ref[0:2, dp * share : dp * share + LANES], star)
        for yl in range(2):
            piece = dp * 2 + yl
            rows = slice(piece * 24, piece * 24 + 24)
            at = ((yl * 4 + dp % 4) * 4 + dp // 4) * PIECE
            out_ref[at : at + 24, :] = keep_ref[rows, :] + sent_ref[other, rows, :]
            out_ref[at + 24 : at + 26, :] = tile


def series_kernel(blocks, low_ref, cot_ref, w_ref, dx_ref):
    row = lax.broadcasted_iota(jnp.int32, (SLAB, SLAB), 0)
    lane = lax.broadcasted_iota(jnp.int32, (SLAB, SLAB), 1)
    unorder = (row == (lane % CHUNKS) * STEPS + lane // CHUNKS).astype(F32).astype(BF16)
    for h in range(blocks):
        cols = slice(h * LANES, (h + 1) * LANES)
        low = jnp.dot(unorder, low_ref[cols, :], preferred_element_type=F32).astype(BF16)
        back = lax.dot_general(low, w_ref[cols, :], (((1,), (1,)), ((), ())), preferred_element_type=F32)
        dx_ref[0, :, cols] = (cot_ref[0, :, cols].astype(F32) + back).astype(BF16)


def piece_kernel(norm, share, got_ref, out_ref):
    first = (lax.axis_index("core") * 2 + lax.axis_index("yl")) * 4
    sources = got_ref.shape[0] // PIECE
    total = got_ref[0:24, :]
    for s in range(1, sources):
        total = total + got_ref[s * PIECE : s * PIECE + 24, :]
    terms = got_ref[pl.ds(24, sources, stride=PIECE), :]
    logs = jnp.sum(got_ref[pl.ds(25, sources, stride=PIECE), :], axis=0, keepdims=True)
    star = jnp.broadcast_to(terms[:, share : share + 1], terms.shape)
    hits = [star == (first + k).astype(F32) for k in range(4)]
    stars = [jnp.sum(jnp.where(hit, terms, 0.0), axis=0, keepdims=True) for hit in hits]
    total = total * norm
    tail = jnp.concatenate(stars + [logs], axis=0) * norm
    for d in range(out_ref.shape[0] // SHARE):
        out_ref[d * SHARE : d * SHARE + 24, :] = total
        out_ref[d * SHARE + 24 : d * SHARE + 29, :] = tail


def final_kernel(got_ref, weight_ref, star_ref, log_ref):
    share = star_ref.shape[1]
    chips = got_ref.shape[0] // SHARE // 2
    for core in range(2):
        for yl in range(2):
            q = core * 2 + yl
            parts = [(core * chips + chip) * SHARE for chip in range(chips) if chip % 2 == yl]
            total = got_ref[parts[0] : parts[0] + SHARE, :]
            for at in parts[1:]:
                total = total + got_ref[at : at + SHARE, :]
            weight_ref[q * 24 : q * 24 + 24, :] = total[0:24, :]
            star_ref[q * 4 : q * 4 + 4, :] = total[24:28, 0:share]
            if q == 0:
                log_ref[...] = total[28:29, 0:share]


def body(series, cotangent, step_times, seg_starts, star_of_row, block_weight, star_table, log_rate):
    _, slab_len, width = series.shape
    blocks = width // LANES
    slabs = lax.axis_size(("yh", "yl", "zh", "core"))
    rows_dp = lax.axis_size(("x", "zl"))
    norm = float(1.0 / (rows_dp * slabs * slab_len) ** 0.5)
    chips = slabs // 2
    log_blocks = log_rate.reshape(blocks, LANES)
    gain = jnp.sqrt(-jnp.expm1(-2.0 * jnp.exp(log_blocks)))
    smem = pl.BlockSpec(memory_space=pltpu.SMEM)
    vmem = pl.BlockSpec(memory_space=pltpu.VMEM)
    hbm = pl.BlockSpec(memory_space=pl.ANY)
    params = pltpu.CompilerParams(vmem_limit_bytes=24 * 1024 * 1024)
    big = pltpu.CompilerParams(vmem_limit_bytes=60 * 1024 * 1024)
    shape = jax.ShapeDtypeStruct
    common = (seg_starts, star_of_row, step_times, series, cotangent, block_weight, star_table, log_blocks)
    ends = pl.pallas_call(
        functools.partial(ends_kernel, blocks, chips),
        out_shape=shape((chips * CARRY, LANES), F32),
        in_specs=[hbm] * 8,
        out_specs=vmem,
        scratch_shapes=[pltpu.VMEM((2, 32, LANES), F32)]
        + [pltpu.SMEM(v.shape, v.dtype) for v in common[:2]]
        + [pltpu.VMEM(v.shape, v.dtype) for v in common[2:]]
        + [pltpu.SemaphoreType.DMA((5,)), pltpu.SemaphoreType.DMA((3,))],
        compiler_params=big,
        name="slab_ends",
    )(*common)
    ends = ends.reshape(chips, 1, CARRY * LANES)
    got = lax.all_gather(lax.all_to_all(ends, ("zh", "yh", "yl"), 0, 0), "core").reshape(slabs * CARRY, LANES)
    base, xt, sums, reach = pl.pallas_call(
        functools.partial(local_kernel, blocks),
        out_shape=[
            shape((width, slab_len), F32),
            shape((width, slab_len), BF16),
            shape((12, 16, LANES), F32),
            shape((2, slab_len, LANES), F32),
        ],
        in_specs=[smem, smem] + [vmem] * 7,
        out_specs=[vmem] * 4,
        compiler_params=params,
        cost_estimate=pl.CostEstimate(flops=20_000_000, bytes_accessed=4_000_000, transcendentals=200_000),
        name="local_scans",
    )(*common, gain)
    half_rows = width // 2 + 32
    low, keep, send = pl.pallas_call(
        functools.partial(combine_kernel, blocks, slabs, rows_dp),
        out_shape=[shape((width, slab_len), BF16)] + [shape((half_rows, LANES), F32)] * 2,
        in_specs=[vmem] * 7,
        out_specs=[vmem] * 3,
        scratch_shapes=[pltpu.VMEM((2, half_rows, LANES), F32)],
        compiler_params=params,
        name="gradients",
    )(log_blocks, gain, got, sums, base, xt, reach)
    sent = lax.all_gather(send, "core")
    pair = pl.pallas_call(
        functools.partial(pair_kernel, rows_dp),
        out_shape=shape((rows_dp * 2 * PIECE, LANES), F32),
        in_specs=[smem, vmem, vmem],
        out_specs=vmem,
        scratch_shapes=[pltpu.VMEM((8, width + LANES), F32)],
        compiler_params=params,
        name="pair_sum",
    )(star_of_row, keep, sent)
    grad_series = pl.pallas_call(
        functools.partial(series_kernel, blocks),
        out_shape=shape(series.shape, BF16),
        in_specs=[vmem] * 3,
        out_specs=vmem,
        compiler_params=params,
        cost_estimate=pl.CostEstimate(flops=100_000_000, bytes_accessed=1_600_000, transcendentals=0),
        name="series_gradient",
    )(low, cotangent, block_weight)
    pair = pair.reshape(rows_dp * 2, 1, PIECE * LANES)
    pieces = lax.all_to_all(pair, ("yl", "zl", "x"), 0, 0).reshape(rows_dp * 2 * PIECE, LANES)
    piece = pl.pallas_call(
        functools.partial(piece_kernel, norm, width // rows_dp),
        out_shape=shape((chips * SHARE, LANES), F32),
        in_specs=[vmem],
        out_specs=vmem,
        compiler_params=params,
        name="sum_pieces",
    )(pieces)
    spread = lax.all_to_all(piece.reshape(chips, 1, SHARE * LANES), ("zh", "yh", "yl"), 0, 0)
    both = lax.all_gather(spread, "core").reshape(slabs * SHARE, LANES)
    share = width // rows_dp
    grad_weight, grad_star, grad_log = pl.pallas_call(
        final_kernel,
        out_shape=[
            jax.ShapeDtypeStruct((share, LANES), F32),
            jax.ShapeDtypeStruct((star_table.shape[0], share), F32),
            jax.ShapeDtypeStruct((1, share), F32),
        ],
        in_specs=[vmem],
        out_specs=[vmem] * 3,
        compiler_params=params,
        name="outputs",
    )(both)
    return grad_series, grad_weight, grad_star, grad_log.reshape(share)


def solution(mesh):
    fine = Mesh(mesh.devices.reshape(4, 4, 4, 2, 2, 2), ("x", "zl", "yh", "yl", "zh", "core"))
    dp, ctx = ("x", "zl"), ("yh", "yl", "zh", "core")
    in_specs = (P(dp, ctx, None), P(dp, ctx, None), P(dp, ctx), P(dp, None), P(dp), P(), P(), P())
    out_specs = (P(dp, ctx, None), P(dp, None), P(None, dp), P(dp))
    return jax.shard_map(body, mesh=fine, in_specs=in_specs, out_specs=out_specs, check_vma=False)
```

```python
import functools
import jax
import jax.numpy as jnp
from jax import lax
from jax.experimental import pallas as pl
from jax.experimental.pallas import tpu as pltpu
from jax.sharding import Mesh, PartitionSpec as P

SLAB = 128
LANES = 128
CHUNKS = 8
STEPS = SLAB // CHUNKS
FAR = 1e9
CARRY = 25
SHARE = 29
PIECE = 26
F32 = jnp.float32
BF16 = jnp.bfloat16


def slab_index():
    chip = (lax.axis_index("yh") * 2 + lax.axis_index("yl")) * 2 + lax.axis_index("zh")
    return chip * 2 + lax.axis_index("core")


def chip_slot(chip, chips):
    return chip % 2 * (chips // 2) + chip // 2


def elapsed_row(starts_ref, times_ref, me):
    position = lax.broadcasted_iota(jnp.int32, (1, SLAB), 1) + me * SLAB
    reset = position == starts_ref[0, 0]
    for k in range(1, starts_ref.shape[1]):
        reset = jnp.logical_or(reset, position == starts_ref[0, k])
    return jnp.where(reset, FAR, times_ref[...])


def ends_kernel(
    blocks, chips, starts_hbm, star_hbm, times_hbm, series_hbm, cot_hbm, w_hbm, table_hbm, lograte_hbm,
    out_ref, ends_ref, starts_ref, star_ref, times_ref, series_ref, cot_ref, w_ref, table_ref, lograte_ref, sems, load_sems,
):
    sources = (starts_hbm, star_hbm, times_hbm, table_hbm, lograte_hbm)
    targets = (starts_ref, star_ref, times_ref, table_ref, lograte_ref)
    copies = [pltpu.make_async_copy(a, b, sems.at[k]) for k, (a, b) in enumerate(zip(sources, targets))]
    sources, targets = (series_hbm, w_hbm, cot_hbm), (series_ref, w_ref, cot_ref)
    loads = [pltpu.make_async_copy(a, b, load_sems.at[k]) for k, (a, b) in enumerate(zip(sources, targets))]
    for copy in copies[:3] + loads + copies[3:]:
        copy.start()
    core = lax.axis_index("core")
    me = slab_index()
    for copy in copies[:3]:
        copy.wait()
    elapsed = elapsed_row(starts_ref, times_ref, me)
    row = lax.broadcasted_iota(jnp.int32, (SLAB, SLAB), 0)
    lane = lax.broadcasted_iota(jnp.int32, (SLAB, SLAB), 1)
    spread = jnp.broadcast_to(elapsed, (SLAB, SLAB))
    to_end = jnp.sum(jnp.where(lane > row, spread, 0.0), axis=1, keepdims=True)
    from_start = jnp.sum(jnp.where(lane <= row, spread, 0.0), axis=1, keepdims=True)
    to_end = jnp.broadcast_to(to_end, (SLAB, LANES))
    from_start = jnp.broadcast_to(from_start, (SLAB, LANES))
    total = jnp.sum(elapsed, axis=1, keepdims=True)
    for copy in copies[3:] + loads:
        copy.wait()
    bias = table_ref[pl.ds(star_ref[0], 1), :]
    for h in range(blocks):
        cols = slice(h * LANES, (h + 1) * LANES)
        proj = jnp.dot(series_ref[0, :, cols], w_ref[cols, :], preferred_element_type=F32) + bias[:, cols]
        grad = cot_ref[0, :, cols].astype(F32)
        slope = -jnp.exp(lograte_ref[h : h + 1, :])
        late = jnp.exp(slope * to_end)
        early = jnp.exp(slope * from_start)
        ends_ref[0, h : h + 1, :] = jnp.sum(late * proj, axis=0, keepdims=True)
        ends_ref[0, blocks + h : blocks + h + 1, :] = jnp.sum(late * grad, axis=0, keepdims=True)
        ends_ref[1, h : h + 1, :] = jnp.sum(early * proj, axis=0, keepdims=True)
        ends_ref[1, blocks + h : blocks + h + 1, :] = jnp.sum(early * grad, axis=0, keepdims=True)
    tail = jnp.broadcast_to(total, (8, LANES))
    ends_ref[0, 2 * blocks : 2 * blocks + 8, :] = tail
    ends_ref[1, 2 * blocks : 2 * blocks + 8, :] = tail
    for chip in range(chips):
        at = chip_slot(chip, chips) * CARRY
        out_ref[at : at + CARRY, :] = ends_ref[jnp.where(2 * chip + 1 - core > me, 0, 1), 0:CARRY, :]


def shift(x, k, fill, sublane):
    if k > 0:
        return jnp.where(sublane < k, fill, pltpu.roll(x, k, 0))
    return jnp.where(sublane >= CHUNKS + k, fill, pltpu.roll(x, CHUNKS + k, 0))


def chunk_entries(ends, through, sublane, sign):
    for k in (1, 2, 4):
        ends = ends + through * shift(ends, sign * k, 0.0, sublane)
        through = through * shift(through, sign * k, 1.0, sublane)
    return shift(ends, sign, 0.0, sublane), shift(through, sign, 1.0, sublane)


def local_kernel(
    blocks, starts_ref, star_ref, times_ref, series_ref, cot_ref, w_ref, table_ref, lograte_ref, gain_ref,
    base_ref, xt_ref, table_sums_ref, reach_ref,
):
    me = slab_index()
    elapsed = elapsed_row(starts_ref, times_ref, me)
    row = lax.broadcasted_iota(jnp.int32, (SLAB, SLAB), 0)
    lane = lax.broadcasted_iota(jnp.int32, (SLAB, SLAB), 1)
    sublane = lax.broadcasted_iota(jnp.int32, (CHUNKS, LANES), 0)
    time_of_row = (row % CHUNKS) * STEPS + row // CHUNKS
    order = (lane == time_of_row).astype(F32).astype(BF16)
    gap = jnp.sum(jnp.where(lane == time_of_row, jnp.broadcast_to(elapsed, (SLAB, SLAB)), 0.0), axis=1, keepdims=True)
    gap = jnp.broadcast_to(gap, (SLAB, LANES))
    spread = jnp.broadcast_to(elapsed, (SLAB, SLAB))
    for k, mask in enumerate((lane <= time_of_row, lane > time_of_row)):
        reach = jnp.sum(jnp.where(mask, spread, 0.0), axis=1, keepdims=True)
        reach_ref[k] = jnp.broadcast_to(reach, (SLAB, LANES))
    bias = table_ref[pl.ds(star_ref[0], 1), :]
    for h in range(blocks):
        cols = slice(h * LANES, (h + 1) * LANES)
        rate = jnp.exp(lograte_ref[h : h + 1, :])
        gain = gain_ref[h : h + 1, :]
        x = jnp.dot(order, series_ref[0, :, cols], preferred_element_type=F32)
        xt_ref[cols, :] = x.T.astype(BF16)
        grad = jnp.dot(order, cot_ref[0, :, cols], preferred_element_type=F32)
        proj = jnp.dot(x.astype(BF16), w_ref[cols, :], preferred_element_type=F32) + bias[:, cols]
        drive = gain * proj
        decay = jnp.exp(-rate * gap)
        tiles = lambda v: [v[j * CHUNKS : (j + 1) * CHUNKS, :] for j in range(STEPS)]
        a, d, g, pr, dt = tiles(decay), tiles(drive), tiles(grad), tiles(proj), tiles(gap)
        zero = jnp.zeros((CHUNKS, LANES), F32)
        before_d, before_g, through = [zero], [zero], [a[0]]
        state_d, state_g = d[0], g[0]
        for j in range(1, STEPS):
            before_d.append(a[j] * state_d)
            before_g.append(a[j] * state_g)
            state_d = before_d[j] + d[j]
            state_g = before_g[j] + g[j]
            through.append(a[j] * through[j - 1])
        after_d, after_g, back = [None] * STEPS, [None] * STEPS, [None] * STEPS
        after_d[-1], after_g[-1], back[-1] = d[-1], g[-1], jnp.ones((CHUNKS, LANES), F32)
        for j in reversed(range(STEPS - 1)):
            after_d[j] = a[j + 1] * after_d[j + 1] + d[j]
            after_g[j] = a[j + 1] * after_g[j + 1] + g[j]
            back[j] = a[j + 1] * back[j + 1]
        enter_d, onto = chunk_entries(state_d, through[-1], sublane, 1)
        enter_g, _ = chunk_entries(state_g, through[-1], sublane, 1)
        leave_d, off = chunk_entries(a[0] * after_d[0], through[-1], sublane, -1)
        leave_g, _ = chunk_entries(a[0] * after_g[0], through[-1], sublane, -1)
        sums = [zero] * 12
        for j in range(STEPS):
            kept_d = before_d[j] + through[j] * enter_d
            kept_g = before_g[j] + through[j] * enter_g
            later_d = after_d[j] + back[j] * leave_d
            later_g = after_g[j] + back[j] * leave_g
            on, off_j = through[j] * onto, back[j] * off
            base = later_g + kept_g + g[j]
            rows = slice(h * LANES + j * CHUNKS, h * LANES + (j + 1) * CHUNKS)
            base_ref[rows, :] = gain * base
            dt_on, dt_off = dt[j] * on, dt[j] * off_j
            terms = (
                dt[j] * (later_g * kept_d + kept_g * later_d),
                dt_off * kept_d,
                dt_on * later_g,
                dt_on * off_j,
                dt_off * kept_g,
                dt_on * later_d,
                base,
                on,
                off_j,
                base * pr[j],
                on * pr[j],
                off_j * pr[j],
            )
            sums = [s + t for s, t in zip(sums, terms)]
        for k, v in enumerate(sums):
            table_sums_ref[k, h : h + 1, :] = jnp.sum(v, axis=0, keepdims=True)


def combine_kernel(
    blocks, slabs, rows_dp, lograte_ref, gain_ref, got_ref, sums_ref, base_ref, xt_ref, reach_ref,
    low_ref, keep_ref, send_ref, part_ref,
):
    half = blocks * LANES // 2
    me = slab_index()
    mine = lax.axis_index("core")
    slope = -jnp.exp(lograte_ref[...])
    slope2 = jnp.concatenate([slope, slope], axis=0)
    start = lambda s: (s % 2 * (slabs // 2) + chip_slot(s // 2, slabs // 2)) * CARRY
    took = lambda s: got_ref[start(s) + 2 * blocks : start(s) + 2 * blocks + 1, :]
    between = [None] * slabs
    run = jnp.zeros((1, LANES), F32)
    for s in reversed(range(slabs)):
        between[s] = run
        run = jnp.where(s < me, run + took(s), 0.0)
    run = jnp.zeros((1, LANES), F32)
    carry_early = jnp.zeros((2 * blocks, LANES), F32)
    carry_late = jnp.zeros((2 * blocks, LANES), F32)
    for s in range(slabs):
        x = jnp.exp(slope2 * jnp.where(s < me, between[s], run)) * got_ref[start(s) : start(s) + 2 * blocks, :]
        carry_early = carry_early + jnp.where(s < me, x, 0.0)
        carry_late = carry_late + jnp.where(s > me, x, 0.0)
        run = jnp.where(s > me, run + took(s), 0.0)
    gain = gain_ref[...]
    early_d, early_g = gain * carry_early[0:blocks], carry_early[blocks:]
    late_d, late_g = gain * carry_late[0:blocks], carry_late[blocks:]
    c = [sums_ref[k, 0:blocks, :] for k in range(12)]
    rate_sum = c[0] + late_g * c[1] + early_d * c[2] + (late_g * early_d + early_g * late_d) * c[3]
    rate_sum = rate_sum + late_d * c[4] + early_g * c[5]
    grad_sum = c[6] + early_g * c[7] + late_g * c[8]
    cross_sum = c[9] + early_g * c[10] + late_g * c[11]
    proj_sum = gain * grad_sum
    log_sum = jnp.exp(2.0 * slope) / gain * cross_sum - rate_sum
    log_sum = -slope * log_sum
    for core in range(2):
        part_ref[core, half : half + blocks, :] = proj_sum
        part_ref[core, half + 16 : half + 16 + blocks, :] = log_sum

    enter, leave = gain * early_g, gain * late_g
    from_start, to_end = reach_ref[0], reach_ref[1]
    for h in range(blocks):
        rows = slice(h * LANES, (h + 1) * LANES)
        row = slice(h, h + 1)
        low = base_ref[rows, :] + jnp.exp(slope[row] * from_start) * enter[row] + jnp.exp(slope[row] * to_end) * leave[row]
        low = low.astype(BF16)
        low_ref[rows, :] = low
        product = jnp.dot(xt_ref[rows, :], low, preferred_element_type=F32)
        for k in range(LANES // 8):
            piece, third = divmod(h * (LANES // 8) + k, 3)
            dp, quarter = divmod(piece, 4)
            core, yl = divmod(quarter, 2)
            at = (dp * 2 + yl) * 24 + third * 8
            part_ref[core, at : at + 8, :] = product[k * 8 : k * 8 + 8, :]
    keep_ref[...] = part_ref[mine]
    send_ref[...] = part_ref[1 - mine]


def pair_kernel(rows_dp, star_ref, keep_ref, sent_ref, out_ref, flat_ref):
    other = 1 - lax.axis_index("core")
    half = keep_ref.shape[0] - 32
    width = 2 * half
    share = width // rows_dp
    flat_ref[0:2, width:] = jnp.zeros((2, flat_ref.shape[1] - width), F32)
    for k in range(2):
        table = keep_ref[half + 16 * k : half + 16 * k + 16, :] + sent_ref[other, half + 16 * k : half + 16 * k + 16, :]
        for h in range(width // LANES):
            flat_ref[k : k + 1, h * LANES : (h + 1) * LANES] = table[h : h + 1, :]
    lane = lax.broadcasted_iota(jnp.int32, (2, LANES), 1)
    star = jnp.broadcast_to(star_ref[0].astype(F32), (2, LANES))
    for dp in range(rows_dp):
        tile = jnp.where(lane < share, flat_ref[0:2, dp * share : dp * share + LANES], star)
        for yl in range(2):
            piece = dp * 2 + yl
            rows = slice(piece * 24, piece * 24 + 24)
            at = piece * PIECE
            out_ref[at : at + 24, :] = keep_ref[rows, :] + sent_ref[other, rows, :]
            out_ref[at + 24 : at + 26, :] = tile


def series_kernel(blocks, low_ref, cot_ref, w_ref, dx_ref):
    row = lax.broadcasted_iota(jnp.int32, (SLAB, SLAB), 0)
    lane = lax.broadcasted_iota(jnp.int32, (SLAB, SLAB), 1)
    unorder = (row == (lane % CHUNKS) * STEPS + lane // CHUNKS).astype(F32).astype(BF16)
    for h in range(blocks):
        cols = slice(h * LANES, (h + 1) * LANES)
        low = jnp.dot(unorder, low_ref[cols, :], preferred_element_type=F32).astype(BF16)
        back = lax.dot_general(low, w_ref[cols, :], (((1,), (1,)), ((), ())), preferred_element_type=F32)
        dx_ref[0, :, cols] = (cot_ref[0, :, cols].astype(F32) + back).astype(BF16)


def piece_kernel(norm, share, got_ref, out_ref):
    first = (lax.axis_index("core") * 2 + lax.axis_index("yl")) * 4
    sources = got_ref.shape[0] // PIECE
    total = got_ref[0:24, :]
    for s in range(1, sources):
        total = total + got_ref[s * PIECE : s * PIECE + 24, :]
    terms = got_ref[pl.ds(24, sources, stride=PIECE), :]
    logs = jnp.sum(got_ref[pl.ds(25, sources, stride=PIECE), :], axis=0, keepdims=True)
    star = jnp.broadcast_to(terms[:, share : share + 1], terms.shape)
    hits = [star == (first + k).astype(F32) for k in range(4)]
    stars = [jnp.sum(jnp.where(hit, terms, 0.0), axis=0, keepdims=True) for hit in hits]
    total = total * norm
    tail = jnp.concatenate(stars + [logs], axis=0) * norm
    for d in range(out_ref.shape[0] // SHARE):
        out_ref[d * SHARE : d * SHARE + 24, :] = total
        out_ref[d * SHARE + 24 : d * SHARE + 29, :] = tail


def final_kernel(got_ref, weight_ref, star_ref, log_ref):
    share = star_ref.shape[1]
    chips = got_ref.shape[0] // SHARE // 2
    for core in range(2):
        for yl in range(2):
            q = core * 2 + yl
            parts = [(core * chips + chip) * SHARE for chip in range(chips) if chip % 2 == yl]
            total = got_ref[parts[0] : parts[0] + SHARE, :]
            for at in parts[1:]:
                total = total + got_ref[at : at + SHARE, :]
            weight_ref[q * 24 : q * 24 + 24, :] = total[0:24, :]
            star_ref[q * 4 : q * 4 + 4, :] = total[24:28, 0:share]
            if q == 0:
                log_ref[...] = total[28:29, 0:share]


def body(series, cotangent, step_times, seg_starts, star_of_row, block_weight, star_table, log_rate):
    _, slab_len, width = series.shape
    blocks = width // LANES
    slabs = lax.axis_size(("yh", "yl", "zh", "core"))
    rows_dp = lax.axis_size(("x", "zl"))
    norm = float(1.0 / (rows_dp * slabs * slab_len) ** 0.5)
    chips = slabs // 2
    log_blocks = log_rate.reshape(blocks, LANES)
    gain = jnp.sqrt(-jnp.expm1(-2.0 * jnp.exp(log_blocks)))
    smem = pl.BlockSpec(memory_space=pltpu.SMEM)
    vmem = pl.BlockSpec(memory_space=pltpu.VMEM)
    hbm = pl.BlockSpec(memory_space=pl.ANY)
    params = pltpu.CompilerParams(vmem_limit_bytes=24 * 1024 * 1024)
    big = pltpu.CompilerParams(vmem_limit_bytes=60 * 1024 * 1024)
    shape = jax.ShapeDtypeStruct
    common = (seg_starts, star_of_row, step_times, series, cotangent, block_weight, star_table, log_blocks)
    ends = pl.pallas_call(
        functools.partial(ends_kernel, blocks, chips),
        out_shape=shape((chips * CARRY, LANES), F32),
        in_specs=[hbm] * 8,
        out_specs=vmem,
        scratch_shapes=[pltpu.VMEM((2, 32, LANES), F32)]
        + [pltpu.SMEM(v.shape, v.dtype) for v in common[:2]]
        + [pltpu.VMEM(v.shape, v.dtype) for v in common[2:]]
        + [pltpu.SemaphoreType.DMA((5,)), pltpu.SemaphoreType.DMA((3,))],
        compiler_params=big,
        name="slab_ends",
    )(*common)
    ends = ends.reshape(chips, 1, CARRY * LANES)
    got = lax.all_gather(lax.all_to_all(ends, ("zh", "yh", "yl"), 0, 0), "core").reshape(slabs * CARRY, LANES)
    base, xt, sums, reach = pl.pallas_call(
        functools.partial(local_kernel, blocks),
        out_shape=[
            shape((width, slab_len), F32),
            shape((width, slab_len), BF16),
            shape((12, 16, LANES), F32),
            shape((2, slab_len, LANES), F32),
        ],
        in_specs=[smem, smem] + [vmem] * 7,
        out_specs=[vmem] * 4,
        compiler_params=params,
        cost_estimate=pl.CostEstimate(flops=20_000_000, bytes_accessed=4_000_000, transcendentals=200_000),
        name="local_scans",
    )(*common, gain)
    half_rows = width // 2 + 32
    low, keep, send = pl.pallas_call(
        functools.partial(combine_kernel, blocks, slabs, rows_dp),
        out_shape=[shape((width, slab_len), BF16)] + [shape((half_rows, LANES), F32)] * 2,
        in_specs=[vmem] * 7,
        out_specs=[vmem] * 3,
        scratch_shapes=[pltpu.VMEM((2, half_rows, LANES), F32)],
        compiler_params=params,
        name="gradients",
    )(log_blocks, gain, got, sums, base, xt, reach)
    sent = lax.all_gather(send, "core")
    pair = pl.pallas_call(
        functools.partial(pair_kernel, rows_dp),
        out_shape=shape((rows_dp * 2 * PIECE, LANES), F32),
        in_specs=[smem, vmem, vmem],
        out_specs=vmem,
        scratch_shapes=[pltpu.VMEM((8, width + LANES), F32)],
        compiler_params=params,
        name="pair_sum",
    )(star_of_row, keep, sent)
    grad_series = pl.pallas_call(
        functools.partial(series_kernel, blocks),
        out_shape=shape(series.shape, BF16),
        in_specs=[vmem] * 3,
        out_specs=vmem,
        compiler_params=params,
        cost_estimate=pl.CostEstimate(flops=100_000_000, bytes_accessed=1_600_000, transcendentals=0),
        name="series_gradient",
    )(low, cotangent, block_weight)
    pair = pair.reshape(rows_dp * 2, 1, PIECE * LANES)
    pieces = lax.all_to_all(pair, ("x", "zl", "yl"), 0, 0).reshape(rows_dp * 2 * PIECE, LANES)
    piece = pl.pallas_call(
        functools.partial(piece_kernel, norm, width // rows_dp),
        out_shape=shape((chips * SHARE, LANES), F32),
        in_specs=[vmem],
        out_specs=vmem,
        compiler_params=params,
        name="sum_pieces",
    )(pieces)
    spread = lax.all_to_all(piece.reshape(chips, 1, SHARE * LANES), ("zh", "yh", "yl"), 0, 0)
    both = lax.all_gather(spread, "core").reshape(slabs * SHARE, LANES)
    share = width // rows_dp
    grad_weight, grad_star, grad_log = pl.pallas_call(
        final_kernel,
        out_shape=[
            jax.ShapeDtypeStruct((share, LANES), F32),
            jax.ShapeDtypeStruct((star_table.shape[0], share), F32),
            jax.ShapeDtypeStruct((1, share), F32),
        ],
        in_specs=[vmem],
        out_specs=[vmem] * 3,
        compiler_params=params,
        name="outputs",
    )(both)
    return grad_series, grad_weight, grad_star, grad_log.reshape(share)


def solution(mesh):
    fine = Mesh(mesh.devices.reshape(4, 4, 4, 2, 2, 2), ("x", "zl", "yh", "yl", "zh", "core"))
    dp, ctx = ("x", "zl"), ("yh", "yl", "zh", "core")
    in_specs = (P(dp, ctx, None), P(dp, ctx, None), P(dp, ctx), P(dp, None), P(dp), P(), P(), P())
    out_specs = (P(dp, ctx, None), P(dp, None), P(None, dp), P(dp))
    return jax.shard_map(body, mesh=fine, in_specs=in_specs, out_specs=out_specs, check_vma=False)
```

```python
import functools
import jax
import jax.numpy as jnp
from jax import lax
from jax.experimental import pallas as pl
from jax.experimental.pallas import tpu as pltpu
from jax.sharding import Mesh, PartitionSpec as P

SLAB = 128
LANES = 128
CHUNKS = 8
STEPS = SLAB // CHUNKS
FAR = 1e9
CARRY = 25
SHARE = 57
ROWS = 48
PIECE = 50
F32 = jnp.float32
BF16 = jnp.bfloat16


def slab_index():
    chip = (lax.axis_index("yh") * 2 + lax.axis_index("yl")) * 2 + lax.axis_index("zh")
    return chip * 2 + lax.axis_index("core")


def chip_slot(chip, chips):
    return chip % 2 * (chips // 2) + chip // 2


def elapsed_row(starts_ref, times_ref, me):
    position = lax.broadcasted_iota(jnp.int32, (1, SLAB), 1) + me * SLAB
    reset = position == starts_ref[0, 0]
    for k in range(1, starts_ref.shape[1]):
        reset = jnp.logical_or(reset, position == starts_ref[0, k])
    return jnp.where(reset, FAR, times_ref[...])


def ends_kernel(
    blocks, chips, starts_hbm, star_hbm, times_hbm, series_hbm, cot_hbm, w_hbm, table_hbm, lograte_hbm,
    out_ref, ends_ref, starts_ref, star_ref, times_ref, series_ref, cot_ref, w_ref, table_ref, lograte_ref, sems, load_sems,
):
    sources = (starts_hbm, star_hbm, times_hbm, table_hbm, lograte_hbm)
    targets = (starts_ref, star_ref, times_ref, table_ref, lograte_ref)
    copies = [pltpu.make_async_copy(a, b, sems.at[k]) for k, (a, b) in enumerate(zip(sources, targets))]
    sources, targets = (series_hbm, w_hbm, cot_hbm), (series_ref, w_ref, cot_ref)
    loads = [pltpu.make_async_copy(a, b, load_sems.at[k]) for k, (a, b) in enumerate(zip(sources, targets))]
    for copy in copies[:3] + loads + copies[3:]:
        copy.start()
    core = lax.axis_index("core")
    me = slab_index()
    for copy in copies[:3]:
        copy.wait()
    elapsed = elapsed_row(starts_ref, times_ref, me)
    row = lax.broadcasted_iota(jnp.int32, (SLAB, SLAB), 0)
    lane = lax.broadcasted_iota(jnp.int32, (SLAB, SLAB), 1)
    spread = jnp.broadcast_to(elapsed, (SLAB, SLAB))
    to_end = jnp.sum(jnp.where(lane > row, spread, 0.0), axis=1, keepdims=True)
    from_start = jnp.sum(jnp.where(lane <= row, spread, 0.0), axis=1, keepdims=True)
    to_end = jnp.broadcast_to(to_end, (SLAB, LANES))
    from_start = jnp.broadcast_to(from_start, (SLAB, LANES))
    total = jnp.sum(elapsed, axis=1, keepdims=True)
    for copy in copies[3:] + loads:
        copy.wait()
    bias = table_ref[pl.ds(star_ref[0], 1), :]
    for h in range(blocks):
        cols = slice(h * LANES, (h + 1) * LANES)
        proj = jnp.dot(series_ref[0, :, cols], w_ref[cols, :], preferred_element_type=F32) + bias[:, cols]
        grad = cot_ref[0, :, cols].astype(F32)
        slope = -jnp.exp(lograte_ref[h : h + 1, :])
        late = jnp.exp(slope * to_end)
        early = jnp.exp(slope * from_start)
        ends_ref[0, h : h + 1, :] = jnp.sum(late * proj, axis=0, keepdims=True)
        ends_ref[0, blocks + h : blocks + h + 1, :] = jnp.sum(late * grad, axis=0, keepdims=True)
        ends_ref[1, h : h + 1, :] = jnp.sum(early * proj, axis=0, keepdims=True)
        ends_ref[1, blocks + h : blocks + h + 1, :] = jnp.sum(early * grad, axis=0, keepdims=True)
    tail = jnp.broadcast_to(total, (8, LANES))
    ends_ref[0, 2 * blocks : 2 * blocks + 8, :] = tail
    ends_ref[1, 2 * blocks : 2 * blocks + 8, :] = tail
    for chip in range(chips):
        at = chip_slot(chip, chips) * CARRY
        out_ref[at : at + CARRY, :] = ends_ref[jnp.where(2 * chip + 1 - core > me, 0, 1), 0:CARRY, :]


def shift(x, k, fill, sublane):
    if k > 0:
        return jnp.where(sublane < k, fill, pltpu.roll(x, k, 0))
    return jnp.where(sublane >= CHUNKS + k, fill, pltpu.roll(x, CHUNKS + k, 0))


def chunk_entries(ends, through, sublane, sign):
    for k in (1, 2, 4):
        ends = ends + through * shift(ends, sign * k, 0.0, sublane)
        through = through * shift(through, sign * k, 1.0, sublane)
    return shift(ends, sign, 0.0, sublane), shift(through, sign, 1.0, sublane)


def local_kernel(
    blocks, starts_ref, star_ref, times_ref, series_ref, cot_ref, w_ref, table_ref, lograte_ref, gain_ref,
    base_ref, xt_ref, table_sums_ref, reach_ref,
):
    me = slab_index()
    elapsed = elapsed_row(starts_ref, times_ref, me)
    row = lax.broadcasted_iota(jnp.int32, (SLAB, SLAB), 0)
    lane = lax.broadcasted_iota(jnp.int32, (SLAB, SLAB), 1)
    sublane = lax.broadcasted_iota(jnp.int32, (CHUNKS, LANES), 0)
    time_of_row = (row % CHUNKS) * STEPS + row // CHUNKS
    order = (lane == time_of_row).astype(F32).astype(BF16)
    gap = jnp.sum(jnp.where(lane == time_of_row, jnp.broadcast_to(elapsed, (SLAB, SLAB)), 0.0), axis=1, keepdims=True)
    gap = jnp.broadcast_to(gap, (SLAB, LANES))
    spread = jnp.broadcast_to(elapsed, (SLAB, SLAB))
    for k, mask in enumerate((lane <= time_of_row, lane > time_of_row)):
        reach = jnp.sum(jnp.where(mask, spread, 0.0), axis=1, keepdims=True)
        reach_ref[k] = jnp.broadcast_to(reach, (SLAB, LANES))
    bias = table_ref[pl.ds(star_ref[0], 1), :]
    for h in range(blocks):
        cols = slice(h * LANES, (h + 1) * LANES)
        rate = jnp.exp(lograte_ref[h : h + 1, :])
        gain = gain_ref[h : h + 1, :]
        x = jnp.dot(order, series_ref[0, :, cols], preferred_element_type=F32)
        xt_ref[cols, :] = x.T.astype(BF16)
        grad = jnp.dot(order, cot_ref[0, :, cols], preferred_element_type=F32)
        proj = jnp.dot(x.astype(BF16), w_ref[cols, :], preferred_element_type=F32) + bias[:, cols]
        drive = gain * proj
        decay = jnp.exp(-rate * gap)
        tiles = lambda v: [v[j * CHUNKS : (j + 1) * CHUNKS, :] for j in range(STEPS)]
        a, d, g, pr, dt = tiles(decay), tiles(drive), tiles(grad), tiles(proj), tiles(gap)
        zero = jnp.zeros((CHUNKS, LANES), F32)
        before_d, before_g, through = [zero], [zero], [a[0]]
        state_d, state_g = d[0], g[0]
        for j in range(1, STEPS):
            before_d.append(a[j] * state_d)
            before_g.append(a[j] * state_g)
            state_d = before_d[j] + d[j]
            state_g = before_g[j] + g[j]
            through.append(a[j] * through[j - 1])
        after_d, after_g, back = [None] * STEPS, [None] * STEPS, [None] * STEPS
        after_d[-1], after_g[-1], back[-1] = d[-1], g[-1], jnp.ones((CHUNKS, LANES), F32)
        for j in reversed(range(STEPS - 1)):
            after_d[j] = a[j + 1] * after_d[j + 1] + d[j]
            after_g[j] = a[j + 1] * after_g[j + 1] + g[j]
            back[j] = a[j + 1] * back[j + 1]
        enter_d, onto = chunk_entries(state_d, through[-1], sublane, 1)
        enter_g, _ = chunk_entries(state_g, through[-1], sublane, 1)
        leave_d, off = chunk_entries(a[0] * after_d[0], through[-1], sublane, -1)
        leave_g, _ = chunk_entries(a[0] * after_g[0], through[-1], sublane, -1)
        sums = [zero] * 12
        for j in range(STEPS):
            kept_d = before_d[j] + through[j] * enter_d
            kept_g = before_g[j] + through[j] * enter_g
            later_d = after_d[j] + back[j] * leave_d
            later_g = after_g[j] + back[j] * leave_g
            on, off_j = through[j] * onto, back[j] * off
            base = later_g + kept_g + g[j]
            rows = slice(h * LANES + j * CHUNKS, h * LANES + (j + 1) * CHUNKS)
            base_ref[rows, :] = gain * base
            dt_on, dt_off = dt[j] * on, dt[j] * off_j
            terms = (
                dt[j] * (later_g * kept_d + kept_g * later_d),
                dt_off * kept_d,
                dt_on * later_g,
                dt_on * off_j,
                dt_off * kept_g,
                dt_on * later_d,
                base,
                on,
                off_j,
                base * pr[j],
                on * pr[j],
                off_j * pr[j],
            )
            sums = [s + t for s, t in zip(sums, terms)]
        for k, v in enumerate(sums):
            table_sums_ref[k, h : h + 1, :] = jnp.sum(v, axis=0, keepdims=True)


def combine_kernel(
    blocks, slabs, rows_dp, lograte_ref, gain_ref, got_ref, sums_ref, base_ref, xt_ref, reach_ref,
    low_ref, keep_ref, send_ref, part_ref,
):
    half = blocks * LANES // 2
    me = slab_index()
    mine = lax.axis_index("core")
    slope = -jnp.exp(lograte_ref[...])
    slope2 = jnp.concatenate([slope, slope], axis=0)
    start = lambda s: (s % 2 * (slabs // 2) + chip_slot(s // 2, slabs // 2)) * CARRY
    took = lambda s: got_ref[start(s) + 2 * blocks : start(s) + 2 * blocks + 1, :]
    between = [None] * slabs
    run = jnp.zeros((1, LANES), F32)
    for s in reversed(range(slabs)):
        between[s] = run
        run = jnp.where(s < me, run + took(s), 0.0)
    run = jnp.zeros((1, LANES), F32)
    carry_early = jnp.zeros((2 * blocks, LANES), F32)
    carry_late = jnp.zeros((2 * blocks, LANES), F32)
    for s in range(slabs):
        x = jnp.exp(slope2 * jnp.where(s < me, between[s], run)) * got_ref[start(s) : start(s) + 2 * blocks, :]
        carry_early = carry_early + jnp.where(s < me, x, 0.0)
        carry_late = carry_late + jnp.where(s > me, x, 0.0)
        run = jnp.where(s > me, run + took(s), 0.0)
    gain = gain_ref[...]
    early_d, early_g = gain * carry_early[0:blocks], carry_early[blocks:]
    late_d, late_g = gain * carry_late[0:blocks], carry_late[blocks:]
    c = [sums_ref[k, 0:blocks, :] for k in range(12)]
    rate_sum = c[0] + late_g * c[1] + early_d * c[2] + (late_g * early_d + early_g * late_d) * c[3]
    rate_sum = rate_sum + late_d * c[4] + early_g * c[5]
    grad_sum = c[6] + early_g * c[7] + late_g * c[8]
    cross_sum = c[9] + early_g * c[10] + late_g * c[11]
    proj_sum = gain * grad_sum
    log_sum = jnp.exp(2.0 * slope) / gain * cross_sum - rate_sum
    log_sum = -slope * log_sum
    for core in range(2):
        part_ref[core, half : half + blocks, :] = proj_sum
        part_ref[core, half + 16 : half + 16 + blocks, :] = log_sum

    enter, leave = gain * early_g, gain * late_g
    from_start, to_end = reach_ref[0], reach_ref[1]
    for h in range(blocks):
        rows = slice(h * LANES, (h + 1) * LANES)
        row = slice(h, h + 1)
        low = base_ref[rows, :] + jnp.exp(slope[row] * from_start) * enter[row] + jnp.exp(slope[row] * to_end) * leave[row]
        low = low.astype(BF16)
        low_ref[rows, :] = low
        product = jnp.dot(xt_ref[rows, :], low, preferred_element_type=F32)
        for k in range(LANES // 8):
            piece, third = divmod(h * (LANES // 8) + k, 3)
            dp, quarter = divmod(piece, 4)
            core, yl = divmod(quarter, 2)
            at = (dp * 2 + yl) * 24 + third * 8
            part_ref[core, at : at + 8, :] = product[k * 8 : k * 8 + 8, :]
    keep_ref[...] = part_ref[mine]
    send_ref[...] = part_ref[1 - mine]


def pair_kernel(rows_dp, star_ref, keep_ref, sent_ref, out_ref, flat_ref):
    other = 1 - lax.axis_index("core")
    half = keep_ref.shape[0] - 32
    width = 2 * half
    share = width // rows_dp
    flat_ref[0:2, width:] = jnp.zeros((2, flat_ref.shape[1] - width), F32)
    for k in range(2):
        table = keep_ref[half + 16 * k : half + 16 * k + 16, :] + sent_ref[other, half + 16 * k : half + 16 * k + 16, :]
        for h in range(width // LANES):
            flat_ref[k : k + 1, h * LANES : (h + 1) * LANES] = table[h : h + 1, :]
    lane = lax.broadcasted_iota(jnp.int32, (2, LANES), 1)
    star = jnp.broadcast_to(star_ref[0].astype(F32), (2, LANES))
    for dp in range(rows_dp):
        tile = jnp.where(lane < share, flat_ref[0:2, dp * share : dp * share + LANES], star)
        rows = slice(dp * ROWS, (dp + 1) * ROWS)
        at = dp * PIECE
        out_ref[at : at + ROWS, :] = keep_ref[rows, :] + sent_ref[other, rows, :]
        out_ref[at + ROWS : at + ROWS + 2, :] = tile


def series_kernel(blocks, low_ref, cot_ref, w_ref, dx_ref):
    row = lax.broadcasted_iota(jnp.int32, (SLAB, SLAB), 0)
    lane = lax.broadcasted_iota(jnp.int32, (SLAB, SLAB), 1)
    unorder = (row == (lane % CHUNKS) * STEPS + lane // CHUNKS).astype(F32).astype(BF16)
    for h in range(blocks):
        cols = slice(h * LANES, (h + 1) * LANES)
        low = jnp.dot(unorder, low_ref[cols, :], preferred_element_type=F32).astype(BF16)
        back = lax.dot_general(low, w_ref[cols, :], (((1,), (1,)), ((), ())), preferred_element_type=F32)
        dx_ref[0, :, cols] = (cot_ref[0, :, cols].astype(F32) + back).astype(BF16)


def piece_kernel(norm, share, got_ref, out_ref):
    first = lax.axis_index("core") * 8
    sources = got_ref.shape[0] // PIECE
    total = got_ref[0:ROWS, :]
    for s in range(1, sources):
        total = total + got_ref[s * PIECE : s * PIECE + ROWS, :]
    terms = got_ref[pl.ds(ROWS, sources, stride=PIECE), :]
    logs = jnp.sum(got_ref[pl.ds(ROWS + 1, sources, stride=PIECE), :], axis=0, keepdims=True)
    star = jnp.broadcast_to(terms[:, share : share + 1], terms.shape)
    hits = [star == (first + k).astype(F32) for k in range(8)]
    stars = [jnp.sum(jnp.where(hit, terms, 0.0), axis=0, keepdims=True) for hit in hits]
    total = total * norm
    tail = jnp.concatenate(stars + [logs], axis=0) * norm
    for d in range(out_ref.shape[0] // SHARE):
        out_ref[d * SHARE : d * SHARE + ROWS, :] = total
        out_ref[d * SHARE + ROWS : (d + 1) * SHARE, :] = tail


def final_kernel(got_ref, weight_ref, star_ref, log_ref):
    share = star_ref.shape[1]
    chips = got_ref.shape[0] // SHARE // 2
    for core in range(2):
        parts = [(core * chips + chip) * SHARE for chip in range(chips)]
        total = got_ref[parts[0] : parts[0] + SHARE, :]
        for at in parts[1:]:
            total = total + got_ref[at : at + SHARE, :]
        weight_ref[core * ROWS : (core + 1) * ROWS, :] = total[0:ROWS, :]
        star_ref[core * 8 : core * 8 + 8, :] = total[ROWS : ROWS + 8, 0:share]
        if core == 0:
            log_ref[...] = total[ROWS + 8 : ROWS + 9, 0:share]


def body(series, cotangent, step_times, seg_starts, star_of_row, block_weight, star_table, log_rate):
    _, slab_len, width = series.shape
    blocks = width // LANES
    slabs = lax.axis_size(("yh", "yl", "zh", "core"))
    rows_dp = lax.axis_size(("x", "zl"))
    norm = float(1.0 / (rows_dp * slabs * slab_len) ** 0.5)
    chips = slabs // 2
    log_blocks = log_rate.reshape(blocks, LANES)
    gain = jnp.sqrt(-jnp.expm1(-2.0 * jnp.exp(log_blocks)))
    smem = pl.BlockSpec(memory_space=pltpu.SMEM)
    vmem = pl.BlockSpec(memory_space=pltpu.VMEM)
    hbm = pl.BlockSpec(memory_space=pl.ANY)
    params = pltpu.CompilerParams(vmem_limit_bytes=24 * 1024 * 1024)
    big = pltpu.CompilerParams(vmem_limit_bytes=60 * 1024 * 1024)
    shape = jax.ShapeDtypeStruct
    common = (seg_starts, star_of_row, step_times, series, cotangent, block_weight, star_table, log_blocks)
    ends = pl.pallas_call(
        functools.partial(ends_kernel, blocks, chips),
        out_shape=shape((chips * CARRY, LANES), F32),
        in_specs=[hbm] * 8,
        out_specs=vmem,
        scratch_shapes=[pltpu.VMEM((2, 32, LANES), F32)]
        + [pltpu.SMEM(v.shape, v.dtype) for v in common[:2]]
        + [pltpu.VMEM(v.shape, v.dtype) for v in common[2:]]
        + [pltpu.SemaphoreType.DMA((5,)), pltpu.SemaphoreType.DMA((3,))],
        compiler_params=big,
        name="slab_ends",
    )(*common)
    ends = ends.reshape(chips, 1, CARRY * LANES)
    got = lax.all_gather(lax.all_to_all(ends, ("zh", "yh", "yl"), 0, 0), "core").reshape(slabs * CARRY, LANES)
    base, xt, sums, reach = pl.pallas_call(
        functools.partial(local_kernel, blocks),
        out_shape=[
            shape((width, slab_len), F32),
            shape((width, slab_len), BF16),
            shape((12, 16, LANES), F32),
            shape((2, slab_len, LANES), F32),
        ],
        in_specs=[smem, smem] + [vmem] * 7,
        out_specs=[vmem] * 4,
        compiler_params=params,
        cost_estimate=pl.CostEstimate(flops=20_000_000, bytes_accessed=4_000_000, transcendentals=200_000),
        name="local_scans",
    )(*common, gain)
    half_rows = width // 2 + 32
    low, keep, send = pl.pallas_call(
        functools.partial(combine_kernel, blocks, slabs, rows_dp),
        out_shape=[shape((width, slab_len), BF16)] + [shape((half_rows, LANES), F32)] * 2,
        in_specs=[vmem] * 7,
        out_specs=[vmem] * 3,
        scratch_shapes=[pltpu.VMEM((2, half_rows, LANES), F32)],
        compiler_params=params,
        name="gradients",
    )(log_blocks, gain, got, sums, base, xt, reach)
    sent = lax.all_gather(send, "core")
    pair = pl.pallas_call(
        functools.partial(pair_kernel, rows_dp),
        out_shape=shape((rows_dp * PIECE, LANES), F32),
        in_specs=[smem, vmem, vmem],
        out_specs=vmem,
        scratch_shapes=[pltpu.VMEM((8, width + LANES), F32)],
        compiler_params=params,
        name="pair_sum",
    )(star_of_row, keep, sent)
    grad_series = pl.pallas_call(
        functools.partial(series_kernel, blocks),
        out_shape=shape(series.shape, BF16),
        in_specs=[vmem] * 3,
        out_specs=vmem,
        compiler_params=params,
        cost_estimate=pl.CostEstimate(flops=100_000_000, bytes_accessed=1_600_000, transcendentals=0),
        name="series_gradient",
    )(low, cotangent, block_weight)
    pair = pair.reshape(rows_dp, 1, PIECE * LANES)
    pieces = lax.all_to_all(pair, ("x", "zl"), 0, 0).reshape(rows_dp * PIECE, LANES)
    piece = pl.pallas_call(
        functools.partial(piece_kernel, norm, width // rows_dp),
        out_shape=shape((chips * SHARE, LANES), F32),
        in_specs=[vmem],
        out_specs=vmem,
        compiler_params=params,
        name="sum_pieces",
    )(pieces)
    spread = lax.all_to_all(piece.reshape(chips, 1, SHARE * LANES), ("zh", "yh", "yl"), 0, 0)
    both = lax.all_gather(spread, "core").reshape(slabs * SHARE, LANES)
    share = width // rows_dp
    grad_weight, grad_star, grad_log = pl.pallas_call(
        final_kernel,
        out_shape=[
            jax.ShapeDtypeStruct((share, LANES), F32),
            jax.ShapeDtypeStruct((star_table.shape[0], share), F32),
            jax.ShapeDtypeStruct((1, share), F32),
        ],
        in_specs=[vmem],
        out_specs=[vmem] * 3,
        compiler_params=params,
        name="outputs",
    )(both)
    return grad_series, grad_weight, grad_star, grad_log.reshape(share)


def solution(mesh):
    fine = Mesh(mesh.devices.reshape(4, 4, 4, 2, 2, 2), ("x", "zl", "yh", "yl", "zh", "core"))
    dp, ctx = ("x", "zl"), ("yh", "yl", "zh", "core")
    in_specs = (P(dp, ctx, None), P(dp, ctx, None), P(dp, ctx), P(dp, None), P(dp), P(), P(), P())
    out_specs = (P(dp, ctx, None), P(dp, None), P(None, dp), P(dp))
    return jax.shard_map(body, mesh=fine, in_specs=in_specs, out_specs=out_specs, check_vma=False)
```

```python
import functools
import jax
import jax.numpy as jnp
from jax import lax
from jax.experimental import pallas as pl
from jax.experimental.pallas import tpu as pltpu
from jax.sharding import Mesh, PartitionSpec as P

SLAB = 128
LANES = 128
CHUNKS = 8
STEPS = SLAB // CHUNKS
FAR = 1e9
CARRY = 25
SHARE = 28
PIECE = 26
F32 = jnp.float32
BF16 = jnp.bfloat16


def slab_index():
    chip = (lax.axis_index("yh") * 2 + lax.axis_index("yl")) * 2 + lax.axis_index("zh")
    return chip * 2 + lax.axis_index("core")


def chip_slot(chip, chips):
    return chip % 2 * (chips // 2) + chip // 2


def elapsed_row(starts_ref, times_ref, me):
    position = lax.broadcasted_iota(jnp.int32, (1, SLAB), 1) + me * SLAB
    reset = position == starts_ref[0, 0]
    for k in range(1, starts_ref.shape[1]):
        reset = jnp.logical_or(reset, position == starts_ref[0, k])
    return jnp.where(reset, FAR, times_ref[...])


def ends_kernel(
    blocks, chips, star_ref, starts_hbm, times_hbm, series_hbm, cot_hbm, w_hbm, table_hbm, lograte_hbm,
    out_ref, ends_ref, starts_ref, times_ref, series_ref, cot_ref, w_ref, table_ref, lograte_ref, sems, load_sems,
):
    sources = (starts_hbm, times_hbm, table_hbm.at[pl.ds(star_ref[0], 1)], lograte_hbm)
    targets = (starts_ref, times_ref, table_ref, lograte_ref)
    copies = [pltpu.make_async_copy(a, b, sems.at[k]) for k, (a, b) in enumerate(zip(sources, targets))]
    sources, targets = (series_hbm, w_hbm, cot_hbm), (series_ref, w_ref, cot_ref)
    loads = [pltpu.make_async_copy(a, b, load_sems.at[k]) for k, (a, b) in enumerate(zip(sources, targets))]
    for copy in copies[:2] + loads + copies[2:]:
        copy.start()
    core = lax.axis_index("core")
    me = slab_index()
    for copy in copies[:2]:
        copy.wait()
    elapsed = elapsed_row(starts_ref, times_ref, me)
    row = lax.broadcasted_iota(jnp.int32, (SLAB, SLAB), 0)
    lane = lax.broadcasted_iota(jnp.int32, (SLAB, SLAB), 1)
    spread = jnp.broadcast_to(elapsed, (SLAB, SLAB))
    to_end = jnp.sum(jnp.where(lane > row, spread, 0.0), axis=1, keepdims=True)
    from_start = jnp.sum(jnp.where(lane <= row, spread, 0.0), axis=1, keepdims=True)
    to_end = jnp.broadcast_to(to_end, (SLAB, LANES))
    from_start = jnp.broadcast_to(from_start, (SLAB, LANES))
    total = jnp.sum(elapsed, axis=1, keepdims=True)
    for copy in copies[2:] + loads:
        copy.wait()
    bias = table_ref[...]
    for h in range(blocks):
        cols = slice(h * LANES, (h + 1) * LANES)
        proj = jnp.dot(series_ref[0, :, cols], w_ref[cols, :], preferred_element_type=F32) + bias[:, cols]
        grad = cot_ref[0, :, cols].astype(F32)
        slope = -jnp.exp(lograte_ref[h : h + 1, :])
        late = jnp.exp(slope * to_end)
        early = jnp.exp(slope * from_start)
        ends_ref[0, h : h + 1, :] = jnp.sum(late * proj, axis=0, keepdims=True)
        ends_ref[0, blocks + h : blocks + h + 1, :] = jnp.sum(late * grad, axis=0, keepdims=True)
        ends_ref[1, h : h + 1, :] = jnp.sum(early * proj, axis=0, keepdims=True)
        ends_ref[1, blocks + h : blocks + h + 1, :] = jnp.sum(early * grad, axis=0, keepdims=True)
    tail = jnp.broadcast_to(total, (8, LANES))
    ends_ref[0, 2 * blocks : 2 * blocks + 8, :] = tail
    ends_ref[1, 2 * blocks : 2 * blocks + 8, :] = tail
    for chip in range(chips):
        at = chip_slot(chip, chips) * CARRY
        out_ref[at : at + CARRY, :] = ends_ref[jnp.where(2 * chip + 1 - core > me, 0, 1), 0:CARRY, :]


def shift(x, k, fill, sublane):
    if k > 0:
        return jnp.where(sublane < k, fill, pltpu.roll(x, k, 0))
    return jnp.where(sublane >= CHUNKS + k, fill, pltpu.roll(x, CHUNKS + k, 0))


def chunk_entries(ends, through, sublane, sign):
    for k in (1, 2, 4):
        ends = ends + through * shift(ends, sign * k, 0.0, sublane)
        through = through * shift(through, sign * k, 1.0, sublane)
    return shift(ends, sign, 0.0, sublane), shift(through, sign, 1.0, sublane)


def local_kernel(
    blocks, starts_ref, star_ref, times_ref, series_ref, cot_ref, w_ref, table_ref, lograte_ref, gain_ref,
    base_ref, xt_ref, table_sums_ref, reach_ref,
):
    me = slab_index()
    elapsed = elapsed_row(starts_ref, times_ref, me)
    row = lax.broadcasted_iota(jnp.int32, (SLAB, SLAB), 0)
    lane = lax.broadcasted_iota(jnp.int32, (SLAB, SLAB), 1)
    sublane = lax.broadcasted_iota(jnp.int32, (CHUNKS, LANES), 0)
    time_of_row = (row % CHUNKS) * STEPS + row // CHUNKS
    order = (lane == time_of_row).astype(F32).astype(BF16)
    gap = jnp.sum(jnp.where(lane == time_of_row, jnp.broadcast_to(elapsed, (SLAB, SLAB)), 0.0), axis=1, keepdims=True)
    gap = jnp.broadcast_to(gap, (SLAB, LANES))
    spread = jnp.broadcast_to(elapsed, (SLAB, SLAB))
    for k, mask in enumerate((lane <= time_of_row, lane > time_of_row)):
        reach = jnp.sum(jnp.where(mask, spread, 0.0), axis=1, keepdims=True)
        reach_ref[k] = jnp.broadcast_to(reach, (SLAB, LANES))
    bias = table_ref[pl.ds(star_ref[0], 1), :]
    for h in range(blocks):
        cols = slice(h * LANES, (h + 1) * LANES)
        rate = jnp.exp(lograte_ref[h : h + 1, :])
        gain = gain_ref[h : h + 1, :]
        x = jnp.dot(order, series_ref[0, :, cols], preferred_element_type=F32)
        xt_ref[cols, :] = x.T.astype(BF16)
        grad = jnp.dot(order, cot_ref[0, :, cols], preferred_element_type=F32)
        proj = jnp.dot(x.astype(BF16), w_ref[cols, :], preferred_element_type=F32) + bias[:, cols]
        drive = gain * proj
        decay = jnp.exp(-rate * gap)
        tiles = lambda v: [v[j * CHUNKS : (j + 1) * CHUNKS, :] for j in range(STEPS)]
        a, d, g, pr, dt = tiles(decay), tiles(drive), tiles(grad), tiles(proj), tiles(gap)
        zero = jnp.zeros((CHUNKS, LANES), F32)
        before_d, before_g, through = [zero], [zero], [a[0]]
        state_d, state_g = d[0], g[0]
        for j in range(1, STEPS):
            before_d.append(a[j] * state_d)
            before_g.append(a[j] * state_g)
            state_d = before_d[j] + d[j]
            state_g = before_g[j] + g[j]
            through.append(a[j] * through[j - 1])
        after_d, after_g, back = [None] * STEPS, [None] * STEPS, [None] * STEPS
        after_d[-1], after_g[-1], back[-1] = d[-1], g[-1], jnp.ones((CHUNKS, LANES), F32)
        for j in reversed(range(STEPS - 1)):
            after_d[j] = a[j + 1] * after_d[j + 1] + d[j]
            after_g[j] = a[j + 1] * after_g[j + 1] + g[j]
            back[j] = a[j + 1] * back[j + 1]
        enter_d, onto = chunk_entries(state_d, through[-1], sublane, 1)
        enter_g, _ = chunk_entries(state_g, through[-1], sublane, 1)
        leave_d, off = chunk_entries(a[0] * after_d[0], through[-1], sublane, -1)
        leave_g, _ = chunk_entries(a[0] * after_g[0], through[-1], sublane, -1)
        sums = [zero] * 12
        for j in range(STEPS):
            kept_d = before_d[j] + through[j] * enter_d
            kept_g = before_g[j] + through[j] * enter_g
            later_d = after_d[j] + back[j] * leave_d
            later_g = after_g[j] + back[j] * leave_g
            on, off_j = through[j] * onto, back[j] * off
            base = later_g + kept_g + g[j]
            rows = slice(h * LANES + j * CHUNKS, h * LANES + (j + 1) * CHUNKS)
            base_ref[rows, :] = gain * base
            dt_on, dt_off = dt[j] * on, dt[j] * off_j
            terms = (
                dt[j] * (later_g * kept_d + kept_g * later_d),
                dt_off * kept_d,
                dt_on * later_g,
                dt_on * off_j,
                dt_off * kept_g,
                dt_on * later_d,
                base,
                on,
                off_j,
                base * pr[j],
                on * pr[j],
                off_j * pr[j],
            )
            sums = [s + t for s, t in zip(sums, terms)]
        for k, v in enumerate(sums):
            table_sums_ref[k, h : h + 1, :] = jnp.sum(v, axis=0, keepdims=True)


def combine_kernel(
    blocks, slabs, rows_dp, lograte_ref, gain_ref, got_ref, sums_ref, base_ref, xt_ref, reach_ref,
    low_ref, keep_ref, send_ref, part_ref,
):
    half = blocks * LANES // 2
    me = slab_index()
    mine = lax.axis_index("core")
    slope = -jnp.exp(lograte_ref[...])
    slope2 = jnp.concatenate([slope, slope], axis=0)
    start = lambda s: (s % 2 * (slabs // 2) + chip_slot(s // 2, slabs // 2)) * CARRY
    took = lambda s: got_ref[start(s) + 2 * blocks : start(s) + 2 * blocks + 1, :]
    between = [None] * slabs
    run = jnp.zeros((1, LANES), F32)
    for s in reversed(range(slabs)):
        between[s] = run
        run = jnp.where(s < me, run + took(s), 0.0)
    run = jnp.zeros((1, LANES), F32)
    carry_early = jnp.zeros((2 * blocks, LANES), F32)
    carry_late = jnp.zeros((2 * blocks, LANES), F32)
    for s in range(slabs):
        x = jnp.exp(slope2 * jnp.where(s < me, between[s], run)) * got_ref[start(s) : start(s) + 2 * blocks, :]
        carry_early = carry_early + jnp.where(s < me, x, 0.0)
        carry_late = carry_late + jnp.where(s > me, x, 0.0)
        run = jnp.where(s > me, run + took(s), 0.0)
    gain = gain_ref[...]
    early_d, early_g = gain * carry_early[0:blocks], carry_early[blocks:]
    late_d, late_g = gain * carry_late[0:blocks], carry_late[blocks:]
    c = [sums_ref[k, 0:blocks, :] for k in range(12)]
    rate_sum = c[0] + late_g * c[1] + early_d * c[2] + (late_g * early_d + early_g * late_d) * c[3]
    rate_sum = rate_sum + late_d * c[4] + early_g * c[5]
    grad_sum = c[6] + early_g * c[7] + late_g * c[8]
    cross_sum = c[9] + early_g * c[10] + late_g * c[11]
    proj_sum = gain * grad_sum
    log_sum = jnp.exp(2.0 * slope) / gain * cross_sum - rate_sum
    log_sum = -slope * log_sum
    for core in range(2):
        part_ref[core, half : half + blocks, :] = proj_sum
        part_ref[core, half + 16 : half + 16 + blocks, :] = log_sum

    enter, leave = gain * early_g, gain * late_g
    from_start, to_end = reach_ref[0], reach_ref[1]
    for h in range(blocks):
        rows = slice(h * LANES, (h + 1) * LANES)
        row = slice(h, h + 1)
        low = base_ref[rows, :] + jnp.exp(slope[row] * from_start) * enter[row] + jnp.exp(slope[row] * to_end) * leave[row]
        low = low.astype(BF16)
        low_ref[rows, :] = low
        product = jnp.dot(xt_ref[rows, :], low, preferred_element_type=F32)
        for k in range(LANES // 8):
            piece, third = divmod(h * (LANES // 8) + k, 3)
            dp, quarter = divmod(piece, 4)
            core, yl = divmod(quarter, 2)
            at = (dp * 2 + yl) * 24 + third * 8
            part_ref[core, at : at + 8, :] = product[k * 8 : k * 8 + 8, :]
    keep_ref[...] = part_ref[mine]
    send_ref[...] = part_ref[1 - mine]


def pair_kernel(rows_dp, star_ref, keep_ref, sent_ref, out_ref, flat_ref):
    other = 1 - lax.axis_index("core")
    half = keep_ref.shape[0] - 32
    width = 2 * half
    share = width // rows_dp
    flat_ref[0:2, width:] = jnp.zeros((2, flat_ref.shape[1] - width), F32)
    for k in range(2):
        table = keep_ref[half + 16 * k : half + 16 * k + 16, :] + sent_ref[other, half + 16 * k : half + 16 * k + 16, :]
        for h in range(width // LANES):
            flat_ref[k : k + 1, h * LANES : (h + 1) * LANES] = table[h : h + 1, :]
    lane = lax.broadcasted_iota(jnp.int32, (2, LANES), 1)
    star = jnp.broadcast_to(star_ref[0].astype(F32), (2, LANES))
    for dp in range(rows_dp):
        tile = jnp.where(lane < share, flat_ref[0:2, dp * share : dp * share + LANES], star)
        for yl in range(2):
            piece = dp * 2 + yl
            rows = slice(piece * 24, piece * 24 + 24)
            at = piece * PIECE
            out_ref[at : at + 24, :] = keep_ref[rows, :] + sent_ref[other, rows, :]
            out_ref[at + 24 : at + 26, :] = tile


def series_kernel(blocks, low_ref, cot_ref, w_ref, dx_ref):
    row = lax.broadcasted_iota(jnp.int32, (SLAB, SLAB), 0)
    lane = lax.broadcasted_iota(jnp.int32, (SLAB, SLAB), 1)
    unorder = (row == (lane % CHUNKS) * STEPS + lane // CHUNKS).astype(F32).astype(BF16)
    for h in range(blocks):
        cols = slice(h * LANES, (h + 1) * LANES)
        low = jnp.dot(unorder, low_ref[cols, :], preferred_element_type=F32).astype(BF16)
        back = lax.dot_general(low, w_ref[cols, :], (((1,), (1,)), ((), ())), preferred_element_type=F32)
        dx_ref[0, :, cols] = (cot_ref[0, :, cols].astype(F32) + back).astype(BF16)


def piece_kernel(norm, share, got_ref, out_ref):
    first = (lax.axis_index("core") * 2 + lax.axis_index("yl")) * 4
    sources = got_ref.shape[0] // PIECE
    total = got_ref[0:24, :]
    for s in range(1, sources):
        total = total + got_ref[s * PIECE : s * PIECE + 24, :]
    terms = got_ref[pl.ds(24, sources, stride=PIECE), :]
    logs = jnp.sum(got_ref[pl.ds(25, sources, stride=PIECE), :], axis=0, keepdims=True)
    star = jnp.broadcast_to(terms[:, share : share + 1], terms.shape)
    hits = [star == (first + k).astype(F32) for k in range(4)]
    stars = [jnp.sum(jnp.where(hit, terms, 0.0), axis=0, keepdims=True) for hit in hits]
    total = total * norm
    lane = lax.broadcasted_iota(jnp.int32, (1, LANES), 1)
    spare = LANES - share
    stars = [jnp.where(lane < share, row, pltpu.roll(logs, (share - k * spare) % LANES, 1)) for k, row in enumerate(stars)]
    tail = jnp.concatenate(stars, axis=0) * norm
    for d in range(out_ref.shape[0] // SHARE):
        out_ref[d * SHARE : d * SHARE + 24, :] = total
        out_ref[d * SHARE + 24 : d * SHARE + 28, :] = tail


def final_kernel(got_ref, weight_ref, star_ref, log_ref):
    share = star_ref.shape[1]
    chips = got_ref.shape[0] // SHARE // 2
    for core in range(2):
        for yl in range(2):
            q = core * 2 + yl
            parts = [(core * chips + chip) * SHARE for chip in range(chips) if chip % 2 == yl]
            total = got_ref[parts[0] : parts[0] + SHARE, :]
            for at in parts[1:]:
                total = total + got_ref[at : at + SHARE, :]
            weight_ref[q * 24 : q * 24 + 24, :] = total[0:24, :]
            star_ref[q * 4 : q * 4 + 4, :] = total[24:28, 0:share]
            if q == 0:
                logs = total[24:25, :]
                lane = lax.broadcasted_iota(jnp.int32, (1, LANES), 1)
                spare = LANES - share
                for k in range(4):
                    row = pltpu.roll(total[24 + k : 25 + k, :], (k * spare - share) % LANES, 1)
                    logs = jnp.where(lane // spare == k, row, logs)
                log_ref[...] = logs[:, 0:share]


def body(series, cotangent, step_times, seg_starts, star_of_row, block_weight, star_table, log_rate):
    _, slab_len, width = series.shape
    blocks = width // LANES
    slabs = lax.axis_size(("yh", "yl", "zh", "core"))
    rows_dp = lax.axis_size(("x", "zl"))
    norm = float(1.0 / (rows_dp * slabs * slab_len) ** 0.5)
    chips = slabs // 2
    log_blocks = log_rate.reshape(blocks, LANES)
    gain = jnp.sqrt(-jnp.expm1(-2.0 * jnp.exp(log_blocks)))
    smem = pl.BlockSpec(memory_space=pltpu.SMEM)
    vmem = pl.BlockSpec(memory_space=pltpu.VMEM)
    hbm = pl.BlockSpec(memory_space=pl.ANY)
    params = pltpu.CompilerParams(vmem_limit_bytes=24 * 1024 * 1024)
    big = pltpu.CompilerParams(vmem_limit_bytes=60 * 1024 * 1024)
    shape = jax.ShapeDtypeStruct
    common = (seg_starts, star_of_row, step_times, series, cotangent, block_weight, star_table, log_blocks)
    ends = pl.pallas_call(
        functools.partial(ends_kernel, blocks, chips),
        out_shape=shape((chips * CARRY, LANES), F32),
        in_specs=[smem] + [hbm] * 7,
        out_specs=vmem,
        scratch_shapes=[pltpu.VMEM((2, 32, LANES), F32)]
        + [pltpu.SMEM(seg_starts.shape, jnp.int32)]
        + [pltpu.VMEM(v.shape, v.dtype) for v in (step_times, series, cotangent, block_weight)]
        + [pltpu.VMEM((1, width), F32), pltpu.VMEM(log_blocks.shape, F32)]
        + [pltpu.SemaphoreType.DMA((4,)), pltpu.SemaphoreType.DMA((3,))],
        compiler_params=big,
        name="slab_ends",
    )(star_of_row, seg_starts, *common[2:])
    ends = ends.reshape(chips, 1, CARRY * LANES)
    got = lax.all_gather(lax.all_to_all(ends, ("zh", "yh", "yl"), 0, 0), "core").reshape(slabs * CARRY, LANES)
    base, xt, sums, reach = pl.pallas_call(
        functools.partial(local_kernel, blocks),
        out_shape=[
            shape((width, slab_len), F32),
            shape((width, slab_len), BF16),
            shape((12, 16, LANES), F32),
            shape((2, slab_len, LANES), F32),
        ],
        in_specs=[smem, smem] + [vmem] * 7,
        out_specs=[vmem] * 4,
        compiler_params=params,
        cost_estimate=pl.CostEstimate(flops=20_000_000, bytes_accessed=4_000_000, transcendentals=200_000),
        name="local_scans",
    )(*common, gain)
    half_rows = width // 2 + 32
    low, keep, send = pl.pallas_call(
        functools.partial(combine_kernel, blocks, slabs, rows_dp),
        out_shape=[shape((width, slab_len), BF16)] + [shape((half_rows, LANES), F32)] * 2,
        in_specs=[vmem] * 7,
        out_specs=[vmem] * 3,
        scratch_shapes=[pltpu.VMEM((2, half_rows, LANES), F32)],
        compiler_params=params,
        name="gradients",
    )(log_blocks, gain, got, sums, base, xt, reach)
    sent = lax.all_gather(send, "core")
    pair = pl.pallas_call(
        functools.partial(pair_kernel, rows_dp),
        out_shape=shape((rows_dp * 2 * PIECE, LANES), F32),
        in_specs=[smem, vmem, vmem],
        out_specs=vmem,
        scratch_shapes=[pltpu.VMEM((8, width + LANES), F32)],
        compiler_params=params,
        name="pair_sum",
    )(star_of_row, keep, sent)
    grad_series = pl.pallas_call(
        functools.partial(series_kernel, blocks),
        out_shape=shape(series.shape, BF16),
        in_specs=[vmem] * 3,
        out_specs=vmem,
        compiler_params=params,
        cost_estimate=pl.CostEstimate(flops=100_000_000, bytes_accessed=1_600_000, transcendentals=0),
        name="series_gradient",
    )(low, cotangent, block_weight)
    pair = pair.reshape(rows_dp * 2, 1, PIECE * LANES)
    pieces = lax.all_to_all(pair, ("x", "zl", "yl"), 0, 0).reshape(rows_dp * 2 * PIECE, LANES)
    piece = pl.pallas_call(
        functools.partial(piece_kernel, norm, width // rows_dp),
        out_shape=shape((chips * SHARE, LANES), F32),
        in_specs=[vmem],
        out_specs=vmem,
        compiler_params=params,
        name="sum_pieces",
    )(pieces)
    spread = lax.all_to_all(piece.reshape(chips, 1, SHARE * LANES), ("zh", "yh", "yl"), 0, 0)
    both = lax.all_gather(spread, "core").reshape(slabs * SHARE, LANES)
    share = width // rows_dp
    grad_weight, grad_star, grad_log = pl.pallas_call(
        final_kernel,
        out_shape=[
            jax.ShapeDtypeStruct((share, LANES), F32),
            jax.ShapeDtypeStruct((star_table.shape[0], share), F32),
            jax.ShapeDtypeStruct((1, share), F32),
        ],
        in_specs=[vmem],
        out_specs=[vmem] * 3,
        compiler_params=params,
        name="outputs",
    )(both)
    return grad_series, grad_weight, grad_star, grad_log.reshape(share)


def solution(mesh):
    fine = Mesh(mesh.devices.reshape(4, 4, 4, 2, 2, 2), ("x", "zl", "yh", "yl", "zh", "core"))
    dp, ctx = ("x", "zl"), ("yh", "yl", "zh", "core")
    in_specs = (P(dp, ctx, None), P(dp, ctx, None), P(dp, ctx), P(dp, None), P(dp), P(), P(), P())
    out_specs = (P(dp, ctx, None), P(dp, None), P(None, dp), P(dp))
    return jax.shard_map(body, mesh=fine, in_specs=in_specs, out_specs=out_specs, check_vma=False)
```

```python
import functools
import jax
import jax.numpy as jnp
from jax import lax
from jax.experimental import pallas as pl
from jax.experimental.pallas import tpu as pltpu
from jax.sharding import Mesh, PartitionSpec as P

SLAB = 128
LANES = 128
CHUNKS = 8
STEPS = SLAB // CHUNKS
FAR = 1e9
CARRY = 25
SHARE = 28
PIECE = 26
F32 = jnp.float32
BF16 = jnp.bfloat16


def slab_index():
    chip = (lax.axis_index("yh") * 2 + lax.axis_index("yl")) * 2 + lax.axis_index("zh")
    return chip * 2 + lax.axis_index("core")


def chip_slot(chip, chips):
    return chip % 2 * (chips // 2) + chip // 2


def elapsed_row(starts_ref, times_ref, me):
    position = lax.broadcasted_iota(jnp.int32, (1, SLAB), 1) + me * SLAB
    reset = position == starts_ref[0, 0]
    for k in range(1, starts_ref.shape[1]):
        reset = jnp.logical_or(reset, position == starts_ref[0, k])
    return jnp.where(reset, FAR, times_ref[...])


def ends_kernel(
    blocks, chips, star_ref, starts_hbm, times_hbm, series_hbm, cot_hbm, w_hbm, table_hbm, lograte_hbm,
    out_ref, ends_ref, starts_ref, times_ref, series_ref, cot_ref, w_ref, table_ref, lograte_ref, sems, load_sems,
):
    sources = (starts_hbm, times_hbm, table_hbm.at[pl.ds(star_ref[0], 1)], lograte_hbm)
    targets = (starts_ref, times_ref, table_ref, lograte_ref)
    copies = [pltpu.make_async_copy(a, b, sems.at[k]) for k, (a, b) in enumerate(zip(sources, targets))]
    sources, targets = (series_hbm, w_hbm, cot_hbm), (series_ref, w_ref, cot_ref)
    loads = [pltpu.make_async_copy(a, b, load_sems.at[k]) for k, (a, b) in enumerate(zip(sources, targets))]
    for copy in copies[:2] + loads + copies[2:]:
        copy.start()
    core = lax.axis_index("core")
    me = slab_index()
    for copy in copies[:2]:
        copy.wait()
    elapsed = elapsed_row(starts_ref, times_ref, me)
    row = lax.broadcasted_iota(jnp.int32, (SLAB, SLAB), 0)
    lane = lax.broadcasted_iota(jnp.int32, (SLAB, SLAB), 1)
    spread = jnp.broadcast_to(elapsed, (SLAB, SLAB))
    to_end = jnp.sum(jnp.where(lane > row, spread, 0.0), axis=1, keepdims=True)
    from_start = jnp.sum(jnp.where(lane <= row, spread, 0.0), axis=1, keepdims=True)
    to_end = jnp.broadcast_to(to_end, (SLAB, LANES))
    from_start = jnp.broadcast_to(from_start, (SLAB, LANES))
    total = jnp.sum(elapsed, axis=1, keepdims=True)
    for copy in copies[2:] + loads:
        copy.wait()
    bias = table_ref[...]
    for h in range(blocks):
        cols = slice(h * LANES, (h + 1) * LANES)
        proj = jnp.dot(series_ref[0, :, cols], w_ref[cols, :], preferred_element_type=F32) + bias[:, cols]
        grad = cot_ref[0, :, cols].astype(F32)
        slope = -jnp.exp(lograte_ref[h : h + 1, :])
        late = jnp.exp(slope * to_end)
        early = jnp.exp(slope * from_start)
        ends_ref[0, h : h + 1, :] = jnp.sum(late * proj, axis=0, keepdims=True)
        ends_ref[0, blocks + h : blocks + h + 1, :] = jnp.sum(late * grad, axis=0, keepdims=True)
        ends_ref[1, h : h + 1, :] = jnp.sum(early * proj, axis=0, keepdims=True)
        ends_ref[1, blocks + h : blocks + h + 1, :] = jnp.sum(early * grad, axis=0, keepdims=True)
    tail = jnp.broadcast_to(total, (8, LANES))
    ends_ref[0, 2 * blocks : 2 * blocks + 8, :] = tail
    ends_ref[1, 2 * blocks : 2 * blocks + 8, :] = tail
    for chip in range(chips):
        at = chip_slot(chip, chips) * CARRY
        out_ref[at : at + CARRY, :] = ends_ref[jnp.where(2 * chip + 1 - core > me, 0, 1), 0:CARRY, :]


def shift(x, k, fill, sublane):
    if k > 0:
        return jnp.where(sublane < k, fill, pltpu.roll(x, k, 0))
    return jnp.where(sublane >= CHUNKS + k, fill, pltpu.roll(x, CHUNKS + k, 0))


def chunk_entries(ends, through, sublane, sign):
    for k in (1, 2, 4):
        ends = ends + through * shift(ends, sign * k, 0.0, sublane)
        through = through * shift(through, sign * k, 1.0, sublane)
    return shift(ends, sign, 0.0, sublane), shift(through, sign, 1.0, sublane)


def local_kernel(
    blocks, starts_ref, star_ref, times_ref, series_ref, cot_ref, w_ref, table_ref, lograte_ref, gain_ref,
    base_ref, xt_ref, table_sums_ref, reach_ref,
):
    me = slab_index()
    elapsed = elapsed_row(starts_ref, times_ref, me)
    row = lax.broadcasted_iota(jnp.int32, (SLAB, SLAB), 0)
    lane = lax.broadcasted_iota(jnp.int32, (SLAB, SLAB), 1)
    sublane = lax.broadcasted_iota(jnp.int32, (CHUNKS, LANES), 0)
    time_of_row = (row % CHUNKS) * STEPS + row // CHUNKS
    order = (lane == time_of_row).astype(F32).astype(BF16)
    gap = jnp.sum(jnp.where(lane == time_of_row, jnp.broadcast_to(elapsed, (SLAB, SLAB)), 0.0), axis=1, keepdims=True)
    gap = jnp.broadcast_to(gap, (SLAB, LANES))
    spread = jnp.broadcast_to(elapsed, (SLAB, SLAB))
    for k, mask in enumerate((lane <= time_of_row, lane > time_of_row)):
        reach = jnp.sum(jnp.where(mask, spread, 0.0), axis=1, keepdims=True)
        reach_ref[k] = jnp.broadcast_to(reach, (SLAB, LANES))
    bias = table_ref[pl.ds(star_ref[0], 1), :]
    for h in range(blocks):
        cols = slice(h * LANES, (h + 1) * LANES)
        rate = jnp.exp(lograte_ref[h : h + 1, :])
        gain = gain_ref[h : h + 1, :]
        x = jnp.dot(order, series_ref[0, :, cols], preferred_element_type=F32)
        xt_ref[cols, :] = x.T.astype(BF16)
        grad = jnp.dot(order, cot_ref[0, :, cols], preferred_element_type=F32)
        proj = jnp.dot(x.astype(BF16), w_ref[cols, :], preferred_element_type=F32) + bias[:, cols]
        drive = gain * proj
        decay = jnp.exp(-rate * gap)
        tiles = lambda v: [v[j * CHUNKS : (j + 1) * CHUNKS, :] for j in range(STEPS)]
        a, d, g, pr, dt = tiles(decay), tiles(drive), tiles(grad), tiles(proj), tiles(gap)
        zero = jnp.zeros((CHUNKS, LANES), F32)
        before_d, before_g, through = [zero], [zero], [a[0]]
        state_d, state_g = d[0], g[0]
        for j in range(1, STEPS):
            before_d.append(a[j] * state_d)
            before_g.append(a[j] * state_g)
            state_d = before_d[j] + d[j]
            state_g = before_g[j] + g[j]
            through.append(a[j] * through[j - 1])
        after_d, after_g, back = [None] * STEPS, [None] * STEPS, [None] * STEPS
        after_d[-1], after_g[-1], back[-1] = d[-1], g[-1], jnp.ones((CHUNKS, LANES), F32)
        for j in reversed(range(STEPS - 1)):
            after_d[j] = a[j + 1] * after_d[j + 1] + d[j]
            after_g[j] = a[j + 1] * after_g[j + 1] + g[j]
            back[j] = a[j + 1] * back[j + 1]
        enter_d, onto = chunk_entries(state_d, through[-1], sublane, 1)
        enter_g, _ = chunk_entries(state_g, through[-1], sublane, 1)
        leave_d, off = chunk_entries(a[0] * after_d[0], through[-1], sublane, -1)
        leave_g, _ = chunk_entries(a[0] * after_g[0], through[-1], sublane, -1)
        sums = [zero] * 12
        for j in range(STEPS):
            kept_d = before_d[j] + through[j] * enter_d
            kept_g = before_g[j] + through[j] * enter_g
            later_d = after_d[j] + back[j] * leave_d
            later_g = after_g[j] + back[j] * leave_g
            on, off_j = through[j] * onto, back[j] * off
            base = later_g + kept_g + g[j]
            rows = slice(h * LANES + j * CHUNKS, h * LANES + (j + 1) * CHUNKS)
            base_ref[rows, :] = gain * base
            dt_on, dt_off = dt[j] * on, dt[j] * off_j
            terms = (
                dt[j] * (later_g * kept_d + kept_g * later_d),
                dt_off * kept_d,
                dt_on * later_g,
                dt_on * off_j,
                dt_off * kept_g,
                dt_on * later_d,
                base,
                on,
                off_j,
                base * pr[j],
                on * pr[j],
                off_j * pr[j],
            )
            sums = [s + t for s, t in zip(sums, terms)]
        for k, v in enumerate(sums):
            table_sums_ref[k, h : h + 1, :] = jnp.sum(v, axis=0, keepdims=True)


def combine_kernel(
    blocks, slabs, rows_dp, lograte_ref, gain_ref, got_ref, sums_ref, base_ref, xt_ref, reach_ref,
    low_ref, keep_ref, send_ref, part_ref,
):
    half = blocks * LANES // 2
    me = slab_index()
    mine = lax.axis_index("core")
    slope = -jnp.exp(lograte_ref[...])
    slope2 = jnp.concatenate([slope, slope], axis=0)
    start = lambda s: (s % 2 * (slabs // 2) + chip_slot(s // 2, slabs // 2)) * CARRY
    took = lambda s: got_ref[start(s) + 2 * blocks : start(s) + 2 * blocks + 1, :]
    between = [None] * slabs
    run = jnp.zeros((1, LANES), F32)
    for s in reversed(range(slabs)):
        between[s] = run
        run = jnp.where(s < me, run + took(s), 0.0)
    run = jnp.zeros((1, LANES), F32)
    carry_early = jnp.zeros((2 * blocks, LANES), F32)
    carry_late = jnp.zeros((2 * blocks, LANES), F32)
    for s in range(slabs):
        x = jnp.exp(slope2 * jnp.where(s < me, between[s], run)) * got_ref[start(s) : start(s) + 2 * blocks, :]
        carry_early = carry_early + jnp.where(s < me, x, 0.0)
        carry_late = carry_late + jnp.where(s > me, x, 0.0)
        run = jnp.where(s > me, run + took(s), 0.0)
    gain = gain_ref[...]
    early_d, early_g = gain * carry_early[0:blocks], carry_early[blocks:]
    late_d, late_g = gain * carry_late[0:blocks], carry_late[blocks:]
    c = [sums_ref[k, 0:blocks, :] for k in range(12)]
    rate_sum = c[0] + late_g * c[1] + early_d * c[2] + (late_g * early_d + early_g * late_d) * c[3]
    rate_sum = rate_sum + late_d * c[4] + early_g * c[5]
    grad_sum = c[6] + early_g * c[7] + late_g * c[8]
    cross_sum = c[9] + early_g * c[10] + late_g * c[11]
    proj_sum = gain * grad_sum
    log_sum = jnp.exp(2.0 * slope) / gain * cross_sum - rate_sum
    log_sum = -slope * log_sum
    for core in range(2):
        part_ref[core, half : half + blocks, :] = proj_sum
        part_ref[core, half + 16 : half + 16 + blocks, :] = log_sum

    enter, leave = gain * early_g, gain * late_g
    from_start, to_end = reach_ref[0], reach_ref[1]
    for h in range(blocks):
        rows = slice(h * LANES, (h + 1) * LANES)
        row = slice(h, h + 1)
        low = base_ref[rows, :] + jnp.exp(slope[row] * from_start) * enter[row] + jnp.exp(slope[row] * to_end) * leave[row]
        low = low.astype(BF16)
        low_ref[rows, :] = low
        product = jnp.dot(xt_ref[rows, :], low, preferred_element_type=F32)
        for k in range(LANES // 8):
            piece, third = divmod(h * (LANES // 8) + k, 3)
            dp, quarter = divmod(piece, 4)
            core, yl = divmod(quarter, 2)
            at = (dp * 2 + yl) * 24 + third * 8
            part_ref[core, at : at + 8, :] = product[k * 8 : k * 8 + 8, :]
    keep_ref[...] = part_ref[mine]
    send_ref[...] = part_ref[1 - mine]


def pair_kernel(rows_dp, star_ref, keep_ref, sent_ref, out_ref, flat_ref):
    other = 1 - lax.axis_index("core")
    half = keep_ref.shape[0] - 32
    width = 2 * half
    share = width // rows_dp
    flat_ref[0:2, width:] = jnp.zeros((2, flat_ref.shape[1] - width), F32)
    for k in range(2):
        table = keep_ref[half + 16 * k : half + 16 * k + 16, :] + sent_ref[other, half + 16 * k : half + 16 * k + 16, :]
        for h in range(width // LANES):
            flat_ref[k : k + 1, h * LANES : (h + 1) * LANES] = table[h : h + 1, :]
    lane = lax.broadcasted_iota(jnp.int32, (2, LANES), 1)
    star = jnp.broadcast_to(star_ref[0].astype(F32), (2, LANES))
    for dp in range(rows_dp):
        tile = jnp.where(lane < share, flat_ref[0:2, dp * share : dp * share + LANES], star)
        for yl in range(2):
            piece = dp * 2 + yl
            rows = slice(piece * 24, piece * 24 + 24)
            at = piece * PIECE
            out_ref[at : at + 24, :] = keep_ref[rows, :] + sent_ref[other, rows, :]
            out_ref[at + 24 : at + 26, :] = tile


def series_kernel(blocks, low_ref, cot_ref, w_ref, dx_ref):
    row = lax.broadcasted_iota(jnp.int32, (SLAB, SLAB), 0)
    lane = lax.broadcasted_iota(jnp.int32, (SLAB, SLAB), 1)
    unorder = (row == (lane % CHUNKS) * STEPS + lane // CHUNKS).astype(F32).astype(BF16)
    for h in range(blocks):
        cols = slice(h * LANES, (h + 1) * LANES)
        low = jnp.dot(unorder, low_ref[cols, :], preferred_element_type=F32).astype(BF16)
        back = lax.dot_general(low, w_ref[cols, :], (((1,), (1,)), ((), ())), preferred_element_type=F32)
        dx_ref[0, :, cols] = (cot_ref[0, :, cols].astype(F32) + back).astype(BF16)


def piece_kernel(norm, share, got_ref, out_ref):
    first = (lax.axis_index("core") * 2 + lax.axis_index("yl")) * 4
    sources = got_ref.shape[0] // PIECE
    total = got_ref[0:24, :]
    for s in range(1, sources):
        total = total + got_ref[s * PIECE : s * PIECE + 24, :]
    terms = got_ref[pl.ds(24, sources, stride=PIECE), :]
    logs = jnp.sum(got_ref[pl.ds(25, sources, stride=PIECE), :], axis=0, keepdims=True)
    star = jnp.broadcast_to(terms[:, share : share + 1], terms.shape)
    hits = [star == (first + k).astype(F32) for k in range(4)]
    stars = [jnp.sum(jnp.where(hit, terms, 0.0), axis=0, keepdims=True) for hit in hits]
    total = total * norm
    lane = lax.broadcasted_iota(jnp.int32, (1, LANES), 1)
    spare = LANES - share
    stars = [jnp.where(lane < share, row, pltpu.roll(logs, (share - k * spare) % LANES, 1)) for k, row in enumerate(stars)]
    tail = jnp.concatenate(stars, axis=0) * norm
    for d in range(out_ref.shape[0] // SHARE):
        out_ref[d * SHARE : d * SHARE + 24, :] = total
        out_ref[d * SHARE + 24 : d * SHARE + 28, :] = tail


def final_kernel(got_ref, weight_ref, star_ref, log_ref):
    share = star_ref.shape[1]
    chips = got_ref.shape[0] // SHARE // 2
    for core in range(2):
        for yl in range(2):
            q = core * 2 + yl
            parts = [(core * chips + chip) * SHARE for chip in range(chips) if chip % 2 == yl]
            total = got_ref[parts[0] : parts[0] + SHARE, :]
            for at in parts[1:]:
                total = total + got_ref[at : at + SHARE, :]
            weight_ref[q * 24 : q * 24 + 24, :] = total[0:24, :]
            star_ref[q * 4 : q * 4 + 4, :] = total[24:28, 0:share]
            if q == 0:
                logs = total[24:25, :]
                lane = lax.broadcasted_iota(jnp.int32, (1, LANES), 1)
                spare = LANES - share
                for k in range(4):
                    row = pltpu.roll(total[24 + k : 25 + k, :], (k * spare - share) % LANES, 1)
                    logs = jnp.where(lane // spare == k, row, logs)
                log_ref[...] = logs[:, 0:share]


def body(series, cotangent, step_times, seg_starts, star_of_row, block_weight, star_table, log_rate):
    _, slab_len, width = series.shape
    blocks = width // LANES
    slabs = lax.axis_size(("yh", "yl", "zh", "core"))
    rows_dp = lax.axis_size(("x", "zl"))
    norm = float(1.0 / (rows_dp * slabs * slab_len) ** 0.5)
    chips = slabs // 2
    log_blocks = log_rate.reshape(blocks, LANES)
    gain = jnp.sqrt(-jnp.expm1(-2.0 * jnp.exp(log_blocks)))
    smem = pl.BlockSpec(memory_space=pltpu.SMEM)
    vmem = pl.BlockSpec(memory_space=pltpu.VMEM)
    hbm = pl.BlockSpec(memory_space=pl.ANY)
    params = pltpu.CompilerParams(vmem_limit_bytes=24 * 1024 * 1024)
    big = pltpu.CompilerParams(vmem_limit_bytes=60 * 1024 * 1024)
    shape = jax.ShapeDtypeStruct
    common = (seg_starts, star_of_row, step_times, series, cotangent, block_weight, star_table, log_blocks)
    ends = pl.pallas_call(
        functools.partial(ends_kernel, blocks, chips),
        out_shape=shape((chips * CARRY, LANES), F32),
        in_specs=[smem] + [hbm] * 7,
        out_specs=vmem,
        scratch_shapes=[pltpu.VMEM((2, 32, LANES), F32)]
        + [pltpu.SMEM(seg_starts.shape, jnp.int32)]
        + [pltpu.VMEM(v.shape, v.dtype) for v in (step_times, series, cotangent, block_weight)]
        + [pltpu.VMEM((1, width), F32), pltpu.VMEM(log_blocks.shape, F32)]
        + [pltpu.SemaphoreType.DMA((4,)), pltpu.SemaphoreType.DMA((3,))],
        compiler_params=big,
        name="slab_ends",
    )(star_of_row, seg_starts, *common[2:])
    ends = ends.reshape(chips, 1, CARRY * LANES)
    got = lax.all_gather(lax.all_to_all(ends, ("zh", "yh", "yl"), 0, 0), "core").reshape(slabs * CARRY, LANES)
    base, xt, sums, reach = pl.pallas_call(
        functools.partial(local_kernel, blocks),
        out_shape=[
            shape((width, slab_len), F32),
            shape((width, slab_len), BF16),
            shape((12, 16, LANES), F32),
            shape((2, slab_len, LANES), F32),
        ],
        in_specs=[smem, smem] + [vmem] * 7,
        out_specs=[vmem] * 4,
        compiler_params=params,
        cost_estimate=pl.CostEstimate(flops=20_000_000, bytes_accessed=4_000_000, transcendentals=200_000),
        name="local_scans",
    )(*common, gain)
    half_rows = width // 2 + 32
    low, keep, send = pl.pallas_call(
        functools.partial(combine_kernel, blocks, slabs, rows_dp),
        out_shape=[shape((width, slab_len), BF16)] + [shape((half_rows, LANES), F32)] * 2,
        in_specs=[vmem] * 7,
        out_specs=[vmem] * 3,
        scratch_shapes=[pltpu.VMEM((2, half_rows, LANES), F32)],
        compiler_params=params,
        name="gradients",
    )(log_blocks, gain, got, sums, base, xt, reach)
    sent = lax.all_gather(send, "core")
    pair = pl.pallas_call(
        functools.partial(pair_kernel, rows_dp),
        out_shape=shape((rows_dp * 2 * PIECE, LANES), F32),
        in_specs=[smem, vmem, vmem],
        out_specs=vmem,
        scratch_shapes=[pltpu.VMEM((8, width + LANES), F32)],
        compiler_params=params,
        name="pair_sum",
    )(star_of_row, keep, sent)
    grad_series = pl.pallas_call(
        functools.partial(series_kernel, blocks),
        out_shape=shape(series.shape, BF16),
        in_specs=[vmem] * 3,
        out_specs=vmem,
        compiler_params=params,
        cost_estimate=pl.CostEstimate(flops=100_000_000, bytes_accessed=1_600_000, transcendentals=0),
        name="series_gradient",
    )(low, cotangent, block_weight)
    pair = pair.reshape(rows_dp * 2, 1, PIECE * LANES)
    pieces = lax.all_to_all(pair, ("x", "zl", "yl"), 0, 0).reshape(rows_dp * 2 * PIECE, LANES)
    pieces, grad_series = lax.optimization_barrier((pieces, grad_series))
    piece = pl.pallas_call(
        functools.partial(piece_kernel, norm, width // rows_dp),
        out_shape=shape((chips * SHARE, LANES), F32),
        in_specs=[vmem],
        out_specs=vmem,
        compiler_params=params,
        name="sum_pieces",
    )(pieces)
    spread = lax.all_to_all(piece.reshape(chips, 1, SHARE * LANES), ("zh", "yh", "yl"), 0, 0)
    both = lax.all_gather(spread, "core").reshape(slabs * SHARE, LANES)
    share = width // rows_dp
    grad_weight, grad_star, grad_log = pl.pallas_call(
        final_kernel,
        out_shape=[
            jax.ShapeDtypeStruct((share, LANES), F32),
            jax.ShapeDtypeStruct((star_table.shape[0], share), F32),
            jax.ShapeDtypeStruct((1, share), F32),
        ],
        in_specs=[vmem],
        out_specs=[vmem] * 3,
        compiler_params=params,
        name="outputs",
    )(both)
    return grad_series, grad_weight, grad_star, grad_log.reshape(share)


def solution(mesh):
    fine = Mesh(mesh.devices.reshape(4, 4, 4, 2, 2, 2), ("x", "zl", "yh", "yl", "zh", "core"))
    dp, ctx = ("x", "zl"), ("yh", "yl", "zh", "core")
    in_specs = (P(dp, ctx, None), P(dp, ctx, None), P(dp, ctx), P(dp, None), P(dp), P(), P(), P())
    out_specs = (P(dp, ctx, None), P(dp, None), P(None, dp), P(dp))
    return jax.shard_map(body, mesh=fine, in_specs=in_specs, out_specs=out_specs, check_vma=False)
```

```python
import functools
import jax
import jax.numpy as jnp
from jax import lax
from jax.experimental import pallas as pl
from jax.experimental.pallas import tpu as pltpu
from jax.sharding import Mesh, PartitionSpec as P

SLAB = 128
LANES = 128
CHUNKS = 8
STEPS = SLAB // CHUNKS
FAR = 1e9
CARRY = 25
SHARE = 28
PIECE = 26
F32 = jnp.float32
BF16 = jnp.bfloat16


def slab_index():
    chip = (lax.axis_index("yh") * 2 + lax.axis_index("yl")) * 2 + lax.axis_index("zh")
    return chip * 2 + lax.axis_index("core")


def chip_slot(chip, chips):
    return chip % 2 * (chips // 2) + chip // 2


def elapsed_row(starts_ref, times_ref, me):
    position = lax.broadcasted_iota(jnp.int32, (1, SLAB), 1) + me * SLAB
    reset = position == starts_ref[0, 0]
    for k in range(1, starts_ref.shape[1]):
        reset = jnp.logical_or(reset, position == starts_ref[0, k])
    return jnp.where(reset, FAR, times_ref[...])


def ends_kernel(
    blocks, chips, star_ref, starts_hbm, times_hbm, series_hbm, cot_hbm, w_hbm, table_hbm, lograte_hbm,
    out_ref, ends_ref, starts_ref, times_ref, series_ref, cot_ref, w_ref, table_ref, lograte_ref, sems, load_sems,
):
    sources = (starts_hbm, times_hbm, table_hbm.at[pl.ds(star_ref[0], 1)], lograte_hbm)
    targets = (starts_ref, times_ref, table_ref, lograte_ref)
    copies = [pltpu.make_async_copy(a, b, sems.at[k]) for k, (a, b) in enumerate(zip(sources, targets))]
    sources, targets = (series_hbm, w_hbm, cot_hbm), (series_ref, w_ref, cot_ref)
    loads = [pltpu.make_async_copy(a, b, load_sems.at[k]) for k, (a, b) in enumerate(zip(sources, targets))]
    for copy in copies[:2] + loads + copies[2:]:
        copy.start()
    core = lax.axis_index("core")
    me = slab_index()
    for copy in copies[:2]:
        copy.wait()
    elapsed = elapsed_row(starts_ref, times_ref, me)
    row = lax.broadcasted_iota(jnp.int32, (SLAB, SLAB), 0)
    lane = lax.broadcasted_iota(jnp.int32, (SLAB, SLAB), 1)
    spread = jnp.broadcast_to(elapsed, (SLAB, SLAB))
    to_end = jnp.sum(jnp.where(lane > row, spread, 0.0), axis=1, keepdims=True)
    from_start = jnp.sum(jnp.where(lane <= row, spread, 0.0), axis=1, keepdims=True)
    to_end = jnp.broadcast_to(to_end, (SLAB, LANES))
    from_start = jnp.broadcast_to(from_start, (SLAB, LANES))
    total = jnp.sum(elapsed, axis=1, keepdims=True)
    for copy in copies[2:] + loads:
        copy.wait()
    bias = table_ref[...]
    for h in range(blocks):
        cols = slice(h * LANES, (h + 1) * LANES)
        proj = jnp.dot(series_ref[0, :, cols], w_ref[cols, :], preferred_element_type=F32) + bias[:, cols]
        grad = cot_ref[0, :, cols].astype(F32)
        slope = -jnp.exp(lograte_ref[h : h + 1, :])
        late = jnp.exp(slope * to_end)
        early = jnp.exp(slope * from_start)
        ends_ref[0, h : h + 1, :] = jnp.sum(late * proj, axis=0, keepdims=True)
        ends_ref[0, blocks + h : blocks + h + 1, :] = jnp.sum(late * grad, axis=0, keepdims=True)
        ends_ref[1, h : h + 1, :] = jnp.sum(early * proj, axis=0, keepdims=True)
        ends_ref[1, blocks + h : blocks + h + 1, :] = jnp.sum(early * grad, axis=0, keepdims=True)
    tail = jnp.broadcast_to(total, (8, LANES))
    ends_ref[0, 2 * blocks : 2 * blocks + 8, :] = tail
    ends_ref[1, 2 * blocks : 2 * blocks + 8, :] = tail
    for chip in range(chips):
        at = chip_slot(chip, chips) * CARRY
        out_ref[at : at + CARRY, :] = ends_ref[jnp.where(2 * chip + 1 - core > me, 0, 1), 0:CARRY, :]


def shift(x, k, fill, sublane):
    if k > 0:
        return jnp.where(sublane < k, fill, pltpu.roll(x, k, 0))
    return jnp.where(sublane >= CHUNKS + k, fill, pltpu.roll(x, CHUNKS + k, 0))


def chunk_entries(ends, through, sublane, sign):
    for k in (1, 2, 4):
        ends = ends + through * shift(ends, sign * k, 0.0, sublane)
        through = through * shift(through, sign * k, 1.0, sublane)
    return shift(ends, sign, 0.0, sublane), shift(through, sign, 1.0, sublane)


def local_kernel(
    blocks, starts_ref, star_ref, times_ref, series_ref, cot_ref, w_ref, table_ref, lograte_ref, gain_ref,
    base_ref, xt_ref, table_sums_ref, reach_ref,
):
    me = slab_index()
    elapsed = elapsed_row(starts_ref, times_ref, me)
    row = lax.broadcasted_iota(jnp.int32, (SLAB, SLAB), 0)
    lane = lax.broadcasted_iota(jnp.int32, (SLAB, SLAB), 1)
    sublane = lax.broadcasted_iota(jnp.int32, (CHUNKS, LANES), 0)
    time_of_row = (row % CHUNKS) * STEPS + row // CHUNKS
    order = (lane == time_of_row).astype(F32).astype(BF16)
    gap = jnp.sum(jnp.where(lane == time_of_row, jnp.broadcast_to(elapsed, (SLAB, SLAB)), 0.0), axis=1, keepdims=True)
    gap = jnp.broadcast_to(gap, (SLAB, LANES))
    spread = jnp.broadcast_to(elapsed, (SLAB, SLAB))
    for k, mask in enumerate((lane <= time_of_row, lane > time_of_row)):
        reach = jnp.sum(jnp.where(mask, spread, 0.0), axis=1, keepdims=True)
        reach_ref[k] = jnp.broadcast_to(reach, (SLAB, LANES))
    bias = table_ref[pl.ds(star_ref[0], 1), :]
    for h in range(blocks):
        cols = slice(h * LANES, (h + 1) * LANES)
        rate = jnp.exp(lograte_ref[h : h + 1, :])
        gain = gain_ref[h : h + 1, :]
        x = jnp.dot(order, series_ref[0, :, cols], preferred_element_type=F32)
        xt_ref[cols, :] = x.T.astype(BF16)
        grad = jnp.dot(order, cot_ref[0, :, cols], preferred_element_type=F32)
        proj = jnp.dot(x.astype(BF16), w_ref[cols, :], preferred_element_type=F32) + bias[:, cols]
        drive = gain * proj
        decay = jnp.exp(-rate * gap)
        tiles = lambda v: [v[j * CHUNKS : (j + 1) * CHUNKS, :] for j in range(STEPS)]
        a, d, g, pr, dt = tiles(decay), tiles(drive), tiles(grad), tiles(proj), tiles(gap)
        zero = jnp.zeros((CHUNKS, LANES), F32)
        before_d, before_g, through = [zero], [zero], [a[0]]
        state_d, state_g = d[0], g[0]
        for j in range(1, STEPS):
            before_d.append(a[j] * state_d)
            before_g.append(a[j] * state_g)
            state_d = before_d[j] + d[j]
            state_g = before_g[j] + g[j]
            through.append(a[j] * through[j - 1])
        after_d, after_g, back = [None] * STEPS, [None] * STEPS, [None] * STEPS
        after_d[-1], after_g[-1], back[-1] = d[-1], g[-1], jnp.ones((CHUNKS, LANES), F32)
        for j in reversed(range(STEPS - 1)):
            after_d[j] = a[j + 1] * after_d[j + 1] + d[j]
            after_g[j] = a[j + 1] * after_g[j + 1] + g[j]
            back[j] = a[j + 1] * back[j + 1]
        enter_d, onto = chunk_entries(state_d, through[-1], sublane, 1)
        enter_g, _ = chunk_entries(state_g, through[-1], sublane, 1)
        leave_d, off = chunk_entries(a[0] * after_d[0], through[-1], sublane, -1)
        leave_g, _ = chunk_entries(a[0] * after_g[0], through[-1], sublane, -1)
        sums = [zero] * 12
        for j in range(STEPS):
            kept_d = before_d[j] + through[j] * enter_d
            kept_g = before_g[j] + through[j] * enter_g
            later_d = after_d[j] + back[j] * leave_d
            later_g = after_g[j] + back[j] * leave_g
            on, off_j = through[j] * onto, back[j] * off
            base = later_g + kept_g + g[j]
            rows = slice(h * LANES + j * CHUNKS, h * LANES + (j + 1) * CHUNKS)
            base_ref[rows, :] = gain * base
            dt_on, dt_off = dt[j] * on, dt[j] * off_j
            terms = (
                dt[j] * (later_g * kept_d + kept_g * later_d),
                dt_off * kept_d,
                dt_on * later_g,
                dt_on * off_j,
                dt_off * kept_g,
                dt_on * later_d,
                base,
                on,
                off_j,
                base * pr[j],
                on * pr[j],
                off_j * pr[j],
            )
            sums = [s + t for s, t in zip(sums, terms)]
        for k, v in enumerate(sums):
            table_sums_ref[k, h : h + 1, :] = jnp.sum(v, axis=0, keepdims=True)


def combine_kernel(
    blocks, slabs, rows_dp, lograte_ref, gain_ref, got_ref, sums_ref, base_ref, xt_ref, reach_ref,
    low_ref, keep_ref, send_ref, part_ref,
):
    half = blocks * LANES // 2
    me = slab_index()
    mine = lax.axis_index("core")
    slope = -jnp.exp(lograte_ref[...])
    slope2 = jnp.concatenate([slope, slope], axis=0)
    start = lambda s: (s % 2 * (slabs // 2) + chip_slot(s // 2, slabs // 2)) * CARRY
    took = lambda s: got_ref[start(s) + 2 * blocks : start(s) + 2 * blocks + 1, :]
    between = [None] * slabs
    run = jnp.zeros((1, LANES), F32)
    for s in reversed(range(slabs)):
        between[s] = run
        run = jnp.where(s < me, run + took(s), 0.0)
    run = jnp.zeros((1, LANES), F32)
    carry_early = jnp.zeros((2 * blocks, LANES), F32)
    carry_late = jnp.zeros((2 * blocks, LANES), F32)
    for s in range(slabs):
        x = jnp.exp(slope2 * jnp.where(s < me, between[s], run)) * got_ref[start(s) : start(s) + 2 * blocks, :]
        carry_early = carry_early + jnp.where(s < me, x, 0.0)
        carry_late = carry_late + jnp.where(s > me, x, 0.0)
        run = jnp.where(s > me, run + took(s), 0.0)
    gain = gain_ref[...]
    early_d, early_g = gain * carry_early[0:blocks], carry_early[blocks:]
    late_d, late_g = gain * carry_late[0:blocks], carry_late[blocks:]
    c = [sums_ref[k, 0:blocks, :] for k in range(12)]
    rate_sum = c[0] + late_g * c[1] + early_d * c[2] + (late_g * early_d + early_g * late_d) * c[3]
    rate_sum = rate_sum + late_d * c[4] + early_g * c[5]
    grad_sum = c[6] + early_g * c[7] + late_g * c[8]
    cross_sum = c[9] + early_g * c[10] + late_g * c[11]
    proj_sum = gain * grad_sum
    log_sum = jnp.exp(2.0 * slope) / gain * cross_sum - rate_sum
    log_sum = -slope * log_sum
    for core in range(2):
        part_ref[core, half : half + blocks, :] = proj_sum
        part_ref[core, half + 16 : half + 16 + blocks, :] = log_sum

    enter, leave = gain * early_g, gain * late_g
    from_start, to_end = reach_ref[0], reach_ref[1]
    for h in range(blocks):
        rows = slice(h * LANES, (h + 1) * LANES)
        row = slice(h, h + 1)
        low = base_ref[rows, :] + jnp.exp(slope[row] * from_start) * enter[row] + jnp.exp(slope[row] * to_end) * leave[row]
        low = low.astype(BF16)
        low_ref[rows, :] = low
        product = jnp.dot(xt_ref[rows, :], low, preferred_element_type=F32)
        for k in range(LANES // 8):
            piece, third = divmod(h * (LANES // 8) + k, 3)
            dp, quarter = divmod(piece, 4)
            core, yl = divmod(quarter, 2)
            at = (dp * 2 + yl) * 24 + third * 8
            part_ref[core, at : at + 8, :] = product[k * 8 : k * 8 + 8, :]
    keep_ref[...] = part_ref[mine]
    send_ref[...] = part_ref[1 - mine]


def pair_kernel(rows_dp, star_ref, keep_ref, sent_ref, out_ref, flat_ref):
    other = 1 - lax.axis_index("core")
    half = keep_ref.shape[0] - 32
    width = 2 * half
    share = width // rows_dp
    flat_ref[0:2, width:] = jnp.zeros((2, flat_ref.shape[1] - width), F32)
    for k in range(2):
        table = keep_ref[half + 16 * k : half + 16 * k + 16, :] + sent_ref[other, half + 16 * k : half + 16 * k + 16, :]
        for h in range(width // LANES):
            flat_ref[k : k + 1, h * LANES : (h + 1) * LANES] = table[h : h + 1, :]
    lane = lax.broadcasted_iota(jnp.int32, (2, LANES), 1)
    star = jnp.broadcast_to(star_ref[0].astype(F32), (2, LANES))
    for dp in range(rows_dp):
        tile = jnp.where(lane < share, flat_ref[0:2, dp * share : dp * share + LANES], star)
        for yl in range(2):
            piece = dp * 2 + yl
            rows = slice(piece * 24, piece * 24 + 24)
            at = piece * PIECE
            out_ref[at : at + 24, :] = keep_ref[rows, :] + sent_ref[other, rows, :]
            out_ref[at + 24 : at + 26, :] = tile


def series_kernel(blocks, low_ref, cot_ref, w_ref, dx_ref):
    row = lax.broadcasted_iota(jnp.int32, (SLAB, SLAB), 0)
    lane = lax.broadcasted_iota(jnp.int32, (SLAB, SLAB), 1)
    unorder = (row == (lane % CHUNKS) * STEPS + lane // CHUNKS).astype(F32).astype(BF16)
    for h in range(blocks):
        cols = slice(h * LANES, (h + 1) * LANES)
        low = jnp.dot(unorder, low_ref[cols, :], preferred_element_type=F32).astype(BF16)
        back = lax.dot_general(low, w_ref[cols, :], (((1,), (1,)), ((), ())), preferred_element_type=F32)
        dx_ref[0, :, cols] = (cot_ref[0, :, cols].astype(F32) + back).astype(BF16)


def piece_kernel(norm, share, got_ref, out_ref):
    first = (lax.axis_index("core") * 2 + lax.axis_index("yl")) * 4
    sources = got_ref.shape[0] // PIECE
    total = got_ref[0:24, :]
    for s in range(1, sources):
        total = total + got_ref[s * PIECE : s * PIECE + 24, :]
    terms = got_ref[pl.ds(24, sources, stride=PIECE), :]
    logs = jnp.sum(got_ref[pl.ds(25, sources, stride=PIECE), :], axis=0, keepdims=True)
    star = jnp.broadcast_to(terms[:, share : share + 1], terms.shape)
    hits = [star == (first + k).astype(F32) for k in range(4)]
    stars = [jnp.sum(jnp.where(hit, terms, 0.0), axis=0, keepdims=True) for hit in hits]
    total = total * norm
    lane = lax.broadcasted_iota(jnp.int32, (1, LANES), 1)
    spare = LANES - share
    stars = [jnp.where(lane < share, row, pltpu.roll(logs, (share - k * spare) % LANES, 1)) for k, row in enumerate(stars)]
    tail = jnp.concatenate(stars, axis=0) * norm
    for d in range(out_ref.shape[0] // SHARE):
        out_ref[d * SHARE : d * SHARE + 24, :] = total
        out_ref[d * SHARE + 24 : d * SHARE + 28, :] = tail


def final_kernel(got_ref, weight_ref, star_ref, log_ref):
    share = star_ref.shape[1]
    chips = got_ref.shape[0] // SHARE // 2
    for core in range(2):
        for yl in range(2):
            q = core * 2 + yl
            parts = [(core * chips + chip) * SHARE for chip in range(chips) if chip // 4 % 2 == yl]
            total = got_ref[parts[0] : parts[0] + SHARE, :]
            for at in parts[1:]:
                total = total + got_ref[at : at + SHARE, :]
            weight_ref[q * 24 : q * 24 + 24, :] = total[0:24, :]
            star_ref[q * 4 : q * 4 + 4, :] = total[24:28, 0:share]
            if q == 0:
                logs = total[24:25, :]
                lane = lax.broadcasted_iota(jnp.int32, (1, LANES), 1)
                spare = LANES - share
                for k in range(4):
                    row = pltpu.roll(total[24 + k : 25 + k, :], (k * spare - share) % LANES, 1)
                    logs = jnp.where(lane // spare == k, row, logs)
                log_ref[...] = logs[:, 0:share]


def body(series, cotangent, step_times, seg_starts, star_of_row, block_weight, star_table, log_rate):
    _, slab_len, width = series.shape
    blocks = width // LANES
    slabs = lax.axis_size(("yh", "yl", "zh", "core"))
    rows_dp = lax.axis_size(("x", "zl"))
    norm = float(1.0 / (rows_dp * slabs * slab_len) ** 0.5)
    chips = slabs // 2
    log_blocks = log_rate.reshape(blocks, LANES)
    gain = jnp.sqrt(-jnp.expm1(-2.0 * jnp.exp(log_blocks)))
    smem = pl.BlockSpec(memory_space=pltpu.SMEM)
    vmem = pl.BlockSpec(memory_space=pltpu.VMEM)
    hbm = pl.BlockSpec(memory_space=pl.ANY)
    params = pltpu.CompilerParams(vmem_limit_bytes=24 * 1024 * 1024)
    big = pltpu.CompilerParams(vmem_limit_bytes=60 * 1024 * 1024)
    shape = jax.ShapeDtypeStruct
    common = (seg_starts, star_of_row, step_times, series, cotangent, block_weight, star_table, log_blocks)
    ends = pl.pallas_call(
        functools.partial(ends_kernel, blocks, chips),
        out_shape=shape((chips * CARRY, LANES), F32),
        in_specs=[smem] + [hbm] * 7,
        out_specs=vmem,
        scratch_shapes=[pltpu.VMEM((2, 32, LANES), F32)]
        + [pltpu.SMEM(seg_starts.shape, jnp.int32)]
        + [pltpu.VMEM(v.shape, v.dtype) for v in (step_times, series, cotangent, block_weight)]
        + [pltpu.VMEM((1, width), F32), pltpu.VMEM(log_blocks.shape, F32)]
        + [pltpu.SemaphoreType.DMA((4,)), pltpu.SemaphoreType.DMA((3,))],
        compiler_params=big,
        name="slab_ends",
    )(star_of_row, seg_starts, *common[2:])
    ends = ends.reshape(chips, 1, CARRY * LANES)
    got = lax.all_gather(lax.all_to_all(ends, ("zh", "yh", "yl"), 0, 0), "core").reshape(slabs * CARRY, LANES)
    base, xt, sums, reach = pl.pallas_call(
        functools.partial(local_kernel, blocks),
        out_shape=[
            shape((width, slab_len), F32),
            shape((width, slab_len), BF16),
            shape((12, 16, LANES), F32),
            shape((2, slab_len, LANES), F32),
        ],
        in_specs=[smem, smem] + [vmem] * 7,
        out_specs=[vmem] * 4,
        compiler_params=params,
        cost_estimate=pl.CostEstimate(flops=20_000_000, bytes_accessed=4_000_000, transcendentals=200_000),
        name="local_scans",
    )(*common, gain)
    half_rows = width // 2 + 32
    low, keep, send = pl.pallas_call(
        functools.partial(combine_kernel, blocks, slabs, rows_dp),
        out_shape=[shape((width, slab_len), BF16)] + [shape((half_rows, LANES), F32)] * 2,
        in_specs=[vmem] * 7,
        out_specs=[vmem] * 3,
        scratch_shapes=[pltpu.VMEM((2, half_rows, LANES), F32)],
        compiler_params=params,
        name="gradients",
    )(log_blocks, gain, got, sums, base, xt, reach)
    sent = lax.all_gather(send, "core")
    pair = pl.pallas_call(
        functools.partial(pair_kernel, rows_dp),
        out_shape=shape((rows_dp * 2 * PIECE, LANES), F32),
        in_specs=[smem, vmem, vmem],
        out_specs=vmem,
        scratch_shapes=[pltpu.VMEM((8, width + LANES), F32)],
        compiler_params=params,
        name="pair_sum",
    )(star_of_row, keep, sent)
    grad_series = pl.pallas_call(
        functools.partial(series_kernel, blocks),
        out_shape=shape(series.shape, BF16),
        in_specs=[vmem] * 3,
        out_specs=vmem,
        compiler_params=params,
        cost_estimate=pl.CostEstimate(flops=100_000_000, bytes_accessed=1_600_000, transcendentals=0),
        name="series_gradient",
    )(low, cotangent, block_weight)
    pair = pair.reshape(rows_dp * 2, 1, PIECE * LANES)
    pieces = lax.all_to_all(pair, ("x", "zl", "yl"), 0, 0).reshape(rows_dp * 2 * PIECE, LANES)
    pieces, grad_series = lax.optimization_barrier((pieces, grad_series))
    piece = pl.pallas_call(
        functools.partial(piece_kernel, norm, width // rows_dp),
        out_shape=shape((chips * SHARE, LANES), F32),
        in_specs=[vmem],
        out_specs=vmem,
        compiler_params=params,
        name="sum_pieces",
    )(pieces)
    spread = lax.all_to_all(piece.reshape(chips, 1, SHARE * LANES), ("zh", "yl", "yh"), 0, 0)
    both = lax.all_gather(spread, "core").reshape(slabs * SHARE, LANES)
    share = width // rows_dp
    grad_weight, grad_star, grad_log = pl.pallas_call(
        final_kernel,
        out_shape=[
            jax.ShapeDtypeStruct((share, LANES), F32),
            jax.ShapeDtypeStruct((star_table.shape[0], share), F32),
            jax.ShapeDtypeStruct((1, share), F32),
        ],
        in_specs=[vmem],
        out_specs=[vmem] * 3,
        compiler_params=params,
        name="outputs",
    )(both)
    return grad_series, grad_weight, grad_star, grad_log.reshape(share)


def solution(mesh):
    fine = Mesh(mesh.devices.reshape(4, 4, 4, 2, 2, 2), ("x", "zl", "yh", "yl", "zh", "core"))
    dp, ctx = ("x", "zl"), ("yh", "yl", "zh", "core")
    in_specs = (P(dp, ctx, None), P(dp, ctx, None), P(dp, ctx), P(dp, None), P(dp), P(), P(), P())
    out_specs = (P(dp, ctx, None), P(dp, None), P(None, dp), P(dp))
    return jax.shard_map(body, mesh=fine, in_specs=in_specs, out_specs=out_specs, check_vma=False)
```
